32 devices in a mesh: groups: 2 (over y), cluster: 4 (over x, core), station: 4 (over z).
Axes of the slice: x: 2, y: 2, z: 4, core: 2. Of those that a mesh axis runs over, the one named last changes fastest.
Arguments:
- waveforms: float32 [256, 16, 3, 256], P(('groups', 'cluster'), 'station'), parts along dimension 0, may hold values from -120 to 120
- event_mask: int32 [256, 16], P(('groups', 'cluster'), 'station'), parts along dimension 0, may hold values 0 or 1
- station_weight: float32 [32], P('groups'), parts along dimension 0, may hold values from 0.01 to 10
- partners: int32 [4, 8], P(None, 'groups'), parts along dimension 1, may hold values from 0 to 3, as said below
- pair_list: int32 [4, 8, 256, 2], P(None, ('groups', 'cluster')), parts along dimension 1, may hold values from 0 to 31
- counts: int32 [8], P('groups'), parts along dimension 0, may hold values from 16 to 32, as said below
Outputs:
- stacked: float32 [4, 8, 256, 512], P(None, ('groups', 'cluster'), 'station'), parts along dimension 1
The draws below stay inside these ranges and needn't reach their ends.
There are 2 independent parts, one for each index of `groups`. The reference program is written for one: setup_inputs(seed, part) draws one part's arguments, and reference() takes and returns one part's arrays. A program takes and returns all parts, laid end to end along the dimension named above; each array names one. Nothing has to cross between parts.
Inputs may be any that keep to these rules, and one draw needn't show every extreme that they name: `partners`: in every round each cluster is paired with itself or with one of its two neighbours on the cluster cycle (index plus or minus one, modulo 4), and the pairing is mutual. `counts`: event slots of a cluster at or above its count are padding. Every draw has a cluster holding 32 events and another holding 32 // 2.
All inputs are finite; a program needn't handle non-finite values. No bound on the sum of `event_mask` on one device may be relied on, other than what follows from the above.
Results may differ from the reference program's by a relative error of at most 0.0003.
Values sent between devices are 32-bit elements; how exact they have to be, the bound alone decides.
No kernel may reach another device: no remote copies, remote signals or barrier semaphores. Data moves between devices by JAX's collectives and lax.ppermute only.
A program may use at most 64 MiB of HBM per device.

```python
import math
import jax
import jax.numpy as jnp
from jax import lax

E_DEV = 32
CH = 3
NT = 256
ROUNDS = 4
PAIRS = 256
NCL = 4
NEV = 128
NST = 16


def draw_waveforms(key, part):
    subkeys = jax.random.split(key, 5)
    wavelet = jax.random.truncated_normal(subkeys[0], -4.0, 4.0, (NST, CH, NT), jnp.float32)
    delays = jax.random.randint(subkeys[1], (NEV,), 0, 32)
    positions = (jnp.arange(NT, dtype=jnp.int32)[None, :] - delays[:, None]) % NT
    delayed_seismograms = jnp.transpose(jnp.take(wavelet, positions, axis=2), (2, 0, 1, 3))
    spread = jax.random.truncated_normal(subkeys[2], -4.0, 4.0, (NEV, NST, CH, NT), jnp.float32)
    noise_level = jnp.exp(jax.random.uniform(subkeys[3], (NEV, NST), jnp.float32, math.log(0.3), math.log(2.0)))
    amplitude = jnp.exp(jax.random.uniform(subkeys[4], (NEV, NST), jnp.float32, math.log(0.1), math.log(10.0)))
    traces = amplitude[:, :, None, None] * (delayed_seismograms + noise_level[:, :, None, None] * spread)
    return traces.astype(jnp.float32)


def draw_partners(key, part):
    subkeys = jax.random.split(key, 2)
    matching_kind = jax.random.randint(subkeys[0], (ROUNDS, 1), 0, 2)
    keep_edge = jax.random.randint(subkeys[1], (ROUNDS, NCL), 0, 2)
    cluster_ids = jnp.arange(NCL, dtype=jnp.int32)[None, :]
    starts_edge = (cluster_ids + matching_kind) % 2 == 0
    edge_start = jnp.where(starts_edge, cluster_ids, (cluster_ids - 1) % NCL)
    kept = jnp.take_along_axis(keep_edge, jnp.broadcast_to(edge_start, (ROUNDS, NCL)).astype(jnp.int32), axis=1)
    direction = jnp.where(starts_edge, 1, -1)
    neighbour = (cluster_ids + direction) % NCL
    return jnp.where(kept == 1, neighbour, cluster_ids).astype(jnp.int32)


def draw_counts(key, part):
    subkeys = jax.random.split(key, 3)
    counts = jax.random.randint(subkeys[0], (NCL,), E_DEV // 2, E_DEV + 1)
    full_cluster = jax.random.randint(subkeys[1], (), 0, NCL)
    half_cluster = (full_cluster + jax.random.randint(subkeys[2], (), 1, NCL)) % NCL
    cluster_ids = jnp.arange(NCL, dtype=jnp.int32)
    counts = jnp.where(cluster_ids == full_cluster, E_DEV, counts)
    counts = jnp.where(cluster_ids == half_cluster, E_DEV // 2, counts)
    return counts.astype(jnp.int32)


def place_ends(drawn, rng, low, high):
    spot = [jax.random.randint(jax.random.fold_in(rng, axis), (), 0, length) for axis, length in enumerate(drawn.shape)]
    widest = drawn.shape.index(max(drawn.shape))
    beside = spot[:widest] + [(spot[widest] + 1) % drawn.shape[widest]] + spot[widest + 1:]
    return drawn.at[tuple(spot)].set(low).at[tuple(beside)].set(high)


def setup_inputs(seed: int = 0, part: int = 0) -> dict:
    splits = jax.random.split(jax.random.key(seed), 7)
    own_keys = jax.random.split(jax.random.fold_in(splits[6], part), 7)
    return {
        "waveforms": draw_waveforms(jax.random.fold_in(jax.random.fold_in(splits[6], part), 71), part),
        "event_mask": place_ends((jax.random.randint(own_keys[1], (NEV, NST), 0, 4) < 3).astype(jnp.int32), jax.random.fold_in(own_keys[1], 1), 0, 1),
        "station_weight": jnp.clip(jnp.exp(jax.random.uniform(own_keys[2], (NST,), jnp.float32, math.log(0.01), math.log(10.0))), 0.01, 10.0),
        "partners": draw_partners(jax.random.fold_in(jax.random.fold_in(splits[6], part), 71), part),
        "pair_list": place_ends(jax.random.randint(own_keys[4], (ROUNDS, NCL, PAIRS, 2), 0, E_DEV), jax.random.fold_in(own_keys[4], 1), 0, E_DEV - 1).astype(jnp.int32),
        "counts": draw_counts(jax.random.fold_in(jax.random.fold_in(splits[6], part), 71), part),
    }


epsilon = 1e-06
HIGHEST = lax.Precision.HIGHEST

def make_tables(seismogram_readings):
    record_duration = 2 * seismogram_readings
    time_points = jnp.arange(seismogram_readings, dtype=jnp.int32)
    rotation_radians = time_points[:, None] * time_points[None, :] % record_duration
    angles = rotation_radians.astype(jnp.float32) * (math.pi / seismogram_readings)
    forward = jnp.concatenate([jnp.cos(angles), -jnp.sin(angles)], axis=1)
    column = jnp.arange(record_duration, dtype=jnp.int32)
    delayed_seismograms = (column + seismogram_readings) % record_duration
    backward_rotation_radians = time_points[:, None] * delayed_seismograms[None, :] % record_duration
    angles_back = backward_rotation_radians.astype(jnp.float32) * (math.pi / seismogram_readings)
    normalizing_multiplier = jnp.where(time_points == 0, 1.0, 2.0).astype(jnp.float32)[:, None] / record_duration
    inverse = jnp.concatenate([normalizing_multiplier * jnp.cos(angles_back), -normalizing_multiplier * jnp.sin(angles_back)], axis=0)
    return (forward, inverse)

def normalized(waveforms, event_mask):
    energy = lax.optimization_barrier(jnp.sum(waveforms * waveforms, axis=-1, keepdims=True))
    scaled = waveforms * lax.rsqrt(energy + epsilon)
    return scaled * event_mask[:, :, None, None].astype(jnp.float32)

def transform(traces, forward):
    events, stations, channels, seismogram_readings = traces.shape
    flattened = traces.reshape(events * stations * channels, seismogram_readings)
    spectra = jnp.dot(flattened, forward, precision=HIGHEST, preferred_element_type=jnp.float32)
    return spectra.reshape(events, stations * channels, 2 * seismogram_readings)

def cross_block(own_side, other_side, first_index, second):
    half_width = own_side.shape[-1] // 2
    left_rows = jnp.take(own_side, first_index, axis=0)
    right_rows = jnp.take(other_side, second, axis=0)
    real_part = lax.optimization_barrier(jnp.sum(left_rows[..., :half_width] * right_rows[..., :half_width] + left_rows[..., half_width:] * right_rows[..., half_width:], axis=1))
    imag_part = lax.optimization_barrier(jnp.sum(left_rows[..., half_width:] * right_rows[..., :half_width] - left_rows[..., :half_width] * right_rows[..., half_width:], axis=1))
    return jnp.concatenate([real_part, imag_part], axis=-1)

def pair_spectra(own_side, other_side, pairs_now, valid_pairs):
    pair_count = pairs_now.shape[0]
    block_rows = math.gcd(pair_count, 64)
    firsts = pairs_now[:, 0].reshape(pair_count // block_rows, block_rows)
    seconds = pairs_now[:, 1].reshape(pair_count // block_rows, block_rows)

    def one_block(indices):
        return cross_block(own_side, other_side, indices[0], indices[1])
    stacked_rows = lax.map(one_block, (firsts, seconds)).reshape(pair_count, own_side.shape[-1])
    return stacked_rows * valid_pairs[:, None]

def reference(waveforms, event_mask, station_weight, partners, pair_list, counts):
    forward, inverse = make_tables(NT)
    blocks = waveforms.reshape(NCL, E_DEV, NST, CH, NT)
    mask_blocks = event_mask.reshape(NCL, E_DEV, NST)

    def spectra_of(inputs):
        return transform(normalized(inputs[0], inputs[1]), forward)
    all_spectra = lax.map(spectra_of, (blocks, mask_blocks))
    weight_rows = jnp.repeat(station_weight, CH)
    network_scale = 1.0 / (CH * jnp.sum(station_weight))
    results = []
    for turn_index in range(ROUNDS):

        def one_cluster(cluster_id):
            partner_now = partners[turn_index, cluster_id]
            own_side = all_spectra[cluster_id] * weight_rows[None, :, None]
            other_side = all_spectra[partner_now]
            pairs_now = pair_list[turn_index, cluster_id]
            valid_pairs = ((pairs_now[:, 0] < counts[cluster_id]) & (pairs_now[:, 1] < counts[partner_now])).astype(jnp.float32)
            cross = pair_spectra(own_side, other_side, pairs_now, valid_pairs)
            return jnp.dot(cross, inverse, precision=HIGHEST, preferred_element_type=jnp.float32) * network_scale
        results.append(lax.map(one_cluster, jnp.arange(NCL, dtype=jnp.int32)))
    return jnp.stack(results)
```

```python
import math

import jax
import jax.numpy as jnp
import ml_dtypes
import numpy as np
from jax import lax
from jax.experimental import pallas as pl
from jax.experimental.pallas import tpu as pltpu
from jax.sharding import PartitionSpec as P

epsilon = 1e-06
SUB, LANES = 8, 128
HALF = SUB // 2
VMEM_BYTES = 40 * 1024 * 1024
F32 = jnp.float32
BF16 = jnp.bfloat16


def split_table(table):
    high = table.astype(ml_dtypes.bfloat16)
    low = (table - high.astype(np.float64)).astype(ml_dtypes.bfloat16)
    return high, low


def forward_table(samples):
    steps = np.arange(samples)
    angles = (steps[:, None] * steps[None, :] % (2 * samples)) * (math.pi / samples)
    return split_table(np.concatenate([np.cos(angles), -np.sin(angles)], axis=1))


def inverse_table(samples):
    record = 2 * samples
    bins = np.arange(samples)
    lags = (np.arange(record) + samples) % record
    angles = (bins[:, None] * lags[None, :] % record) * (math.pi / samples)
    gain = np.where(bins == 0, 1.0, 2.0)[:, None] / record
    return split_table(np.concatenate([gain * np.cos(angles), -gain * np.sin(angles)], axis=0))


def split_dot(value, high_ref, low_ref):
    high = value.astype(BF16)
    low = (value - high.astype(F32)).astype(BF16)
    total = jnp.dot(high, low_ref[...], preferred_element_type=F32)
    total += jnp.dot(low, high_ref[...], preferred_element_type=F32)
    return total + jnp.dot(high, high_ref[...], preferred_element_type=F32)


def prepare_kernel(waves_ref, mask_ref, weight_ref, out_ref):
    twos, _, _, stations, _ = waves_ref.shape
    events = 2 * twos
    rows = 3 * SUB * twos
    station_here = lax.axis_index("station")
    for parity in range(2):
        for channel in range(2):
            spot = channel * HALF
            out_ref[parity, :, spot : spot + HALF, :] = waves_ref[:, parity, channel]
        spot = parity * HALF
        out_ref[2, :, spot : spot + HALF, :] = waves_ref[:, parity, 2]
    station_id = lax.broadcasted_iota(jnp.int32, (stations, events), 0)
    weight = jnp.zeros((stations, events), F32)
    for station in range(stations):
        weight = jnp.where(station_id == station, weight_ref[station_here, station], weight)
    amplitude = mask_ref[...].astype(F32) * jnp.sqrt(weight)
    row = lax.broadcasted_iota(jnp.int32, (rows, events), 0)
    group, row_here = row // (SUB * twos), row % (SUB * twos)
    event_of_row = jnp.where(group < 2, 2 * (row_here // SUB) + group, row_here // HALF)
    event_id = lax.broadcasted_iota(jnp.int32, (rows, events), 1)
    picked = lax.dot_general(
        (event_of_row == event_id).astype(F32),
        amplitude,
        (((1,), (1,)), ((), ())),
        precision=lax.Precision.HIGHEST,
        preferred_element_type=F32,
    )
    row = lax.broadcasted_iota(jnp.int32, (rows, stations), 0)
    station_id = lax.broadcasted_iota(jnp.int32, (rows, stations), 1)
    factor = jnp.sum(jnp.where(row % HALF == station_id, picked, 0.0), axis=1, keepdims=True)
    traces = out_ref[...]
    energy = jnp.sum(traces * traces, axis=-1, keepdims=True)
    scale = lax.rsqrt(energy + epsilon) * factor.reshape(energy.shape)
    out_ref[...] = traces * scale


def prepare(waveforms, event_mask, station_weight):
    events, stations, channels, samples = waveforms.shape
    waves = jnp.transpose(waveforms, (0, 2, 1, 3)).reshape(events // 2, 2, channels, stations, samples)
    weights = station_weight.reshape(-1, stations)
    return pl.pallas_call(
        prepare_kernel,
        out_shape=jax.ShapeDtypeStruct((3, events // 2, SUB, samples), F32),
        in_specs=[
            pl.BlockSpec(memory_space=pltpu.VMEM),
            pl.BlockSpec(memory_space=pltpu.VMEM),
            pl.BlockSpec(memory_space=pltpu.SMEM),
        ],
        out_specs=pl.BlockSpec(memory_space=pltpu.VMEM),
        compiler_params=pltpu.CompilerParams(vmem_limit_bytes=VMEM_BYTES),
        name="prepare",
    )(waves, event_mask.T, weights)


def fill_spectra(traces_ref, high_ref, low_ref, spectra_ref, part):
    _, twos, _, samples = traces_ref.shape
    low_half = lax.broadcasted_iota(jnp.int32, (twos, SUB, LANES), 1) < HALF
    for parity in range(2):
        spectrum = split_dot(traces_ref[parity].reshape(twos * SUB, samples), high_ref, low_ref)
        for block in range(4):
            tile = spectrum[:, block * LANES : (block + 1) * LANES].reshape(twos, SUB, LANES)
            spectra_ref[part, :twos, parity, block + block // 2] = tile
    spectrum = split_dot(traces_ref[2].reshape(twos * SUB, samples), high_ref, low_ref)
    for side in range(2):
        spot = 2 * side * LANES
        lower = spectrum[:, spot : spot + LANES].reshape(twos, SUB, LANES)
        upper = spectrum[:, spot + LANES : spot + 2 * LANES].reshape(twos, SUB, LANES)
        turned_lower, turned_upper = pltpu.roll(lower, HALF, 1), pltpu.roll(upper, HALF, 1)
        spectra_ref[part, :twos, 0, 3 * side + 2] = jnp.where(low_half, lower, turned_upper)
        spectra_ref[part, :twos, 1, 3 * side + 2] = jnp.where(low_half, turned_lower, upper)


def cross_kernel(has_base, swap, *refs):
    partners_ref, counts_ref, pairs_ref, own_ref, sibling_ref, across_ref, high_ref, low_ref, *refs = refs
    if has_base:
        base_ref, *refs = refs
    *out_refs, spectra_ref, sums_ref = refs
    rounds, _, _, all_pairs = pairs_ref.shape
    twos = own_ref.shape[1]
    slots = 2 * (twos + 1)
    here = lax.axis_index("cluster")
    length = lax.axis_size("station")
    station_here = lax.axis_index("station")
    blocks = length // 2
    block_pairs = all_pairs // length
    sibling = jnp.where(here % 2 == 0, here + 1, here - 1)
    for part, traces_ref in enumerate((own_ref, sibling_ref, across_ref)):
        fill_spectra(traces_ref, high_ref, low_ref, spectra_ref, part)
    spectra_ref[0, twos] = jnp.zeros(spectra_ref.shape[2:], F32)
    flat_ref = spectra_ref.reshape(3 * slots, 6, SUB, LANES)
    own_count = counts_ref[here]
    low_half = lax.broadcasted_iota(jnp.int32, (SUB, LANES), 0) < HALF

    def folded(lower, upper, both):
        turned = pltpu.roll(jnp.where(low_half, upper, lower), HALF, 0)
        return jnp.where(low_half, lower, upper) + turned + both

    for turn in range(rounds):
        partner = partners_ref[turn, here]
        part = jnp.where(partner == here, 0, jnp.where(partner == sibling, slots, 2 * slots))
        partner_count = counts_ref[partner]
        for block in range(blocks):
            if blocks == 2:
                source = station_here if block == 0 else station_here + 1 - 2 * (station_here % 2)
            else:
                source = station_here // blocks * blocks + block
            start = source * block_pairs

            def one_pair(pair, carry):
                first = pairs_ref[turn, 0, 0, start + pair]
                second = pairs_ref[turn, 0, 1, start + pair]
                valid = (first < own_count) & (second < partner_count)
                left = flat_ref.at[jnp.where(valid, first, 2 * twos)]
                right = flat_ref.at[part + second]
                real, imag = [], []
                for tile in range(3):
                    left_real, left_imag = left[tile], left[tile + 3]
                    right_real, right_imag = right[tile], right[tile + 3]
                    real.append(left_real * right_real + left_imag * right_imag)
                    imag.append(left_imag * right_real - left_real * right_imag)
                spot = pl.multiple_of(pair * SUB, SUB)
                sums_ref[0, pl.ds(spot, SUB), :] = folded(*real)
                sums_ref[1, pl.ds(spot, SUB), :] = folded(*imag)
                return carry

            lax.fori_loop(0, block_pairs, one_pair, 0, unroll=8)
            out_ref = out_refs[block] if swap else out_refs[0]
            base_row = (turn * blocks + block) * block_pairs
            row = turn * block_pairs if swap else base_row
            for side in range(2):
                for half in range(2):
                    total = None
                    for lane_row in range(HALF):
                        piece = sums_ref[side, pl.ds(half * HALF + lane_row, block_pairs, stride=SUB), :]
                        total = piece if total is None else total + piece
                    column = (2 * side + half) * LANES
                    if has_base:
                        total += base_ref[base_row : base_row + block_pairs, column : column + LANES]
                    out_ref[row : row + block_pairs, column : column + LANES] = total


def cross_sums(scalars, traces, tables, base, swap):
    rounds, _, _, all_pairs = scalars[2].shape
    _, twos, _, samples = traces[0].shape
    length = lax.axis_size("station")
    half_rows = rounds * all_pairs // 2
    out_count = length // 2 if swap else 1
    block_pairs = all_pairs // length
    operands = [*scalars, *traces, *tables] + ([] if base is None else [base])
    vmem = pl.BlockSpec(memory_space=pltpu.VMEM)
    smem = pl.BlockSpec(memory_space=pltpu.SMEM)
    shape = jax.ShapeDtypeStruct((half_rows // out_count, 2 * samples), F32)
    return pl.pallas_call(
        lambda *refs: cross_kernel(base is not None, swap, *refs),
        out_shape=[shape] * out_count,
        in_specs=[smem] * 3 + [vmem] * (len(operands) - 3),
        out_specs=[vmem] * out_count,
        scratch_shapes=[
            pltpu.VMEM((3, twos + 1, 2, 6, SUB, LANES), F32),
            pltpu.VMEM((2, block_pairs * SUB, LANES), F32),
        ],
        compiler_params=pltpu.CompilerParams(vmem_limit_bytes=VMEM_BYTES),
        cost_estimate=pl.CostEstimate(flops=2 * 10**9, bytes_accessed=4 * 10**6, transcendentals=0),
        name="cross_sums",
    )(*operands)


def finish_kernel(channels, kept_ref, swapped_ref, weight_ref, high_ref, low_ref, out_ref):
    cross = kept_ref[...] + swapped_ref[...]
    scale = 1.0 / (channels * jnp.sum(weight_ref[...], axis=1, keepdims=True))
    out_ref[...] = split_dot(cross, high_ref, low_ref) * scale


def finish(channels, kept, swapped, station_weight, tables):
    return pl.pallas_call(
        lambda *refs: finish_kernel(channels, *refs),
        out_shape=jax.ShapeDtypeStruct(kept.shape, F32),
        compiler_params=pltpu.CompilerParams(vmem_limit_bytes=VMEM_BYTES),
        cost_estimate=pl.CostEstimate(flops=10**9, bytes_accessed=3 * 10**6, transcendentals=0),
        name="finish",
    )(kept, swapped, station_weight.reshape(1, -1), *tables)


def on_device(waveforms, event_mask, station_weight, partners, pair_list, counts):
    events, stations, channels, samples = waveforms.shape
    rounds, _, all_pairs, _ = pair_list.shape
    clusters = lax.axis_size("cluster")
    length = lax.axis_size("station")
    assert (stations, channels, samples) == (HALF, 3, 2 * LANES) and events % 2 == 0
    assert clusters % 2 == 0 and length % 4 == 0
    forward = [jnp.asarray(table) for table in forward_table(samples)]
    inverse = [jnp.asarray(table) for table in inverse_table(samples)]
    to_sibling = [(i, i ^ 1) for i in range(clusters)]
    to_across = [(i, (i + 1 if i % 2 else i - 1) % clusters) for i in range(clusters)]
    to_mirror = [(i, length - 1 - i) for i in range(length)]
    scalars = (partners, counts, jnp.transpose(pair_list, (0, 1, 3, 2)))

    own = prepare(waveforms, event_mask, station_weight)
    mirrored = lax.ppermute(own, "station", to_mirror)
    across = lax.ppermute(own, "cluster", to_across)
    sibling = lax.ppermute(own, "cluster", to_sibling)
    swap = length == 4
    (base,) = cross_sums(scalars, (own, sibling, across), forward, None, False)
    mirrored_across = lax.ppermute(mirrored, "cluster", to_across)
    mirrored_sibling = lax.ppermute(mirrored, "cluster", to_sibling)
    traces = (mirrored, mirrored_sibling, mirrored_across)
    if swap:
        kept, sent = cross_sums(scalars, traces, forward, base, True)
        received = lax.ppermute(sent, "station", [(i, i ^ 1) for i in range(length)])
    else:
        (partial,) = cross_sums(scalars, traces, forward, base, False)
        partial = partial.reshape(rounds, all_pairs // 2, 2 * samples)
        halves = np.arange(length).reshape(2, length // 2).tolist()
        kept = lax.psum_scatter(partial, "station", scatter_dimension=1, axis_index_groups=halves, tiled=True)
        kept = kept.reshape(-1, 2 * samples)
        received = jnp.zeros_like(kept)
    result = finish(channels, kept, received, station_weight, inverse)
    return result.reshape(rounds, 1, all_pairs // length, 2 * samples)


def solution(mesh):
    return jax.shard_map(
        on_device,
        mesh=mesh,
        in_specs=(
            P(("groups", "cluster"), "station", None, None),
            P(("groups", "cluster"), "station"),
            P("groups"),
            P(None, "groups"),
            P(None, ("groups", "cluster"), None, None),
            P("groups"),
        ),
        out_specs=P(None, ("groups", "cluster"), "station", None),
        check_vma=False,
    )
```

```python
import math

import jax
import jax.numpy as jnp
import ml_dtypes
import numpy as np
from jax import lax
from jax.experimental import pallas as pl
from jax.experimental.pallas import tpu as pltpu
from jax.sharding import PartitionSpec as P

epsilon = 1e-06
SUB, LANES = 8, 128
HALF = SUB // 2
VMEM_BYTES = 40 * 1024 * 1024
F32 = jnp.float32
BF16 = jnp.bfloat16


def split_table(table):
    high = table.astype(ml_dtypes.bfloat16)
    low = (table - high.astype(np.float64)).astype(ml_dtypes.bfloat16)
    return high, low


def forward_table(samples):
    steps = np.arange(samples)
    angles = (steps[:, None] * steps[None, :] % (2 * samples)) * (math.pi / samples)
    return split_table(np.concatenate([np.cos(angles), -np.sin(angles)], axis=1))


def inverse_table(samples):
    record = 2 * samples
    bins = np.arange(samples)
    lags = (np.arange(record) + samples) % record
    angles = (bins[:, None] * lags[None, :] % record) * (math.pi / samples)
    gain = np.where(bins == 0, 1.0, 2.0)[:, None] / record
    return split_table(np.concatenate([gain * np.cos(angles), -gain * np.sin(angles)], axis=0))


def split_dot(value, high_ref, low_ref):
    high = value.astype(BF16)
    low = (value - high.astype(F32)).astype(BF16)
    total = jnp.dot(high, low_ref[...], preferred_element_type=F32)
    total += jnp.dot(low, high_ref[...], preferred_element_type=F32)
    return total + jnp.dot(high, high_ref[...], preferred_element_type=F32)


def prepare_kernel(waves_hbm, mask_hbm, weight_ref, all_ref, first_ref, rest_ref, waves_ref, mask_ref, sems):
    waves_copy = pltpu.make_async_copy(waves_hbm, waves_ref, sems.at[0])
    mask_copy = pltpu.make_async_copy(mask_hbm, mask_ref, sems.at[1])
    waves_copy.start()
    mask_copy.start()
    twos, _, _, stations, _ = waves_ref.shape
    events = 2 * twos
    rows = 3 * SUB * twos
    first_weight = lax.axis_index("station") * stations
    station_id = lax.broadcasted_iota(jnp.int32, (stations, events), 0)
    weight = jnp.zeros((stations, events), F32)
    for station in range(stations):
        weight = jnp.where(station_id == station, weight_ref[first_weight + station], weight)
    row = lax.broadcasted_iota(jnp.int32, (rows, events), 0)
    group, row_here = row // (SUB * twos), row % (SUB * twos)
    event_of_row = jnp.where(group < 2, 2 * (row_here // SUB) + group, row_here // HALF)
    event_id = lax.broadcasted_iota(jnp.int32, (rows, events), 1)
    at_event = (event_of_row == event_id).astype(F32)
    row = lax.broadcasted_iota(jnp.int32, (rows, stations), 0)
    at_station = row % HALF == lax.broadcasted_iota(jnp.int32, (rows, stations), 1)
    mask_copy.wait()
    amplitude = mask_ref[...].astype(F32) * jnp.sqrt(weight)
    picked = lax.dot_general(
        at_event,
        amplitude,
        (((1,), (1,)), ((), ())),
        precision=lax.Precision.HIGHEST,
        preferred_element_type=F32,
    )
    factor = jnp.sum(jnp.where(at_station, picked, 0.0), axis=1, keepdims=True)
    waves_copy.wait()
    for parity in range(2):
        for channel in range(2):
            spot = channel * HALF
            all_ref[parity, :, spot : spot + HALF, :] = waves_ref[:, parity, channel]
        spot = parity * HALF
        all_ref[2, :, spot : spot + HALF, :] = waves_ref[:, parity, 2]
    traces = all_ref[...]
    energy = jnp.sum(traces * traces, axis=-1, keepdims=True)
    traces = traces * (lax.rsqrt(energy + epsilon) * factor.reshape(energy.shape))
    all_ref[...] = traces
    first_ref[...] = traces[:2]
    rest_ref[...] = traces[2:]


def prepare(waveforms, event_mask, station_weight):
    events, stations, channels, samples = waveforms.shape
    waves = jnp.transpose(waveforms, (0, 2, 1, 3)).reshape(events // 2, 2, channels, stations, samples)
    hbm = pl.BlockSpec(memory_space=pltpu.HBM)
    vmem = pl.BlockSpec(memory_space=pltpu.VMEM)
    return pl.pallas_call(
        prepare_kernel,
        out_shape=[jax.ShapeDtypeStruct((parts, events // 2, SUB, samples), F32) for parts in (3, 2, 1)],
        in_specs=[hbm, hbm, pl.BlockSpec(memory_space=pltpu.SMEM)],
        out_specs=[vmem] * 3,
        scratch_shapes=[
            pltpu.VMEM(waves.shape, F32),
            pltpu.VMEM((stations, events), event_mask.dtype),
            pltpu.SemaphoreType.DMA((2,)),
        ],
        compiler_params=pltpu.CompilerParams(vmem_limit_bytes=VMEM_BYTES),
        name="prepare",
    )(waves, event_mask.T, station_weight)


def fill_spectra(trace_refs, high_ref, low_ref, spectra_ref, part):
    pieces = [(ref, index) for ref in trace_refs for index in range(ref.shape[0])]
    _, twos, _, samples = trace_refs[0].shape
    low_half = lax.broadcasted_iota(jnp.int32, (twos, SUB, LANES), 1) < HALF
    for parity in range(2):
        ref, index = pieces[parity]
        spectrum = split_dot(ref[index].reshape(twos * SUB, samples), high_ref, low_ref)
        for block in range(4):
            tile = spectrum[:, block * LANES : (block + 1) * LANES].reshape(twos, SUB, LANES)
            spectra_ref[part, :twos, parity, block + block // 2] = tile
    ref, index = pieces[2]
    spectrum = split_dot(ref[index].reshape(twos * SUB, samples), high_ref, low_ref)
    for side in range(2):
        spot = 2 * side * LANES
        lower = spectrum[:, spot : spot + LANES].reshape(twos, SUB, LANES)
        upper = spectrum[:, spot + LANES : spot + 2 * LANES].reshape(twos, SUB, LANES)
        turned_lower, turned_upper = pltpu.roll(lower, HALF, 1), pltpu.roll(upper, HALF, 1)
        spectra_ref[part, :twos, 0, 3 * side + 2] = jnp.where(low_half, lower, turned_upper)
        spectra_ref[part, :twos, 1, 3 * side + 2] = jnp.where(low_half, turned_lower, upper)
    if part == 0:
        spectra_ref[0, twos] = jnp.zeros(spectra_ref.shape[2:], F32)


def add_pairs(scalar_refs, turns, wanted, spectra_ref, base_refs, out_refs, sums_ref):
    partners_ref, counts_ref, pairs_ref = scalar_refs
    _, _, _, all_pairs = pairs_ref.shape
    slots = 2 * spectra_ref.shape[1]
    here = lax.axis_index("cluster")
    length = lax.axis_size("station")
    station_here = lax.axis_index("station")
    blocks = length // 2
    block_pairs = all_pairs // length
    sibling = jnp.where(here % 2 == 0, here + 1, here - 1)
    flat_ref = spectra_ref.reshape(spectra_ref.shape[0] * slots, 6, SUB, LANES)
    own_count = counts_ref[here]
    low_half = lax.broadcasted_iota(jnp.int32, (SUB, LANES), 0) < HALF

    def folded(lower, upper, both):
        turned = pltpu.roll(jnp.where(low_half, upper, lower), HALF, 0)
        return jnp.where(low_half, lower, upper) + turned + both

    def one_turn(place, turn, partner, part):
        partner_count = counts_ref[partner]
        for block in range(blocks):
            if len(out_refs) == 2:
                source = station_here if block == 0 else station_here + 1 - 2 * (station_here % 2)
            else:
                source = station_here // blocks * blocks + block
            start = source * block_pairs

            def one_pair(pair, carry):
                first = pairs_ref[turn, 0, 0, start + pair]
                second = pairs_ref[turn, 0, 1, start + pair]
                valid = (first < own_count) & (second < partner_count)
                left = flat_ref.at[jnp.where(valid, first, slots - 2)]
                right = flat_ref.at[part * slots + second]
                real, imag = [], []
                for tile in range(3):
                    left_real, left_imag = left[tile], left[tile + 3]
                    right_real, right_imag = right[tile], right[tile + 3]
                    real.append(left_real * right_real + left_imag * right_imag)
                    imag.append(left_imag * right_real - left_real * right_imag)
                spot = pl.multiple_of(pair * SUB, SUB)
                sums_ref[0, pl.ds(spot, SUB), :] = folded(*real)
                sums_ref[1, pl.ds(spot, SUB), :] = folded(*imag)
                return carry

            lax.fori_loop(0, block_pairs, one_pair, 0, unroll=min(16, block_pairs))
            if len(out_refs) == 2:
                which, row = block, place * block_pairs
            else:
                which, row = 0, (place * blocks + block) * block_pairs
            for side in range(2):
                for half in range(2):
                    spot = pl.ds((2 * side + half) * LANES, LANES)
                    total = None if base_refs is None else base_refs[which][row : row + block_pairs, spot]
                    for lane_row in range(HALF):
                        piece = sums_ref[side, pl.ds(half * HALF + lane_row, block_pairs, stride=SUB), :]
                        total = piece if total is None else total + piece
                    out_refs[which][row : row + block_pairs, spot] = total

    for place, turn in enumerate(turns):
        partner = partners_ref[turn, here]
        part = jnp.where(partner == here, 0, jnp.where(partner == sibling, 1, 2))
        if wanted is None:
            one_turn(place, turn, partner, part)
        else:
            pl.when(wanted(part))(lambda: one_turn(place, turn, partner, part))


def half_turns(rounds, half):
    return range(half * rounds // 2, (half + 1) * rounds // 2)


def first_sums_kernel(outs, *refs):
    scalar_refs, (own, sibling, across, high, low), refs = refs[:3], refs[3:8], refs[8:]
    out_refs, (spectra_ref, sums_ref) = refs[: 2 * outs], refs[2 * outs :]
    for part, traces in enumerate((own, sibling, across)):
        fill_spectra([traces], high, low, spectra_ref, part)
    for half in range(2):
        turns = half_turns(scalar_refs[2].shape[0], half)
        add_pairs(scalar_refs, turns, None, spectra_ref, None, out_refs[half * outs : (half + 1) * outs], sums_ref)


def near_sums_kernel(outs, *refs):
    scalar_refs, (own_a, own_b, sibling_a, sibling_b, high, low), refs = refs[:3], refs[3:9], refs[9:]
    base_refs, refs = refs[: 2 * outs], refs[2 * outs :]
    spectra_ref, out_refs, sums_ref = refs[0], refs[1:-1], refs[-1]
    fill_spectra([own_a, own_b], high, low, spectra_ref, 0)
    fill_spectra([sibling_a, sibling_b], high, low, spectra_ref, 1)
    for half in range(2):
        turns = half_turns(scalar_refs[2].shape[0], half)
        some = slice(half * outs, (half + 1) * outs)
        add_pairs(
            scalar_refs, turns, lambda part: part < 2, spectra_ref, base_refs[some], out_refs[some], sums_ref
        )


def far_sums_kernel(outs, half, *refs):
    scalar_refs, refs = refs[:3], refs[3:]
    if half == 0:
        (across_a, across_b, high, low), refs = refs[:4], refs[4:]
    spectra_in, base_refs, refs = refs[0], refs[1 : 1 + outs], refs[1 + outs :]
    if half == 0:
        spectra_ref, refs = refs[0], refs[1:]
        fill_spectra([across_a, across_b], high, low, spectra_ref, 2)
    else:
        spectra_ref = spectra_in
    out_refs, (sums_ref,) = refs[:outs], refs[outs:]
    turns = half_turns(scalar_refs[2].shape[0], half)
    add_pairs(scalar_refs, turns, lambda part: part == 2, spectra_ref, base_refs, out_refs, sums_ref)


def call_sums(kernel, name, scalars, arrays, updated, out_shapes, scratch, flops):
    vmem = pl.BlockSpec(memory_space=pltpu.VMEM)
    smem = pl.BlockSpec(memory_space=pltpu.SMEM)
    operands = [*scalars, *arrays, *updated]
    shapes = [*out_shapes, *(jax.ShapeDtypeStruct(value.shape, value.dtype) for value in updated)]
    first_in, first_out = len(operands) - len(updated), len(shapes) - len(updated)
    return pl.pallas_call(
        kernel,
        out_shape=shapes,
        in_specs=[smem] * len(scalars) + [vmem] * (len(operands) - len(scalars)),
        out_specs=[vmem] * len(shapes),
        scratch_shapes=scratch,
        input_output_aliases={first_in + i: first_out + i for i in range(len(updated))},
        compiler_params=pltpu.CompilerParams(vmem_limit_bytes=VMEM_BYTES),
        cost_estimate=pl.CostEstimate(flops=flops, bytes_accessed=10**6, transcendentals=0),
        name=name,
    )(*operands)


def finish_kernel(channels, kept_ref, swapped_ref, weight_ref, high_ref, low_ref, *refs):
    out_ref = refs[-1]
    total = sum(weight_ref[station] for station in range(weight_ref.shape[0]))
    scale = 1.0 / (channels * jnp.full((1, out_ref.shape[1]), total, F32))
    out_ref[...] = split_dot(kept_ref[...] + swapped_ref[...], high_ref, low_ref) * scale


def finish(channels, kept, swapped, station_weight, tables, half, result):
    rows, lags = kept.shape
    vmem = pl.BlockSpec(memory_space=pltpu.VMEM)
    smem = pl.BlockSpec(memory_space=pltpu.SMEM)
    operands = [kept, swapped, station_weight, *tables]
    specs = [vmem, vmem, smem, vmem, vmem]
    if result is not None:
        operands.append(result)
        specs.append(pl.BlockSpec(memory_space=pltpu.HBM))
    return pl.pallas_call(
        lambda *refs: finish_kernel(channels, *refs),
        grid=(1,),
        out_shape=jax.ShapeDtypeStruct((2 * rows, lags), F32),
        in_specs=specs,
        out_specs=pl.BlockSpec((rows, lags), lambda i: (half, 0)),
        input_output_aliases={} if result is None else {5: 0},
        compiler_params=pltpu.CompilerParams(vmem_limit_bytes=VMEM_BYTES),
        cost_estimate=pl.CostEstimate(flops=10**9, bytes_accessed=10**6, transcendentals=0),
        name="finish",
    )(*operands)


def on_device(waveforms, event_mask, station_weight, partners, pair_list, counts):
    events, stations, channels, samples = waveforms.shape
    rounds, _, all_pairs, _ = pair_list.shape
    clusters = lax.axis_size("cluster")
    length = lax.axis_size("station")
    assert (stations, channels, samples) == (HALF, 3, 2 * LANES)
    assert events % 2 == 0 and rounds % 2 == 0 and clusters % 2 == 0 and length % 4 == 0
    forward = [jnp.asarray(table) for table in forward_table(samples)]
    inverse = [jnp.asarray(table) for table in inverse_table(samples)]
    scalars = (partners, counts, jnp.transpose(pair_list, (0, 1, 3, 2)))

    def to_sibling(value):
        return lax.ppermute(value, "cluster", [(i, i ^ 1) for i in range(clusters)])

    def to_across(value):
        return lax.ppermute(value, "cluster", [(i, (i + 1 if i % 2 else i - 1) % clusters) for i in range(clusters)])

    def to_mirror(value):
        return lax.ppermute(value, "station", [(i, length - 1 - i) for i in range(length)])

    swap = length == 4
    outs = 2 if swap else 1
    half_shape = jax.ShapeDtypeStruct((rounds * all_pairs // 4 // outs, 2 * samples), F32)
    spectra_shape = (3, events // 2 + 1, 2, 6, SUB, LANES)
    sums = pltpu.VMEM((2, all_pairs // length * SUB, LANES), F32)

    own, own_first, own_rest = prepare(waveforms, event_mask, station_weight)
    mirror_first = to_mirror(own_first)
    across = to_across(own)
    sibling = to_sibling(own)
    own_rest, mirror_first, across = lax.optimization_barrier((own_rest, mirror_first, across))
    mirror_rest = to_mirror(own_rest)
    far_first = to_across(mirror_first)
    near_first = to_sibling(mirror_first)
    partial = call_sums(
        lambda *refs: first_sums_kernel(outs, *refs),
        "first_sums",
        scalars,
        [own, sibling, across, *forward],
        [],
        [half_shape] * (2 * outs),
        [pltpu.VMEM(spectra_shape, F32), sums],
        4 * 10**9,
    )
    far_rest = to_across(mirror_rest)
    near_rest = to_sibling(mirror_rest)
    spectra, *partial = call_sums(
        lambda *refs: near_sums_kernel(outs, *refs),
        "near_sums",
        scalars,
        [mirror_first, mirror_rest, near_first, near_rest, *forward],
        partial,
        [jax.ShapeDtypeStruct(spectra_shape, F32)],
        [sums],
        3 * 10**9,
    )
    spectra, *early = call_sums(
        lambda *refs: far_sums_kernel(outs, 0, *refs),
        "far_sums",
        scalars,
        [far_first, far_rest, *forward],
        [spectra, *partial[:outs]],
        [],
        [sums],
        2 * 10**9,
    )
    late = call_sums(
        lambda *refs: far_sums_kernel(outs, 1, *refs),
        "far_sums",
        scalars,
        [spectra],
        partial[outs:],
        [],
        [sums],
        2 * 10**9,
    )
    result = None
    for half, values in enumerate((early, late)):
        if swap:
            kept, sent = values
            received = lax.ppermute(sent, "station", [(i, i ^ 1) for i in range(length)])
        else:
            groups = np.arange(length).reshape(2, length // 2).tolist()
            value = values[0].reshape(rounds // 2, all_pairs // 2, 2 * samples)
            kept = lax.psum_scatter(value, "station", scatter_dimension=1, axis_index_groups=groups, tiled=True)
            kept = kept.reshape(-1, 2 * samples)
            received = jnp.zeros_like(kept)
        result = finish(channels, kept, received, station_weight, inverse, half, result)
    return result.reshape(rounds, 1, all_pairs // length, 2 * samples)


def solution(mesh):
    return jax.shard_map(
        on_device,
        mesh=mesh,
        in_specs=(
            P(("groups", "cluster"), "station", None, None),
            P(("groups", "cluster"), "station"),
            P("groups"),
            P(None, "groups"),
            P(None, ("groups", "cluster"), None, None),
            P("groups"),
        ),
        out_specs=P(None, ("groups", "cluster"), "station", None),
        check_vma=False,
    )
```

```python
import math

import jax
import jax.numpy as jnp
import ml_dtypes
import numpy as np
from jax import lax
from jax.experimental import pallas as pl
from jax.experimental.pallas import tpu as pltpu
from jax.sharding import PartitionSpec as P

epsilon = 1e-06
SUB, LANES = 8, 128
HALF = SUB // 2
VMEM_BYTES = 40 * 1024 * 1024
F32 = jnp.float32
BF16 = jnp.bfloat16


def split_table(table):
    high = table.astype(ml_dtypes.bfloat16)
    low = (table - high.astype(np.float64)).astype(ml_dtypes.bfloat16)
    return np.stack([high, low])


def forward_table(samples):
    steps = np.arange(samples)
    angles = (steps[:, None] * steps[None, :] % (2 * samples)) * (math.pi / samples)
    return split_table(np.concatenate([np.cos(angles), -np.sin(angles)], axis=1))


def inverse_table(samples):
    record = 2 * samples
    bins = np.arange(samples)
    lags = (np.arange(record) + samples) % record
    angles = (bins[:, None] * lags[None, :] % record) * (math.pi / samples)
    gain = np.where(bins == 0, 1.0, 2.0)[:, None] / record
    return split_table(np.concatenate([gain * np.cos(angles), -gain * np.sin(angles)], axis=0))


def split_dot(value, table_ref):
    rows = value.shape[0]
    high = value.astype(BF16)
    low = (value - high.astype(F32)).astype(BF16)
    both = jnp.dot(jnp.concatenate([high, low], axis=0), table_ref[0], preferred_element_type=F32)
    return both[:rows] + (both[rows:] + jnp.dot(high, table_ref[1], preferred_element_type=F32))


def prepare_kernel(waves_hbm, mask_hbm, weight_ref, all_ref, even_ref, odd_ref, both_ref, waves_ref, mask_ref, sems):
    waves_copy = pltpu.make_async_copy(waves_hbm, waves_ref, sems.at[0])
    mask_copy = pltpu.make_async_copy(mask_hbm, mask_ref, sems.at[1])
    waves_copy.start()
    mask_copy.start()
    twos, _, channels, stations, _ = waves_ref.shape
    events = 2 * twos
    rows = 3 * SUB * twos
    network = channels * sum(weight_ref[station] for station in range(weight_ref.shape[0]))
    first_weight = lax.axis_index("station") * stations
    station_id = lax.broadcasted_iota(jnp.int32, (stations, events), 0)
    weight = jnp.zeros((stations, events), F32)
    for station in range(stations):
        weight = jnp.where(station_id == station, weight_ref[first_weight + station], weight)
    row = lax.broadcasted_iota(jnp.int32, (rows, events), 0)
    group, row_here = row // (SUB * twos), row % (SUB * twos)
    event_of_row = jnp.where(group < 2, 2 * (row_here // SUB) + group, row_here // HALF)
    event_id = lax.broadcasted_iota(jnp.int32, (rows, events), 1)
    at_event = (event_of_row == event_id).astype(F32)
    row = lax.broadcasted_iota(jnp.int32, (rows, stations), 0)
    at_station = row % HALF == lax.broadcasted_iota(jnp.int32, (rows, stations), 1)
    mask_copy.wait()
    amplitude = mask_ref[...].astype(F32) * jnp.sqrt(weight / network)
    picked = lax.dot_general(
        at_event,
        amplitude,
        (((1,), (1,)), ((), ())),
        precision=lax.Precision.HIGHEST,
        preferred_element_type=F32,
    )
    factor = jnp.sum(jnp.where(at_station, picked, 0.0), axis=1, keepdims=True)
    waves_copy.wait()
    for parity in range(2):
        for channel in range(2):
            spot = channel * HALF
            all_ref[parity, :, spot : spot + HALF, :] = waves_ref[:, parity, channel]
        spot = parity * HALF
        all_ref[2, :, spot : spot + HALF, :] = waves_ref[:, parity, 2]
    traces = all_ref[...]
    energy = jnp.sum(traces * traces, axis=-1, keepdims=True)
    traces = traces * (lax.rsqrt(energy + epsilon) * factor.reshape(energy.shape))
    all_ref[...] = traces
    even_ref[...] = traces[0:1]
    odd_ref[...] = traces[1:2]
    both_ref[...] = traces[2:3]


def prepare(waveforms, event_mask, station_weight):
    events, stations, channels, samples = waveforms.shape
    waves = jnp.transpose(waveforms, (0, 2, 1, 3)).reshape(events // 2, 2, channels, stations, samples)
    hbm = pl.BlockSpec(memory_space=pltpu.HBM)
    vmem = pl.BlockSpec(memory_space=pltpu.VMEM)
    return pl.pallas_call(
        prepare_kernel,
        out_shape=[jax.ShapeDtypeStruct((parts, events // 2, SUB, samples), F32) for parts in (3, 1, 1, 1)],
        in_specs=[hbm, hbm, pl.BlockSpec(memory_space=pltpu.SMEM)],
        out_specs=[vmem] * 4,
        scratch_shapes=[
            pltpu.VMEM(waves.shape, F32),
            pltpu.VMEM((stations, events), event_mask.dtype),
            pltpu.SemaphoreType.DMA((2,)),
        ],
        compiler_params=pltpu.CompilerParams(vmem_limit_bytes=VMEM_BYTES),
        name="prepare",
    )(waves, event_mask.T, station_weight)


def fill_spectra(trace_refs, table_ref, spectra_ref, part):
    pieces = [(ref, index) for ref in trace_refs for index in range(ref.shape[0])]
    _, twos, _, samples = trace_refs[0].shape
    low_half = lax.broadcasted_iota(jnp.int32, (twos, SUB, LANES), 1) < HALF
    for parity in range(2):
        ref, index = pieces[parity]
        spectrum = split_dot(ref[index].reshape(twos * SUB, samples), table_ref)
        for block in range(4):
            tile = spectrum[:, block * LANES : (block + 1) * LANES].reshape(twos, SUB, LANES)
            spectra_ref[part, :twos, parity, block + block // 2] = tile
    ref, index = pieces[2]
    spectrum = split_dot(ref[index].reshape(twos * SUB, samples), table_ref)
    for side in range(2):
        spot = 2 * side * LANES
        lower = spectrum[:, spot : spot + LANES].reshape(twos, SUB, LANES)
        upper = spectrum[:, spot + LANES : spot + 2 * LANES].reshape(twos, SUB, LANES)
        turned_lower, turned_upper = pltpu.roll(lower, HALF, 1), pltpu.roll(upper, HALF, 1)
        spectra_ref[part, :twos, 0, 3 * side + 2] = jnp.where(low_half, lower, turned_upper)
        spectra_ref[part, :twos, 1, 3 * side + 2] = jnp.where(low_half, turned_lower, upper)
    if part == 0:
        spectra_ref[0, twos] = jnp.zeros(spectra_ref.shape[2:], F32)


def add_pairs(scalar_refs, turns, wanted, spectra_ref, base_refs, out_refs, sums_ref):
    partners_ref, counts_ref, pairs_ref = scalar_refs
    _, _, _, all_pairs = pairs_ref.shape
    slots = 2 * spectra_ref.shape[1]
    here = lax.axis_index("cluster")
    length = lax.axis_size("station")
    station_here = lax.axis_index("station")
    blocks = length // 2
    block_pairs = all_pairs // length
    sibling = jnp.where(here % 2 == 0, here + 1, here - 1)
    flat_ref = spectra_ref.reshape(spectra_ref.shape[0] * slots, 6, SUB, LANES)
    own_count = counts_ref[here]
    low_half = lax.broadcasted_iota(jnp.int32, (SUB, LANES), 0) < HALF

    def folded(lower, upper, both):
        turned = pltpu.roll(jnp.where(low_half, upper, lower), HALF, 0)
        return jnp.where(low_half, lower, upper) + turned + both

    def one_turn(place, turn, partner, part):
        partner_count = counts_ref[partner]
        for block in range(blocks):
            if len(out_refs) == 2:
                source = station_here if block == 0 else station_here + 1 - 2 * (station_here % 2)
            else:
                source = station_here // blocks * blocks + block
            start = source * block_pairs

            def one_pair(pair, carry):
                first = pairs_ref[turn, 0, 0, start + pair]
                second = pairs_ref[turn, 0, 1, start + pair]
                valid = (first < own_count) & (second < partner_count)
                left = flat_ref.at[jnp.where(valid, first, slots - 2)]
                right = flat_ref.at[part * slots + second]
                real, imag = [], []
                for tile in range(3):
                    left_real, left_imag = left[tile], left[tile + 3]
                    right_real, right_imag = right[tile], right[tile + 3]
                    real.append(left_real * right_real + left_imag * right_imag)
                    imag.append(left_imag * right_real - left_real * right_imag)
                spot = pl.multiple_of(pair * SUB, SUB)
                sums_ref[0, pl.ds(spot, SUB), :] = folded(*real)
                sums_ref[1, pl.ds(spot, SUB), :] = folded(*imag)
                return carry

            lax.fori_loop(0, block_pairs, one_pair, 0, unroll=min(16, block_pairs))
            if len(out_refs) == 2:
                which, row = block, place * block_pairs
            else:
                which, row = 0, (place * blocks + block) * block_pairs
            for side in range(2):
                for half in range(2):
                    spot = pl.ds((2 * side + half) * LANES, LANES)
                    total = None if base_refs is None else base_refs[which][row : row + block_pairs, spot]
                    for lane_row in range(HALF):
                        piece = sums_ref[side, pl.ds(half * HALF + lane_row, block_pairs, stride=SUB), :]
                        total = piece if total is None else total + piece
                    out_refs[which][row : row + block_pairs, spot] = total

    for place, turn in enumerate(turns):
        partner = partners_ref[turn, here]
        part = jnp.where(partner == here, 0, jnp.where(partner == sibling, 1, 2))
        if wanted is None:
            one_turn(place, turn, partner, part)
        else:
            pl.when(wanted(part))(lambda: one_turn(place, turn, partner, part))


def half_turns(rounds, half):
    return range(half * rounds // 2, (half + 1) * rounds // 2)


def near_sums_kernel(count, outs, first, *refs):
    scalar_refs, refs = refs[:3], refs[3:]
    own_refs, sibling_refs, table_ref, refs = refs[:count], refs[count : 2 * count], refs[2 * count], refs[2 * count + 1 :]
    base_refs, refs = ([None] * (2 * outs), refs) if first else (refs[: 2 * outs], refs[2 * outs :])
    spectra_ref, out_refs, sums_ref = refs[0], refs[1:-1], refs[-1]
    fill_spectra(own_refs, table_ref, spectra_ref, 0)
    fill_spectra(sibling_refs, table_ref, spectra_ref, 1)
    for half in range(2):
        turns = half_turns(scalar_refs[2].shape[0], half)
        some = slice(half * outs, (half + 1) * outs)
        base = None if first else base_refs[some]
        add_pairs(scalar_refs, turns, lambda part: part < 2, spectra_ref, base, out_refs[some], sums_ref)


def far_sums_kernel(count, outs, first, halves, *refs):
    scalar_refs, across_refs, refs = refs[:3], refs[3 : 3 + count], refs[3 + count :]
    if count:
        table_ref, refs = refs[0], refs[1:]
    spectra_in, base_refs, refs = refs[0], refs[1 : 1 + outs * len(halves)], refs[1 + outs * len(halves) :]
    if count:
        spectra_ref, refs = refs[0], refs[1:]
        fill_spectra(across_refs, table_ref, spectra_ref, 2)
    else:
        spectra_ref = spectra_in
    out_refs, sums_ref = refs[:-1], refs[-1]
    for place, half in enumerate(halves):
        turns = half_turns(scalar_refs[2].shape[0], half)
        some = slice(place * outs, (place + 1) * outs)
        base = None if first else base_refs[some]
        add_pairs(scalar_refs, turns, lambda part: part == 2, spectra_ref, base, out_refs[some], sums_ref)


def call_sums(kernel, name, scalars, arrays, updated, out_shapes, scratch, flops):
    vmem = pl.BlockSpec(memory_space=pltpu.VMEM)
    smem = pl.BlockSpec(memory_space=pltpu.SMEM)
    operands = [*scalars, *arrays, *updated]
    shapes = [*out_shapes, *(jax.ShapeDtypeStruct(value.shape, value.dtype) for value in updated)]
    first_in, first_out = len(operands) - len(updated), len(shapes) - len(updated)
    return pl.pallas_call(
        kernel,
        out_shape=shapes,
        in_specs=[smem] * len(scalars) + [vmem] * (len(operands) - len(scalars)),
        out_specs=[vmem] * len(shapes),
        scratch_shapes=scratch,
        input_output_aliases={first_in + i: first_out + i for i in range(len(updated))},
        compiler_params=pltpu.CompilerParams(vmem_limit_bytes=VMEM_BYTES),
        cost_estimate=pl.CostEstimate(flops=flops, bytes_accessed=10**6, transcendentals=0),
        name=name,
    )(*operands)


def finish_kernel(early_ref, early_swapped_ref, late_ref, late_swapped_ref, table_ref, out_ref):
    rows = early_ref.shape[0]
    out_ref[:rows] = split_dot(early_ref[...] + early_swapped_ref[...], table_ref)
    out_ref[rows:] = split_dot(late_ref[...] + late_swapped_ref[...], table_ref)


def finish(values, table):
    rows, lags = values[0].shape
    return pl.pallas_call(
        finish_kernel,
        out_shape=jax.ShapeDtypeStruct((2 * rows, lags), F32),
        compiler_params=pltpu.CompilerParams(vmem_limit_bytes=VMEM_BYTES),
        cost_estimate=pl.CostEstimate(flops=10**9, bytes_accessed=10**6, transcendentals=0),
        name="finish",
    )(*values, table)


def on_device(waveforms, event_mask, station_weight, partners, pair_list, counts):
    events, stations, channels, samples = waveforms.shape
    rounds, _, all_pairs, _ = pair_list.shape
    clusters = lax.axis_size("cluster")
    length = lax.axis_size("station")
    assert (stations, channels, samples) == (HALF, 3, 2 * LANES)
    assert events % 2 == 0 and rounds % 2 == 0 and clusters % 2 == 0 and length % 4 == 0
    forward = jnp.asarray(forward_table(samples))
    inverse = jnp.asarray(inverse_table(samples))
    scalars = (partners, counts, jnp.transpose(pair_list, (0, 1, 3, 2)))

    def to_sibling(value):
        return lax.ppermute(value, "cluster", [(i, i ^ 1) for i in range(clusters)])

    def to_across(value):
        return lax.ppermute(value, "cluster", [(i, (i + 1 if i % 2 else i - 1) % clusters) for i in range(clusters)])

    def to_mirror(value):
        return lax.ppermute(value, "station", [(i, length - 1 - i) for i in range(length)])

    swap = length == 4
    outs = 2 if swap else 1
    half_shape = jax.ShapeDtypeStruct((rounds * all_pairs // 4 // outs, 2 * samples), F32)
    spectra_shape = jax.ShapeDtypeStruct((3, events // 2 + 1, 2, 6, SUB, LANES), F32)
    sums = pltpu.VMEM((2, all_pairs // length * SUB, LANES), F32)

    def near_sums(own, sibling, partial):
        first = partial is None
        return call_sums(
            lambda *refs: near_sums_kernel(len(own), outs, first, *refs),
            "near_sums",
            scalars,
            [*own, *sibling, forward],
            [] if first else partial,
            [spectra_shape] + [half_shape] * (2 * outs if first else 0),
            [sums],
            4 * 10**9,
        )

    def far_sums(across, spectra, partial, first, halves):
        filled = [spectra] if across else []
        return call_sums(
            lambda *refs: far_sums_kernel(len(across), outs, first, halves, *refs),
            "far_sums",
            scalars,
            [*across, forward] if across else [spectra],
            [*filled, *partial],
            [],
            [sums],
            2 * 10**9,
        )

    own, *pieces = prepare(waveforms, event_mask, station_weight)
    mirror = [to_mirror(piece) for piece in pieces]
    across = to_across(own)
    sibling = to_sibling(own)
    spectra, *partial = near_sums([own], [sibling], None)
    spectra, *partial = far_sums([across], spectra, partial, True, (0, 1))
    mirror, partial = lax.optimization_barrier((mirror, partial))
    far, near = [], []
    for piece in mirror:
        far.append(to_across(piece))
        near.append(to_sibling(piece))
    spectra, *partial = near_sums(mirror, near, partial)
    spectra, *early = far_sums(far, spectra, partial[:outs], False, (0,))
    late = far_sums([], spectra, partial[outs:], False, (1,))
    values = []
    for half in (early, late):
        if swap:
            kept, sent = half
            received = lax.ppermute(sent, "station", [(i, i ^ 1) for i in range(length)])
        else:
            groups = np.arange(length).reshape(2, length // 2).tolist()
            value = half[0].reshape(rounds // 2, all_pairs // 2, 2 * samples)
            kept = lax.psum_scatter(value, "station", scatter_dimension=1, axis_index_groups=groups, tiled=True)
            kept = kept.reshape(-1, 2 * samples)
            received = jnp.zeros_like(kept)
        values += [kept, received]
    result = finish(values, inverse)
    return result.reshape(rounds, 1, all_pairs // length, 2 * samples)


def solution(mesh):
    return jax.shard_map(
        on_device,
        mesh=mesh,
        in_specs=(
            P(("groups", "cluster"), "station", None, None),
            P(("groups", "cluster"), "station"),
            P("groups"),
            P(None, "groups"),
            P(None, ("groups", "cluster"), None, None),
            P("groups"),
        ),
        out_specs=P(None, ("groups", "cluster"), "station", None),
        check_vma=False,
    )
```

```python
import math

import jax
import jax.numpy as jnp
import ml_dtypes
import numpy as np
from jax import lax
from jax.experimental import pallas as pl
from jax.experimental.pallas import tpu as pltpu
from jax.sharding import PartitionSpec as P

epsilon = 1e-06
SUB, LANES = 8, 128
HALF = SUB // 2
VMEM_BYTES = 40 * 1024 * 1024
PREPARE_VMEM_BYTES = 62 * 1024 * 1024
F32 = jnp.float32
BF16 = jnp.bfloat16


def split_table(table):
    high = table.astype(ml_dtypes.bfloat16)
    low = (table - high.astype(np.float64)).astype(ml_dtypes.bfloat16)
    return np.stack([high, low])


def forward_table(samples):
    steps = np.arange(samples)
    angles = (steps[:, None] * steps[None, :] % (2 * samples)) * (math.pi / samples)
    return split_table(np.concatenate([np.cos(angles), -np.sin(angles)], axis=1))


def inverse_table(samples):
    record = 2 * samples
    bins = np.arange(samples)
    lags = (np.arange(record) + samples) % record
    angles = (bins[:, None] * lags[None, :] % record) * (math.pi / samples)
    gain = np.where(bins == 0, 1.0, 2.0)[:, None] / record
    return split_table(np.concatenate([gain * np.cos(angles), -gain * np.sin(angles)], axis=0))


def split_dot(value, table_ref):
    rows = value.shape[0]
    high = value.astype(BF16)
    low = (value - high.astype(F32)).astype(BF16)
    both = jnp.dot(jnp.concatenate([high, low], axis=0), table_ref[0], preferred_element_type=F32)
    return both[:rows] + (both[rows:] + jnp.dot(high, table_ref[1], preferred_element_type=F32))


def prepare_kernel(waves_hbm, mask_hbm, weight_hbm, all_ref, *refs):
    *piece_refs, waves_ref, mask_ref, weight_ref, sems = refs
    copies = [
        pltpu.make_async_copy(weight_hbm, weight_ref, sems.at[0]),
        pltpu.make_async_copy(mask_hbm, mask_ref, sems.at[1]),
        pltpu.make_async_copy(waves_hbm, waves_ref, sems.at[2]),
    ]
    for copy in copies:
        copy.start()
    twos, _, channels, stations, _ = waves_ref.shape
    events = 2 * twos
    rows = 3 * SUB * twos
    row = lax.broadcasted_iota(jnp.int32, (rows, events), 0)
    group, row_here = row // (SUB * twos), row % (SUB * twos)
    event_of_row = jnp.where(group < 2, 2 * (row_here // SUB) + group, row_here // HALF)
    at_event = (event_of_row == lax.broadcasted_iota(jnp.int32, (rows, events), 1)).astype(F32)
    row = lax.broadcasted_iota(jnp.int32, (rows, stations), 0)
    at_station = row % HALF == lax.broadcasted_iota(jnp.int32, (rows, stations), 1)
    station_id = lax.broadcasted_iota(jnp.int32, (stations, events), 0)
    first_weight = lax.axis_index("station") * stations
    copies[0].wait()
    network = channels * sum(weight_ref[station] for station in range(weight_ref.shape[0]))
    weight = jnp.zeros((stations, events), F32)
    for station in range(stations):
        weight = jnp.where(station_id == station, weight_ref[first_weight + station], weight)
    copies[1].wait()
    amplitude = mask_ref[...].astype(F32) * jnp.sqrt(weight / network)
    picked = lax.dot_general(
        at_event,
        amplitude,
        (((1,), (1,)), ((), ())),
        precision=lax.Precision.HIGHEST,
        preferred_element_type=F32,
    )
    factor = jnp.sum(jnp.where(at_station, picked, 0.0), axis=1, keepdims=True).reshape(3, twos, SUB, 1)
    copies[2].wait()
    for group in range(3):
        for side in range(2):
            part = waves_ref[:, group, side] if group < 2 else waves_ref[:, side, 2]
            all_ref[group, :, side * HALF : (side + 1) * HALF, :] = part
        traces = all_ref[group]
        energy = jnp.sum(traces * traces, axis=-1, keepdims=True)
        traces = traces * (lax.rsqrt(energy + epsilon) * factor[group])
        all_ref[group] = traces
        for piece, piece_ref in enumerate(piece_refs):
            piece_ref[group] = traces[piece * twos // 2 : (piece + 1) * twos // 2]


def prepare(waveforms, event_mask, station_weight):
    events, stations, channels, samples = waveforms.shape
    waves = jnp.transpose(waveforms, (0, 2, 1, 3)).reshape(events // 2, 2, channels, stations, samples)
    hbm = pl.BlockSpec(memory_space=pltpu.HBM)
    vmem = pl.BlockSpec(memory_space=pltpu.VMEM)
    return pl.pallas_call(
        prepare_kernel,
        out_shape=[jax.ShapeDtypeStruct((3, events // share, SUB, samples), F32) for share in (2, 4, 4)],
        in_specs=[hbm] * 3,
        out_specs=[vmem] * 3,
        scratch_shapes=[
            pltpu.VMEM(waves.shape, F32),
            pltpu.VMEM((stations, events), event_mask.dtype),
            pltpu.SMEM(station_weight.shape, F32),
            pltpu.SemaphoreType.DMA((3,)),
        ],
        compiler_params=pltpu.CompilerParams(vmem_limit_bytes=PREPARE_VMEM_BYTES),
        name="prepare",
    )(waves, event_mask.T, station_weight)


def index_kernel(events, partners_ref, counts_ref, pairs_ref, index_ref):
    rounds, _, _, all_pairs = pairs_ref.shape
    here = lax.axis_index("cluster")
    sibling = jnp.where(here % 2 == 0, here + 1, here - 1)
    own_count = counts_ref[here]
    for turn in range(rounds):
        partner = partners_ref[turn, here]
        part = jnp.where(partner == here, 0, jnp.where(partner == sibling, 1, 2))
        first, second = pairs_ref[turn, 0, 0:1], pairs_ref[turn, 0, 1:2]
        valid = (first < own_count) & (second < counts_ref[partner])
        index_ref[turn, 0:1] = jnp.where(valid, first, events)
        index_ref[turn, 1:2] = second + part * (events + 2)
        index_ref[turn, 2:3] = jnp.full((1, all_pairs), part, jnp.int32)


def pair_index(partners, counts, pair_list, events):
    rounds, _, all_pairs, _ = pair_list.shape
    vmem = pl.BlockSpec(memory_space=pltpu.VMEM)
    smem = pl.BlockSpec(memory_space=pltpu.SMEM)
    return pl.pallas_call(
        lambda *refs: index_kernel(events, *refs),
        out_shape=jax.ShapeDtypeStruct((rounds, 3, all_pairs), jnp.int32),
        in_specs=[smem, smem, vmem],
        out_specs=vmem,
        compiler_params=pltpu.CompilerParams(vmem_limit_bytes=VMEM_BYTES),
        name="pair_index",
    )(partners, counts, jnp.transpose(pair_list, (0, 1, 3, 2)))


def fill_spectra(traces_ref, part, piece, table_ref, spectra_ref):
    _, twos, _, samples = traces_ref.shape
    spot = pl.ds(piece * twos, twos)
    spectrum = split_dot(traces_ref[...].reshape(3 * twos * SUB, samples), table_ref)
    tiles = [
        spectrum[:, block * LANES : (block + 1) * LANES].reshape(3, twos, SUB, LANES) for block in range(4)
    ]
    for group in range(2):
        for block in range(4):
            spectra_ref[part, spot, group, block + block // 2] = tiles[block][group]
    low_half = lax.broadcasted_iota(jnp.int32, (twos, SUB, LANES), 1) < HALF
    for side in range(2):
        lower, upper = tiles[2 * side][2], tiles[2 * side + 1][2]
        turned_lower, turned_upper = pltpu.roll(lower, HALF, 1), pltpu.roll(upper, HALF, 1)
        spectra_ref[part, spot, 0, 3 * side + 2] = jnp.where(low_half, lower, turned_upper)
        spectra_ref[part, spot, 1, 3 * side + 2] = jnp.where(low_half, turned_lower, upper)


def clear_last(spectra_ref):
    spectra_ref[0, spectra_ref.shape[1] - 1] = jnp.zeros(spectra_ref.shape[2:], F32)


def spectra_kernel(places, first, *refs):
    trace_refs, table_ref, spectra_ref = refs[: len(places)], refs[len(places)], refs[-1]
    for (part, piece), traces_ref in zip(places, trace_refs, strict=True):
        fill_spectra(traces_ref, part, piece, table_ref, spectra_ref)
    if first:
        clear_last(spectra_ref)


def add_pairs(index_ref, turns, wanted, spectra_ref, base_refs, out_refs, sums_ref):
    _, _, all_pairs = index_ref.shape
    slots = 2 * spectra_ref.shape[1]
    length = lax.axis_size("station")
    station_here = lax.axis_index("station")
    blocks = length // 2
    block_pairs = all_pairs // length
    flat_ref = spectra_ref.reshape(spectra_ref.shape[0] * slots, 6, SUB, LANES)
    low_half = lax.broadcasted_iota(jnp.int32, (SUB, LANES), 0) < HALF

    def folded(lower, upper, both):
        turned = pltpu.roll(jnp.where(low_half, upper, lower), HALF, 0)
        return jnp.where(low_half, lower, upper) + turned + both

    def one_turn(place, turn):
        for block in range(blocks):
            if len(out_refs) == 2:
                source = station_here if block == 0 else station_here + 1 - 2 * (station_here % 2)
            else:
                source = station_here // blocks * blocks + block
            start = source * block_pairs

            def one_pair(pair, carry):
                left = flat_ref.at[index_ref[turn, 0, start + pair]]
                right = flat_ref.at[index_ref[turn, 1, start + pair]]
                real, imag = [], []
                for tile in range(3):
                    left_real, left_imag = left[tile], left[tile + 3]
                    right_real, right_imag = right[tile], right[tile + 3]
                    real.append(left_real * right_real + left_imag * right_imag)
                    imag.append(left_imag * right_real - left_real * right_imag)
                spot = pl.multiple_of(pair * SUB, SUB)
                sums_ref[0, pl.ds(spot, SUB), :] = folded(*real)
                sums_ref[1, pl.ds(spot, SUB), :] = folded(*imag)
                return carry

            lax.fori_loop(0, block_pairs, one_pair, 0, unroll=min(16, block_pairs))
            if len(out_refs) == 2:
                which, row = block, place * block_pairs
            else:
                which, row = 0, (place * blocks + block) * block_pairs
            for side in range(2):
                for half in range(2):
                    spot = pl.ds((2 * side + half) * LANES, LANES)
                    total = None if base_refs is None else base_refs[which][row : row + block_pairs, spot]
                    for lane_row in range(HALF):
                        piece = sums_ref[side, pl.ds(half * HALF + lane_row, block_pairs, stride=SUB), :]
                        total = piece if total is None else total + piece
                    out_refs[which][row : row + block_pairs, spot] = total

    for place, turn in enumerate(turns):
        pl.when(wanted(index_ref[turn, 2, 0]))(lambda: one_turn(place, turn))


def half_turns(rounds, half):
    return range(half * rounds // 2, (half + 1) * rounds // 2)


def first_near_kernel(outs, index_ref, own_ref, sibling_ref, table_ref, spectra_ref, *refs):
    out_refs, sums_ref = refs[:-1], refs[-1]
    fill_spectra(own_ref, 0, 0, table_ref, spectra_ref)
    fill_spectra(sibling_ref, 1, 0, table_ref, spectra_ref)
    clear_last(spectra_ref)
    for half in range(2):
        turns = half_turns(index_ref.shape[0], half)
        some = out_refs[half * outs : (half + 1) * outs]
        add_pairs(index_ref, turns, lambda part: part < 2, spectra_ref, None, some, sums_ref)


def first_far_kernel(outs, index_ref, across_ref, table_ref, *refs):
    spectra_ref, out_refs, sums_ref = refs[2 * outs + 1], refs[2 * outs + 2 : -1], refs[-1]
    fill_spectra(across_ref, 2, 0, table_ref, spectra_ref)
    for half in range(2):
        turns = half_turns(index_ref.shape[0], half)
        some = out_refs[half * outs : (half + 1) * outs]
        add_pairs(index_ref, turns, lambda part: part == 2, spectra_ref, None, some, sums_ref)


def near_kernel(outs, index_ref, sibling_ref, table_ref, *refs):
    base_refs, refs = refs[1 : 2 * outs + 1], refs[2 * outs + 1 :]
    spectra_ref, out_refs, sums_ref = refs[0], refs[1:-1], refs[-1]
    fill_spectra(sibling_ref, 1, 1, table_ref, spectra_ref)
    for half in range(2):
        turns = half_turns(index_ref.shape[0], half)
        some = slice(half * outs, (half + 1) * outs)
        add_pairs(index_ref, turns, lambda part: part < 2, spectra_ref, base_refs[some], out_refs[some], sums_ref)


def far_kernel(outs, half, index_ref, *refs):
    if half == 0:
        across_ref, table_ref, _, *refs = refs
        base_refs, spectra_ref, refs = refs[:outs], refs[outs], refs[outs + 1 :]
        fill_spectra(across_ref, 2, 1, table_ref, spectra_ref)
    else:
        spectra_ref, base_refs, refs = refs[0], refs[1 : outs + 1], refs[outs + 1 :]
    out_refs, sums_ref = refs[:-1], refs[-1]
    turns = half_turns(index_ref.shape[0], half)
    add_pairs(index_ref, turns, lambda part: part == 2, spectra_ref, base_refs, out_refs, sums_ref)


def call_kernel(kernel, name, operands, specs, updated, out_shapes, scratch, flops):
    vmem = pl.BlockSpec(memory_space=pltpu.VMEM)
    operands = [*operands, *updated]
    shapes = [*(jax.ShapeDtypeStruct(value.shape, value.dtype) for value in updated), *out_shapes]
    first_in = len(operands) - len(updated)
    in_specs = [vmem] * len(operands)
    out_specs = [vmem] * len(shapes)
    for place, spec in specs.items():
        in_specs[place] = spec
        if place >= first_in:
            out_specs[place - first_in] = spec
    return pl.pallas_call(
        kernel,
        out_shape=shapes,
        in_specs=in_specs,
        out_specs=out_specs,
        scratch_shapes=scratch,
        input_output_aliases={first_in + i: i for i in range(len(updated))},
        compiler_params=pltpu.CompilerParams(vmem_limit_bytes=VMEM_BYTES),
        cost_estimate=pl.CostEstimate(flops=flops, bytes_accessed=flops // 1000, transcendentals=0),
        name=name,
    )(*operands)


def finish_kernel(early_ref, early_swapped_ref, late_ref, late_swapped_ref, table_ref, out_ref):
    rows = early_ref.shape[0]
    out_ref[:rows] = split_dot(early_ref[...] + early_swapped_ref[...], table_ref)
    out_ref[rows:] = split_dot(late_ref[...] + late_swapped_ref[...], table_ref)


def finish(values, table):
    rows, lags = values[0].shape
    return pl.pallas_call(
        finish_kernel,
        out_shape=jax.ShapeDtypeStruct((2 * rows, lags), F32),
        compiler_params=pltpu.CompilerParams(vmem_limit_bytes=VMEM_BYTES),
        cost_estimate=pl.CostEstimate(flops=10**9, bytes_accessed=10**6, transcendentals=0),
        name="finish",
    )(*values, table)


def on_device(waveforms, event_mask, station_weight, partners, pair_list, counts):
    events, stations, channels, samples = waveforms.shape
    rounds, _, all_pairs, _ = pair_list.shape
    clusters = lax.axis_size("cluster")
    length = lax.axis_size("station")
    assert (stations, channels, samples) == (HALF, 3, 2 * LANES)
    assert events % 4 == 0 and rounds % 2 == 0 and clusters % 2 == 0 and length % 4 == 0
    forward = jnp.asarray(forward_table(samples))
    inverse = jnp.asarray(inverse_table(samples))

    def to_sibling(value):
        return lax.ppermute(value, "cluster", [(i, i ^ 1) for i in range(clusters)])

    def to_across(value):
        return lax.ppermute(value, "cluster", [(i, (i + 1 if i % 2 else i - 1) % clusters) for i in range(clusters)])

    def to_mirror(value):
        return lax.ppermute(value, "station", [(i, length - 1 - i) for i in range(length)])

    swap = length == 4
    outs = 2 if swap else 1
    half_shape = jax.ShapeDtypeStruct((rounds * all_pairs // 4 // outs, 2 * samples), F32)
    spectra_shape = jax.ShapeDtypeStruct((3, events // 2 + 1, 2, 6, SUB, LANES), F32)
    sums = pltpu.VMEM((2, all_pairs // length * SUB, LANES), F32)

    smem = {0: pl.BlockSpec(memory_space=pltpu.SMEM)}

    def add_spectra(traces, places, spectra, flops):
        return call_kernel(
            lambda *refs: spectra_kernel(places, not spectra, *refs),
            "add_spectra",
            [*traces, forward],
            {},
            spectra,
            [] if spectra else [spectra_shape],
            [],
            flops,
        )

    own, first_piece, last_piece = prepare(waveforms, event_mask, station_weight)
    index = pair_index(partners, counts, pair_list, events)
    mirror_first = to_mirror(first_piece)
    mirror_last = to_mirror(last_piece)
    across = to_across(own)
    sibling = to_sibling(own)
    spectra, *partial = call_kernel(
        lambda *refs: first_near_kernel(outs, *refs),
        "first_near",
        [index, own, sibling, forward],
        smem,
        [],
        [spectra_shape] + [half_shape] * (2 * outs),
        [sums],
        1,
    )
    _, *partial = call_kernel(
        lambda *refs: first_far_kernel(outs, *refs),
        "first_far",
        [index, across, forward],
        smem,
        [spectra, *partial],
        [],
        [sums],
        1,
    )
    mirror_first, *partial = lax.optimization_barrier((mirror_first, *partial))
    far_first, near_first = to_across(mirror_first), to_sibling(mirror_first)
    (other,) = add_spectra([mirror_first], [(0, 0)], [], 1)
    mirror_last, other = lax.optimization_barrier((mirror_last, other))
    far_last, near_last = to_across(mirror_last), to_sibling(mirror_last)
    (other,) = add_spectra([mirror_last, near_first, far_first], [(0, 1), (1, 0), (2, 0)], [other], 1)
    other, *partial = call_kernel(
        lambda *refs: near_kernel(outs, *refs),
        "near_sums",
        [index, near_last, forward],
        smem,
        [other, *partial],
        [],
        [sums],
        1,
    )
    other, *early = call_kernel(
        lambda *refs: far_kernel(outs, 0, *refs),
        "far_sums",
        [index, far_last, forward],
        smem,
        [other, *partial[:outs]],
        [],
        [sums],
        1,
    )
    late = call_kernel(
        lambda *refs: far_kernel(outs, 1, *refs),
        "far_sums",
        [index, other],
        smem,
        partial[outs:],
        [],
        [sums],
        2 * 10**9,
    )
    values = []
    for half in (early, late):
        if swap:
            kept, sent = half
            received = lax.ppermute(sent, "station", [(i, i ^ 1) for i in range(length)])
        else:
            groups = np.arange(length).reshape(2, length // 2).tolist()
            value = half[0].reshape(rounds // 2, all_pairs // 2, 2 * samples)
            kept = lax.psum_scatter(value, "station", scatter_dimension=1, axis_index_groups=groups, tiled=True)
            kept = kept.reshape(-1, 2 * samples)
            received = jnp.zeros_like(kept)
        values += [kept, received]
    result = finish(values, inverse)
    return result.reshape(rounds, 1, all_pairs // length, 2 * samples)


def solution(mesh):
    return jax.shard_map(
        on_device,
        mesh=mesh,
        in_specs=(
            P(("groups", "cluster"), "station", None, None),
            P(("groups", "cluster"), "station"),
            P("groups"),
            P(None, "groups"),
            P(None, ("groups", "cluster"), None, None),
            P("groups"),
        ),
        out_specs=P(None, ("groups", "cluster"), "station", None),
        check_vma=False,
    )
```

```python
import math

import jax
import jax.numpy as jnp
import ml_dtypes
import numpy as np
from jax import lax
from jax.experimental import pallas as pl
from jax.experimental.pallas import tpu as pltpu
from jax.sharding import PartitionSpec as P

epsilon = 1e-06
SUB, LANES = 8, 128
HALF = SUB // 2
VMEM_BYTES = 16 * 1024 * 1024
PREPARE_VMEM_BYTES = 62 * 1024 * 1024
F32 = jnp.float32
BF16 = jnp.bfloat16


def split_table(table):
    high = table.astype(ml_dtypes.bfloat16)
    low = (table - high.astype(np.float64)).astype(ml_dtypes.bfloat16)
    return np.stack([high, low])


def forward_table(samples):
    steps = np.arange(samples)
    angles = (steps[:, None] * steps[None, :] % (2 * samples)) * (math.pi / samples)
    return split_table(np.concatenate([np.cos(angles), -np.sin(angles)], axis=1))


def inverse_table(samples):
    record = 2 * samples
    bins = np.arange(samples)
    lags = (np.arange(record) + samples) % record
    angles = (bins[:, None] * lags[None, :] % record) * (math.pi / samples)
    gain = np.where(bins == 0, 1.0, 2.0)[:, None] / record
    return split_table(np.concatenate([gain * np.cos(angles), -gain * np.sin(angles)], axis=0))


def split_dot(value, table_ref):
    rows = value.shape[0]
    high = value.astype(BF16)
    low = (value - high.astype(F32)).astype(BF16)
    both = jnp.dot(jnp.concatenate([high, low], axis=0), table_ref[0], preferred_element_type=F32)
    return both[:rows] + (both[rows:] + jnp.dot(high, table_ref[1], preferred_element_type=F32))


def prepare_kernel(waves_hbm, mask_hbm, weight_hbm, all_ref, *refs):
    *piece_refs, waves_ref, mask_ref, weight_ref, sems = refs
    copies = [
        pltpu.make_async_copy(weight_hbm, weight_ref, sems.at[0]),
        pltpu.make_async_copy(mask_hbm, mask_ref, sems.at[1]),
        pltpu.make_async_copy(waves_hbm, waves_ref, sems.at[2]),
    ]
    for copy in copies:
        copy.start()
    twos, _, channels, stations, _ = waves_ref.shape
    events = 2 * twos
    rows = 3 * SUB * twos
    row = lax.broadcasted_iota(jnp.int32, (rows, events), 0)
    group, row_here = row // (SUB * twos), row % (SUB * twos)
    event_of_row = jnp.where(group < 2, 2 * (row_here // SUB) + group, row_here // HALF)
    at_event = (event_of_row == lax.broadcasted_iota(jnp.int32, (rows, events), 1)).astype(F32)
    row = lax.broadcasted_iota(jnp.int32, (rows, stations), 0)
    at_station = row % HALF == lax.broadcasted_iota(jnp.int32, (rows, stations), 1)
    station_id = lax.broadcasted_iota(jnp.int32, (stations, events), 0)
    first_weight = lax.axis_index("station") * stations
    copies[0].wait()
    network = channels * sum(weight_ref[station] for station in range(weight_ref.shape[0]))
    weight = jnp.zeros((stations, events), F32)
    for station in range(stations):
        weight = jnp.where(station_id == station, weight_ref[first_weight + station], weight)
    copies[1].wait()
    amplitude = mask_ref[...].astype(F32) * jnp.sqrt(weight / network)
    picked = lax.dot_general(
        at_event,
        amplitude,
        (((1,), (1,)), ((), ())),
        precision=lax.Precision.HIGHEST,
        preferred_element_type=F32,
    )
    factor = jnp.sum(jnp.where(at_station, picked, 0.0), axis=1, keepdims=True).reshape(3, twos, SUB, 1)
    copies[2].wait()
    for group in range(3):
        for side in range(2):
            part = waves_ref[:, group, side] if group < 2 else waves_ref[:, side, 2]
            all_ref[group, :, side * HALF : (side + 1) * HALF, :] = part
        traces = all_ref[group]
        energy = jnp.sum(traces * traces, axis=-1, keepdims=True)
        traces = traces * (lax.rsqrt(energy + epsilon) * factor[group])
        all_ref[group] = traces
        for piece, piece_ref in enumerate(piece_refs):
            piece_ref[group] = traces[piece * twos // 2 : (piece + 1) * twos // 2]


def prepare(waveforms, event_mask, station_weight):
    events, stations, channels, samples = waveforms.shape
    waves = jnp.transpose(waveforms, (0, 2, 1, 3)).reshape(events // 2, 2, channels, stations, samples)
    hbm = pl.BlockSpec(memory_space=pltpu.HBM)
    vmem = pl.BlockSpec(memory_space=pltpu.VMEM)
    return pl.pallas_call(
        prepare_kernel,
        out_shape=[jax.ShapeDtypeStruct((3, events // share, SUB, samples), F32) for share in (2, 4, 4)],
        in_specs=[hbm] * 3,
        out_specs=[vmem] * 3,
        scratch_shapes=[
            pltpu.VMEM(waves.shape, F32),
            pltpu.VMEM((stations, events), event_mask.dtype),
            pltpu.SMEM(station_weight.shape, F32),
            pltpu.SemaphoreType.DMA((3,)),
        ],
        compiler_params=pltpu.CompilerParams(vmem_limit_bytes=PREPARE_VMEM_BYTES),
        name="prepare",
    )(waves, event_mask.T, station_weight)


def index_kernel(events, partners_ref, counts_ref, pairs_ref, index_ref, order_ref):
    rounds, _, _, all_pairs = pairs_ref.shape
    here = lax.axis_index("cluster")
    sibling = jnp.where(here % 2 == 0, here + 1, here - 1)
    own_count = counts_ref[here]
    partners = [partners_ref[turn, here] for turn in range(rounds)]
    parts = [jnp.where(partner == here, 0, jnp.where(partner == sibling, 1, 2)) for partner in partners]
    across = jnp.int32(0)
    for turn in range(rounds):
        part = parts[turn]
        across += (part == 2).astype(jnp.int32)
        place = jnp.int32(0)
        for other in range(rounds):
            ahead = parts[other] <= part if other < turn else parts[other] < part
            place += ahead.astype(jnp.int32)
        order_ref[place] = jnp.int32(turn)
        first, second = pairs_ref[turn, 0, 0:1], pairs_ref[turn, 0, 1:2]
        valid = (first < own_count) & (second < counts_ref[partners[turn]])
        index_ref[place, 0:1] = jnp.where(valid, first, events)
        index_ref[place, 1:2] = second + part * (events + 2)
        index_ref[place, 2:3] = jnp.full((1, all_pairs), part, jnp.int32)
    order_ref[rounds] = across


def pair_index(partners, counts, pair_list, events):
    rounds, _, all_pairs, _ = pair_list.shape
    vmem = pl.BlockSpec(memory_space=pltpu.VMEM)
    smem = pl.BlockSpec(memory_space=pltpu.SMEM)
    return pl.pallas_call(
        lambda *refs: index_kernel(events, *refs),
        out_shape=[
            jax.ShapeDtypeStruct((rounds, 3, all_pairs), jnp.int32),
            jax.ShapeDtypeStruct((rounds + 1,), jnp.int32),
        ],
        in_specs=[smem, smem, vmem],
        out_specs=[vmem, smem],
        compiler_params=pltpu.CompilerParams(vmem_limit_bytes=VMEM_BYTES),
        name="pair_index",
    )(partners, counts, jnp.transpose(pair_list, (0, 1, 3, 2)))


def fill_spectra(traces_ref, part, piece, table_ref, spectra_ref):
    _, twos, _, samples = traces_ref.shape
    spot = pl.ds(piece * twos, twos)
    spectrum = split_dot(traces_ref[...].reshape(3 * twos * SUB, samples), table_ref)
    tiles = [
        spectrum[:, block * LANES : (block + 1) * LANES].reshape(3, twos, SUB, LANES) for block in range(4)
    ]
    for group in range(2):
        for block in range(4):
            spectra_ref[part, spot, group, block + block // 2] = tiles[block][group]
    low_half = lax.broadcasted_iota(jnp.int32, (twos, SUB, LANES), 1) < HALF
    for side in range(2):
        lower, upper = tiles[2 * side][2], tiles[2 * side + 1][2]
        turned_lower, turned_upper = pltpu.roll(lower, HALF, 1), pltpu.roll(upper, HALF, 1)
        spectra_ref[part, spot, 0, 3 * side + 2] = jnp.where(low_half, lower, turned_upper)
        spectra_ref[part, spot, 1, 3 * side + 2] = jnp.where(low_half, turned_lower, upper)


def clear_last(spectra_ref):
    spectra_ref[0, spectra_ref.shape[1] - 1] = jnp.zeros(spectra_ref.shape[2:], F32)


def spectra_kernel(places, first, *refs):
    trace_refs, table_ref, spectra_ref = refs[: len(places)], refs[len(places)], refs[-1]
    for (part, piece), traces_ref in zip(places, trace_refs, strict=True):
        fill_spectra(traces_ref, part, piece, table_ref, spectra_ref)
    if first:
        clear_last(spectra_ref)


def add_pairs(index_ref, turns, wanted, spectra_ref, base_refs, out_refs, sums_ref):
    _, _, all_pairs = index_ref.shape
    slots = 2 * spectra_ref.shape[1]
    length = lax.axis_size("station")
    station_here = lax.axis_index("station")
    blocks = length // 2
    block_pairs = all_pairs // length
    flat_ref = spectra_ref.reshape(spectra_ref.shape[0] * slots, 6, SUB, LANES)
    low_half = lax.broadcasted_iota(jnp.int32, (SUB, LANES), 0) < HALF

    def folded(lower, upper, both):
        turned = pltpu.roll(jnp.where(low_half, upper, lower), HALF, 0)
        return jnp.where(low_half, lower, upper) + turned + both

    def one_turn(place, turn):
        for block in range(blocks):
            if len(out_refs) == 2:
                source = station_here if block == 0 else station_here + 1 - 2 * (station_here % 2)
            else:
                source = station_here // blocks * blocks + block
            start = source * block_pairs

            def one_pair(pair, carry):
                left = flat_ref.at[index_ref[turn, 0, start + pair]]
                right = flat_ref.at[index_ref[turn, 1, start + pair]]
                real, imag = [], []
                for tile in range(3):
                    left_real, left_imag = left[tile], left[tile + 3]
                    right_real, right_imag = right[tile], right[tile + 3]
                    real.append(left_real * right_real + left_imag * right_imag)
                    imag.append(left_imag * right_real - left_real * right_imag)
                spot = pl.multiple_of(pair * SUB, SUB)
                sums_ref[0, pl.ds(spot, SUB), :] = folded(*real)
                sums_ref[1, pl.ds(spot, SUB), :] = folded(*imag)
                return carry

            lax.fori_loop(0, block_pairs, one_pair, 0, unroll=min(16, block_pairs))
            if len(out_refs) == 2:
                which, row = block, place * block_pairs
            else:
                which, row = 0, (place * blocks + block) * block_pairs
            for side in range(2):
                for half in range(2):
                    spot = pl.ds((2 * side + half) * LANES, LANES)
                    total = None if base_refs is None else base_refs[which][row : row + block_pairs, spot]
                    for lane_row in range(HALF):
                        piece = sums_ref[side, pl.ds(half * HALF + lane_row, block_pairs, stride=SUB), :]
                        total = piece if total is None else total + piece
                    out_refs[which][row : row + block_pairs, spot] = total

    for place, turn in enumerate(turns):
        pl.when(wanted(index_ref[turn, 2, 0]))(lambda: one_turn(place, turn))


def half_turns(rounds, half):
    return range(half * rounds // 2, (half + 1) * rounds // 2)


def index_copy(index_hbm, index_ref, sem):
    copy = pltpu.make_async_copy(index_hbm, index_ref, sem)
    copy.start()
    return copy


def first_near_kernel(outs, index_hbm, own_ref, sibling_ref, table_ref, spectra_ref, *refs):
    *out_refs, sums_ref, index_ref, sem = refs
    copy = index_copy(index_hbm, index_ref, sem)
    fill_spectra(own_ref, 0, 0, table_ref, spectra_ref)
    fill_spectra(sibling_ref, 1, 0, table_ref, spectra_ref)
    clear_last(spectra_ref)
    copy.wait()
    for half in range(2):
        turns = half_turns(index_ref.shape[0], half)
        some = out_refs[half * outs : (half + 1) * outs]
        add_pairs(index_ref, turns, lambda part: part < 2, spectra_ref, None, some, sums_ref)


def first_far_kernel(outs, index_hbm, first_ref, last_ref, table_ref, *refs):
    spectra_ref, *out_refs, sums_ref, index_ref, sem = refs[2 * outs + 1 :]
    copy = index_copy(index_hbm, index_ref, sem)
    fill_spectra(first_ref, 2, 0, table_ref, spectra_ref)
    fill_spectra(last_ref, 2, 1, table_ref, spectra_ref)
    copy.wait()
    for half in range(2):
        turns = half_turns(index_ref.shape[0], half)
        some = out_refs[half * outs : (half + 1) * outs]
        add_pairs(index_ref, turns, lambda part: part == 2, spectra_ref, None, some, sums_ref)


def more_kernel(outs, places, half, parts, has_base, *refs):
    count = len(places)
    index_hbm, trace_refs, refs = refs[0], refs[1 : 1 + count], refs[1 + count :]
    if count:
        table_ref, refs = refs[0], refs[1:]
    base_refs, refs = (refs[1 : 1 + outs], refs[1 + outs :]) if has_base else (None, refs[1:])
    spectra_ref, *out_refs, sums_ref, index_ref, sem = refs
    copy = index_copy(index_hbm, index_ref, sem)
    for (traces_part, piece), traces_ref in zip(places, trace_refs, strict=True):
        fill_spectra(traces_ref, traces_part, piece, table_ref, spectra_ref)
    if not has_base:
        for out_ref in out_refs:
            out_ref[...] = jnp.zeros(out_ref.shape, F32)
    copy.wait()
    turns = half_turns(index_ref.shape[0], half)
    low, high = parts

    def wanted(part):
        return (part >= low) & (part <= high)

    add_pairs(index_ref, turns, wanted, spectra_ref, base_refs, out_refs, sums_ref)


def call_kernel(kernel, name, operands, specs, updated, out_shapes, scratch, flops):
    vmem = pl.BlockSpec(memory_space=pltpu.VMEM)
    operands = [*operands, *updated]
    shapes = [*(jax.ShapeDtypeStruct(value.shape, value.dtype) for value in updated), *out_shapes]
    first_in = len(operands) - len(updated)
    in_specs = [vmem] * len(operands)
    out_specs = [vmem] * len(shapes)
    for place, spec in specs.items():
        in_specs[place] = spec
        if place >= first_in:
            out_specs[place - first_in] = spec
    return pl.pallas_call(
        kernel,
        out_shape=shapes,
        in_specs=in_specs,
        out_specs=out_specs,
        scratch_shapes=scratch,
        input_output_aliases={first_in + i: i for i in range(len(updated))},
        compiler_params=pltpu.CompilerParams(vmem_limit_bytes=VMEM_BYTES),
        cost_estimate=pl.CostEstimate(flops=flops, bytes_accessed=flops // 1000, transcendentals=0),
        name=name,
    )(*operands)


def finish_kernel(half, order_ref, kept_ref, swapped_ref, table_ref, *refs):
    out_hbm, result_ref, order_smem, sems = refs[-4:]
    copy = index_copy(order_ref, order_smem, sems.at[0])
    places = half_turns(order_ref.shape[0] - 1, half)
    rows = kept_ref.shape[0] // len(places)
    result_ref[...] = split_dot(kept_ref[...] + swapped_ref[...], table_ref)
    copy.wait()
    copies = [
        pltpu.make_async_copy(
            result_ref.at[pl.ds(number * rows, rows)],
            out_hbm.at[pl.ds(pl.multiple_of(order_smem[place] * rows, SUB), rows)],
            sems.at[number],
        )
        for number, place in enumerate(places)
    ]
    for copy in copies:
        copy.start()
    for copy in copies:
        copy.wait()


def finish(order, kept, swapped, table, half, result):
    rows, lags = kept.shape
    vmem = pl.BlockSpec(memory_space=pltpu.VMEM)
    hbm = pl.BlockSpec(memory_space=pltpu.HBM)
    operands = [order, kept, swapped, table] + ([] if result is None else [result])
    return pl.pallas_call(
        lambda *refs: finish_kernel(half, *refs),
        out_shape=jax.ShapeDtypeStruct((2 * rows, lags), F32),
        in_specs=[pl.BlockSpec(memory_space=pl.ANY), vmem, vmem, vmem] + [hbm] * (len(operands) - 4),
        out_specs=hbm,
        scratch_shapes=[
            pltpu.VMEM((rows, lags), F32),
            pltpu.SMEM(order.shape, order.dtype),
            pltpu.SemaphoreType.DMA((order.shape[0] // 2,)),
        ],
        input_output_aliases={} if result is None else {4: 0},
        compiler_params=pltpu.CompilerParams(vmem_limit_bytes=VMEM_BYTES),
        cost_estimate=pl.CostEstimate(flops=1, bytes_accessed=1, transcendentals=0),
        name="finish",
    )(*operands)


def on_device(waveforms, event_mask, station_weight, partners, pair_list, counts):
    events, stations, channels, samples = waveforms.shape
    rounds, _, all_pairs, _ = pair_list.shape
    clusters = lax.axis_size("cluster")
    length = lax.axis_size("station")
    assert (stations, channels, samples) == (HALF, 3, 2 * LANES)
    assert events % 4 == 0 and rounds % 2 == 0 and clusters % 2 == 0 and length % 4 == 0
    forward = jnp.asarray(forward_table(samples))
    inverse = jnp.asarray(inverse_table(samples))

    def to_sibling(value):
        return lax.ppermute(value, "cluster", [(i, i ^ 1) for i in range(clusters)])

    def to_across(value):
        return lax.ppermute(value, "cluster", [(i, (i + 1 if i % 2 else i - 1) % clusters) for i in range(clusters)])

    def to_mirror(value):
        return lax.ppermute(value, "station", [(i, length - 1 - i) for i in range(length)])

    def swap_stations(value):
        return lax.ppermute(value, "station", [(i, i ^ 1) for i in range(length)])

    def spread(value):
        groups = np.arange(length).reshape(2, length // 2).tolist()
        value = value.reshape(rounds // 2, all_pairs // 2, 2 * samples)
        kept = lax.psum_scatter(value, "station", scatter_dimension=1, axis_index_groups=groups, tiled=True)
        kept = kept.reshape(-1, 2 * samples)
        return kept, jnp.zeros_like(kept)

    swap = length == 4
    outs = 2 if swap else 1
    half_shape = jax.ShapeDtypeStruct((rounds * all_pairs // 4 // outs, 2 * samples), F32)
    spectra_shape = jax.ShapeDtypeStruct((3, events // 2 + 1, 2, 6, SUB, LANES), F32)
    scratch = [
        pltpu.VMEM((2, all_pairs // length * SUB, LANES), F32),
        pltpu.SMEM((rounds, 3, all_pairs), jnp.int32),
        pltpu.SemaphoreType.DMA,
    ]

    anywhere = {0: pl.BlockSpec(memory_space=pl.ANY)}

    def add_spectra(traces, places, spectra, flops):
        return call_kernel(
            lambda *refs: spectra_kernel(places, not spectra, *refs),
            "add_spectra",
            [*traces, forward],
            {},
            spectra,
            [] if spectra else [spectra_shape],
            [],
            flops,
        )

    def more_sums(name, traces, places, half, parts, spectra, base):
        return call_kernel(
            lambda *refs: more_kernel(outs, places, half, parts, bool(base), *refs),
            name,
            [index, *traces, forward] if traces else [index],
            anywhere,
            [spectra, *base],
            [] if base else [half_shape] * outs,
            scratch,
            1,
        )

    own, first_piece, last_piece = prepare(waveforms, event_mask, station_weight)
    index, order = pair_index(partners, counts, pair_list, events)
    mirror_first, mirror_last = to_mirror(first_piece), to_mirror(last_piece)
    across = [to_across(first_piece), to_across(last_piece)]
    sibling = to_sibling(own)
    spectra, *partial = call_kernel(
        lambda *refs: first_near_kernel(outs, *refs),
        "first_near",
        [index, own, sibling, forward],
        anywhere,
        [],
        [spectra_shape] + [half_shape] * (2 * outs),
        scratch,
        1,
    )
    mirror_first, *partial = lax.optimization_barrier((mirror_first, *partial))
    far_first, near_first = to_across(mirror_first), to_sibling(mirror_first)
    (other,) = add_spectra([mirror_first], [(0, 0)], [], 1)
    other, *partial = lax.optimization_barrier((other, *partial))
    _, *partial = call_kernel(
        lambda *refs: first_far_kernel(outs, *refs),
        "first_far",
        [index, *across, forward],
        anywhere,
        [spectra, *partial],
        [],
        scratch,
        1,
    )
    mirror_last, other, *partial = lax.optimization_barrier((mirror_last, other, *partial))
    far_last, near_last = to_across(mirror_last), to_sibling(mirror_last)
    early, late = partial[:outs], partial[outs:]
    other, *early = more_sums("own_sums", [mirror_last], [(0, 1)], 0, (0, 0), other, early)
    (other,) = add_spectra([near_first, far_first], [(1, 0), (2, 0)], [other], 1)
    other, *early = more_sums("sibling_sums", [near_last], [(1, 1)], 0, (1, 1), other, early)
    if swap:
        early.append(swap_stations(early.pop()))
    other, *late = more_sums("near_sums", [], [], 1, (0, 1), other, late)
    other, *late = more_sums("across_sums", [far_last], [(2, 1)], 1, (2, 2), other, late)
    if swap:
        late.append(swap_stations(late.pop()))

        def with_across(spectra, kept):
            _, more_kept, more_sent = more_sums("across_sums", [], [], 0, (2, 2), spectra, [])
            return kept + more_kept + swap_stations(more_sent)

        early[0] = lax.cond(order[rounds] > rounds // 2, with_across, lambda _, kept: kept, other, early[0])
    else:
        _, *early = more_sums("across_sums", [], [], 0, (2, 2), other, early)
        early, late = spread(early[0]), spread(late[0])
    result = finish(order, *early, inverse, 0, None)
    result = finish(order, *late, inverse, 1, result)
    return result.reshape(rounds, 1, all_pairs // length, 2 * samples)


def solution(mesh):
    return jax.shard_map(
        on_device,
        mesh=mesh,
        in_specs=(
            P(("groups", "cluster"), "station", None, None),
            P(("groups", "cluster"), "station"),
            P("groups"),
            P(None, "groups"),
            P(None, ("groups", "cluster"), None, None),
            P("groups"),
        ),
        out_specs=P(None, ("groups", "cluster"), "station", None),
        check_vma=False,
    )
```

```python
import math

import jax
import jax.numpy as jnp
import ml_dtypes
import numpy as np
from jax import lax
from jax.experimental import pallas as pl
from jax.experimental.pallas import tpu as pltpu
from jax.sharding import PartitionSpec as P

epsilon = 1e-06
SUB, LANES = 8, 128
HALF = SUB // 2
TILES = 6
ENTRIES = 3
UNROLL = 4
FIRST_SHARE = 9
VMEM_BYTES = 16 * 1024 * 1024
PREPARE_VMEM_BYTES = 62 * 1024 * 1024
F32 = jnp.float32
BF16 = jnp.bfloat16


def split_table(table):
    high = table.astype(ml_dtypes.bfloat16)
    low = (table - high.astype(np.float64)).astype(ml_dtypes.bfloat16)
    return np.stack([high, low])


def forward_table(samples):
    steps = np.arange(samples)
    angles = (steps[:, None] * steps[None, :] % (2 * samples)) * (math.pi / samples)
    return split_table(np.concatenate([np.cos(angles), -np.sin(angles)], axis=1))


def inverse_table(samples):
    record = 2 * samples
    bins = np.arange(samples)
    lags = (np.arange(record) + samples) % record
    angles = (bins[:, None] * lags[None, :] % record) * (math.pi / samples)
    gain = np.where(bins == 0, 1.0, 2.0)[:, None] / record
    return split_table(np.concatenate([gain * np.cos(angles), -gain * np.sin(angles)], axis=0))


def split_dot(value, table_ref):
    rows = value.shape[0]
    high = value.astype(BF16)
    low = (value - high.astype(F32)).astype(BF16)
    both = jnp.dot(jnp.concatenate([high, low], axis=0), table_ref[0], preferred_element_type=F32)
    return both[:rows] + (both[rows:] + jnp.dot(high, table_ref[1], preferred_element_type=F32))


def piece_spots(twos):
    count = twos * FIRST_SHARE // 16
    return [(0, count), (count, twos - count)]


def prepare_kernel(waves_hbm, mask_hbm, weight_hbm, *refs):
    all_hbm, *out_hbms, waves_ref, mask_ref, weight_ref, result_ref, sems = refs
    pieces = len(out_hbms)
    twos, _, channels, stations, _ = waves_ref.shape
    spots = piece_spots(twos)
    copies = [
        pltpu.make_async_copy(weight_hbm, weight_ref, sems.at[0]),
        pltpu.make_async_copy(mask_hbm, mask_ref, sems.at[1]),
    ]
    for piece, (first, count) in enumerate(spots):
        spot = pl.ds(first, count)
        copies.append(pltpu.make_async_copy(waves_hbm.at[spot], waves_ref.at[spot], sems.at[2 + piece]))
    for copy in copies:
        copy.start()
    events = 2 * twos
    rows = 3 * SUB * twos
    row = lax.broadcasted_iota(jnp.int32, (rows, events), 0)
    group, row_here = row // (SUB * twos), row % (SUB * twos)
    event_of_row = jnp.where(group < 2, 2 * (row_here // SUB) + group, row_here // HALF)
    at_event = (event_of_row == lax.broadcasted_iota(jnp.int32, (rows, events), 1)).astype(F32)
    row = lax.broadcasted_iota(jnp.int32, (rows, stations), 0)
    at_station = row % HALF == lax.broadcasted_iota(jnp.int32, (rows, stations), 1)
    station_id = lax.broadcasted_iota(jnp.int32, (stations, events), 0)
    first_weight = lax.axis_index("station") * stations
    copies[0].wait()
    network = channels * sum(weight_ref[station] for station in range(weight_ref.shape[0]))
    weight = jnp.zeros((stations, events), F32)
    for station in range(stations):
        weight = jnp.where(station_id == station, weight_ref[first_weight + station], weight)
    copies[1].wait()
    amplitude = mask_ref[...].astype(F32) * jnp.sqrt(weight / network)
    picked = lax.dot_general(
        at_event,
        amplitude,
        (((1,), (1,)), ((), ())),
        precision=lax.Precision.HIGHEST,
        preferred_element_type=F32,
    )
    factor = jnp.sum(jnp.where(at_station, picked, 0.0), axis=1, keepdims=True).reshape(3, twos, SUB, 1)
    results = []
    for piece, (first, count) in enumerate(spots):
        copies[2 + piece].wait()
        spot = slice(first, first + count)
        for group in range(3):
            for side in range(2):
                part = waves_ref[spot, group, side] if group < 2 else waves_ref[spot, side, 2]
                result_ref[group, spot, side * HALF : (side + 1) * HALF, :] = part
            traces = result_ref[group, spot]
            energy = jnp.sum(traces * traces, axis=-1, keepdims=True)
            result_ref[group, spot] = traces * (lax.rsqrt(energy + epsilon) * factor[group, spot])
        for number, target in enumerate((out_hbms[piece], all_hbm.at[:, pl.ds(first, count)])):
            sem = sems.at[2 + pieces + 2 * piece + number]
            results.append(pltpu.make_async_copy(result_ref.at[:, pl.ds(first, count)], target, sem))
            results[-1].start()
    for copy in results:
        copy.wait()


def prepare(waveforms, event_mask, station_weight):
    events, stations, channels, samples = waveforms.shape
    waves = jnp.transpose(waveforms, (0, 2, 1, 3)).reshape(events // 2, 2, channels, stations, samples)
    hbm = pl.BlockSpec(memory_space=pltpu.HBM)
    spots = piece_spots(events // 2)
    pieces = len(spots)
    shape = (3, events // 2, SUB, samples)
    return pl.pallas_call(
        prepare_kernel,
        out_shape=[jax.ShapeDtypeStruct(shape, F32)]
        + [jax.ShapeDtypeStruct((3, count, SUB, samples), F32) for _, count in spots],
        in_specs=[hbm] * 3,
        out_specs=[hbm] * (1 + pieces),
        scratch_shapes=[
            pltpu.VMEM(waves.shape, F32),
            pltpu.VMEM((stations, events), event_mask.dtype),
            pltpu.SMEM(station_weight.shape, F32),
            pltpu.VMEM(shape, F32),
            pltpu.SemaphoreType.DMA((2 + 3 * pieces,)),
        ],
        compiler_params=pltpu.CompilerParams(vmem_limit_bytes=PREPARE_VMEM_BYTES),
        name="prepare",
    )(waves, event_mask.T, station_weight)


def index_kernel(events, partners_ref, counts_ref, pairs_ref, index_ref, order_ref):
    rounds, _, _, all_pairs = pairs_ref.shape
    here = lax.axis_index("cluster")
    sibling = jnp.where(here % 2 == 0, here + 1, here - 1)
    own_count = counts_ref[here]
    partners = [partners_ref[turn, here] for turn in range(rounds)]
    parts = [jnp.where(partner == here, 0, jnp.where(partner == sibling, 1, 2)) for partner in partners]
    across = jnp.int32(0)
    lane = lax.broadcasted_iota(jnp.int32, (1, LANES), 1)
    order = jnp.zeros((1, LANES), jnp.int32)
    for turn in range(rounds):
        part = parts[turn]
        across += (part == 2).astype(jnp.int32)
        place = jnp.int32(0)
        for other in range(rounds):
            ahead = parts[other] <= part if other < turn else parts[other] < part
            place += ahead.astype(jnp.int32)
        order = jnp.where(lane == place, turn, order)
        first, second = pairs_ref[turn, 0, 0:1], pairs_ref[turn, 0, 1:2]
        valid = (first < own_count) & (second < counts_ref[partners[turn]])
        entries = (
            TILES * jnp.where(valid, first, events),
            TILES * (second + part * (events + 2)),
            jnp.full((1, all_pairs), part, jnp.int32),
        )
        for kind, entry in enumerate(entries):
            for row in range(all_pairs // LANES):
                spot = (ENTRIES * place + kind) * (all_pairs // LANES) + row
                index_ref[pl.ds(spot, 1)] = entry[:, row * LANES : (row + 1) * LANES]
    order_ref[...] = jnp.where(lane == rounds, across, order)


def pair_index(partners, counts, pair_list, events):
    rounds, _, all_pairs, _ = pair_list.shape
    vmem = pl.BlockSpec(memory_space=pltpu.VMEM)
    smem = pl.BlockSpec(memory_space=pltpu.SMEM)
    return pl.pallas_call(
        lambda *refs: index_kernel(events, *refs),
        out_shape=[
            jax.ShapeDtypeStruct((rounds * ENTRIES * all_pairs // LANES, LANES), jnp.int32),
            jax.ShapeDtypeStruct((1, LANES), jnp.int32),
        ],
        in_specs=[smem, smem, vmem],
        out_specs=[vmem, vmem],
        compiler_params=pltpu.CompilerParams(vmem_limit_bytes=VMEM_BYTES),
        name="pair_index",
    )(partners, counts, jnp.transpose(pair_list, (0, 1, 3, 2)))


def fill_spectra(traces_ref, part, first, table_ref, spectra_ref):
    _, twos, _, samples = traces_ref.shape
    spot = pl.ds(first, twos)
    spectrum = split_dot(traces_ref[...].reshape(3 * twos * SUB, samples), table_ref)
    tiles = [
        spectrum[:, block * LANES : (block + 1) * LANES].reshape(3, twos, SUB, LANES) for block in range(4)
    ]
    low_half = lax.broadcasted_iota(jnp.int32, (twos, SUB, LANES), 1) < HALF
    for group in range(3):
        for side in range(2):
            lower, upper = tiles[2 * side][group], tiles[2 * side + 1][group]
            first = jnp.where(low_half, lower, pltpu.roll(upper, HALF, 1))
            second = jnp.where(low_half, pltpu.roll(lower, HALF, 1), upper)
            if group < 2:
                spectra_ref[part, spot, group, 3 * side] = first
                spectra_ref[part, spot, group, 3 * side + 1] = second
            else:
                spectra_ref[part, spot, 0, 3 * side + 2] = first
                spectra_ref[part, spot, 1, 3 * side + 2] = second


def clear_last(spectra_ref):
    spectra_ref[0, spectra_ref.shape[1] - 1] = jnp.zeros(spectra_ref.shape[2:], F32)


def spectra_kernel(places, first, *refs):
    trace_refs, table_ref, spectra_ref = refs[: len(places)], refs[len(places)], refs[-1]
    for (part, pair), traces_ref in zip(places, trace_refs, strict=True):
        fill_spectra(traces_ref, part, pair, table_ref, spectra_ref)
    if first:
        clear_last(spectra_ref)


def add_pairs(index_ref, all_pairs, turns, wanted, blocks, spectra_ref, base_refs, out_refs):
    slots = 2 * spectra_ref.shape[1]
    length = lax.axis_size("station")
    station_here = lax.axis_index("station")
    swap = length == 4
    block_pairs = all_pairs // length
    flat_ref = spectra_ref.reshape(spectra_ref.shape[0] * slots * TILES, SUB, LANES)
    row_id = lax.broadcasted_iota(jnp.int32, (SUB, LANES), 0)
    in_four, in_two, in_one = row_id < 4, row_id % 4 < 2, row_id % 2 < 1

    def down(value, rows):
        return pltpu.roll(value, rows % SUB, 0)

    def fold_four(sums):
        even, odd = (
            jnp.where(in_two, one + down(one, -2), other + down(other, 2)) for one, other in (sums[0::2], sums[1::2])
        )
        return jnp.where(in_one, even + down(even, -1), odd + down(odd, 1))

    def fold_eight(sums):
        one, other = fold_four(sums[:4]), fold_four(sums[4:])
        return jnp.where(in_four, one, down(other, 4)), jnp.where(in_four, down(one, 4), other)

    def one_turn(place, turn):
        for number, block in enumerate(blocks):
            if swap:
                source = station_here if block == 0 else station_here + 1 - 2 * (station_here % 2)
                which, row = number, place * block_pairs
            else:
                source = station_here // len(blocks) * len(blocks) + block
                which, row = 0, (place * len(blocks) + block) * block_pairs
            start = source * block_pairs

            def eight_pairs(group, carry):
                real, imag = [], []
                first = start + group * SUB
                for spot in range(SUB):
                    entry = ENTRIES * turn * all_pairs + spot
                    left = flat_ref[pl.ds(index_ref[entry + first], TILES)]
                    right = flat_ref[pl.ds(index_ref[entry + all_pairs + first], TILES)]
                    reals, imags = [], []
                    for tile in range(3):
                        left_real, left_imag = left[tile], left[tile + 3]
                        right_real, right_imag = right[tile], right[tile + 3]
                        reals.append(left_real * right_real + left_imag * right_imag)
                        imags.append(left_imag * right_real - left_real * right_imag)
                    real.append(reals[0] + reals[1] + reals[2])
                    imag.append(imags[0] + imags[1] + imags[2])
                rows = pl.ds(pl.multiple_of(row + group * SUB, SUB), SUB)
                for column, total in enumerate((*fold_eight(real), *fold_eight(imag))):
                    spot = pl.ds(column * LANES, LANES)
                    if base_refs is not None:
                        total += base_refs[which][rows, spot]
                    out_refs[which][rows, spot] = total
                return carry

            lax.fori_loop(0, block_pairs // SUB, eight_pairs, 0, unroll=min(UNROLL, block_pairs // SUB))

    for place, turn in enumerate(turns):
        pl.when(wanted(index_ref[(ENTRIES * turn + 2) * all_pairs]))(lambda: one_turn(place, turn))


def half_turns(rounds, half):
    return range(half * rounds // 2, (half + 1) * rounds // 2)


def index_copy(index_hbm, index_ref, sem):
    copy = pltpu.make_async_copy(index_hbm, index_ref, sem)
    copy.start()
    return copy


def first_near_kernel(blocks, rounds, all_pairs, index_hbm, own_ref, sibling_ref, table_ref, spectra_ref, *refs):
    *out_refs, index_ref, sem = refs
    copy = index_copy(index_hbm, index_ref, sem)
    fill_spectra(own_ref, 0, 0, table_ref, spectra_ref)
    fill_spectra(sibling_ref, 1, 0, table_ref, spectra_ref)
    clear_last(spectra_ref)
    copy.wait()
    for half in range(2):
        turns = half_turns(rounds, half)
        some = out_refs[half * len(out_refs) // 2 : (half + 1) * len(out_refs) // 2]
        add_pairs(index_ref, all_pairs, turns, lambda part: part < 2, blocks, spectra_ref, None, some)


def first_far_kernel(blocks, rounds, all_pairs, index_hbm, first_ref, last_ref, table_ref, *refs):
    spectra_ref, *out_refs, index_ref, sem = refs[len(refs) // 2 - 1 :]
    copy = index_copy(index_hbm, index_ref, sem)
    fill_spectra(first_ref, 2, 0, table_ref, spectra_ref)
    fill_spectra(last_ref, 2, first_ref.shape[1], table_ref, spectra_ref)
    copy.wait()
    for half in range(2):
        turns = half_turns(rounds, half)
        some = out_refs[half * len(out_refs) // 2 : (half + 1) * len(out_refs) // 2]
        add_pairs(index_ref, all_pairs, turns, lambda part: part == 2, blocks, spectra_ref, None, some)


def more_kernel(rounds, all_pairs, places, jobs, has_base, *refs):
    count = len(places)
    index_hbm, trace_refs, refs = refs[0], refs[1 : 1 + count], refs[1 + count :]
    if count:
        table_ref, refs = refs[0], refs[1:]
    *refs, index_ref, sem = refs
    arrays = len(refs) // 2 - 1 if has_base else len(refs) - 2
    base_refs, (spectra_ref, *out_refs) = refs[1 : 1 + arrays] if has_base else None, refs[-1 - arrays :]
    copy = index_copy(index_hbm, index_ref, sem)
    for (part, pair), traces_ref in zip(places, trace_refs, strict=True):
        fill_spectra(traces_ref, part, pair, table_ref, spectra_ref)
    if not has_base:
        for out_ref in out_refs:
            out_ref[...] = jnp.zeros(out_ref.shape, F32)
    copy.wait()
    for half, parts, blocks, first, last in jobs:

        def wanted(part, parts=parts):
            return (part >= parts[0]) & (part <= parts[-1])

        turns = half_turns(rounds, half)
        base = base_refs[first:last] if has_base else None
        add_pairs(index_ref, all_pairs, turns, wanted, blocks, spectra_ref, base, out_refs[first:last])


def call_kernel(kernel, name, operands, specs, updated, out_shapes, scratch, flops):
    vmem = pl.BlockSpec(memory_space=pltpu.VMEM)
    operands = [*operands, *updated]
    shapes = [*(jax.ShapeDtypeStruct(value.shape, value.dtype) for value in updated), *out_shapes]
    first_in = len(operands) - len(updated)
    in_specs = [vmem] * len(operands)
    out_specs = [vmem] * len(shapes)
    for place, spec in specs.items():
        in_specs[place] = spec
        if place >= first_in:
            out_specs[place - first_in] = spec
    return pl.pallas_call(
        kernel,
        out_shape=shapes,
        in_specs=in_specs,
        out_specs=out_specs,
        scratch_shapes=scratch,
        input_output_aliases={first_in + i: i for i in range(len(updated))},
        compiler_params=pltpu.CompilerParams(vmem_limit_bytes=VMEM_BYTES),
        cost_estimate=pl.CostEstimate(flops=flops, bytes_accessed=flops // 1000, transcendentals=0),
        name=name,
    )(*operands)


def invert_kernel(cross_ref, table_ref, out_ref):
    out_ref[...] = split_dot(cross_ref[...], table_ref)


def finish_kernel(turns, invert, order_ref, kept_ref, swapped_ref, table_ref, *refs):
    out_hbm, result_ref, sems = refs[-3:]
    rows = kept_ref.shape[0] // len(turns)
    lane = lax.broadcasted_iota(jnp.int32, (1, LANES), 1)
    order = order_ref[...].astype(F32)
    targets = [jnp.sum(jnp.where(lane == turn, order, 0.0)).astype(jnp.int32) for turn in turns]
    total = kept_ref[...] + swapped_ref[...]
    result_ref[...] = split_dot(total, table_ref) if invert else total
    copies = [
        pltpu.make_async_copy(
            result_ref.at[pl.ds(number * rows, rows)],
            out_hbm.at[pl.ds(pl.multiple_of(target * rows, SUB), rows)],
            sems.at[number],
        )
        for number, target in enumerate(targets)
    ]
    for copy in copies:
        copy.start()
    for copy in copies:
        copy.wait()


def finish(order, kept, swapped, table, turns, invert, result):
    rows, lags = kept.shape
    vmem = pl.BlockSpec(memory_space=pltpu.VMEM)
    hbm = pl.BlockSpec(memory_space=pltpu.HBM)
    operands = [order, kept, swapped, table] + ([] if result is None else [result])
    return pl.pallas_call(
        lambda *refs: finish_kernel(turns, invert, *refs),
        out_shape=jax.ShapeDtypeStruct((2 * rows, lags), F32),
        in_specs=[vmem] * 4 + [hbm] * (len(operands) - 4),
        out_specs=hbm,
        scratch_shapes=[
            pltpu.VMEM((rows, lags), F32),
            pltpu.SemaphoreType.DMA((len(turns),)),
        ],
        input_output_aliases={} if result is None else {4: 0},
        compiler_params=pltpu.CompilerParams(vmem_limit_bytes=VMEM_BYTES),
        cost_estimate=pl.CostEstimate(flops=1, bytes_accessed=1, transcendentals=0),
        name="finish",
    )(*operands)


def on_device(waveforms, event_mask, station_weight, partners, pair_list, counts):
    events, stations, channels, samples = waveforms.shape
    rounds, _, all_pairs, _ = pair_list.shape
    clusters = lax.axis_size("cluster")
    length = lax.axis_size("station")
    assert (stations, channels, samples) == (HALF, 3, 2 * LANES)
    assert events % 4 == 0 and rounds % 2 == 0 and clusters % 2 == 0 and length % 4 == 0
    forward = jnp.asarray(forward_table(samples))
    inverse = jnp.asarray(inverse_table(samples))

    def to_sibling(value):
        return lax.ppermute(value, "cluster", [(i, i ^ 1) for i in range(clusters)])

    def to_across(value):
        return lax.ppermute(value, "cluster", [(i, (i + 1 if i % 2 else i - 1) % clusters) for i in range(clusters)])

    def to_mirror(value):
        return lax.ppermute(value, "station", [(i, length - 1 - i) for i in range(length)])

    def swap_stations(value):
        return lax.ppermute(value, "station", [(i, i ^ 1) for i in range(length)])

    def spread(value):
        groups = np.arange(length).reshape(2, length // 2).tolist()
        value = value.reshape(rounds // 2, all_pairs // 2, 2 * samples)
        kept = lax.psum_scatter(value, "station", scatter_dimension=1, axis_index_groups=groups, tiled=True)
        kept = kept.reshape(-1, 2 * samples)
        return kept, jnp.zeros_like(kept)

    def invert(cross, table):
        return call_kernel(invert_kernel, "invert", [cross, table], {}, [], [half_shape], [], 1)[0]

    swap = length == 4
    blocks = list(range(length // 2))
    outs = 2 if swap else 1
    half_shape = jax.ShapeDtypeStruct((rounds * all_pairs // 4 // outs, 2 * samples), F32)
    spectra_shape = jax.ShapeDtypeStruct((3, events // 2 + 1, 2, TILES, SUB, LANES), F32)
    scratch = [
        pltpu.SMEM((rounds * ENTRIES * all_pairs,), jnp.int32),
        pltpu.SemaphoreType.DMA,
    ]

    anywhere = {0: pl.BlockSpec(memory_space=pl.ANY)}

    def add_spectra(traces, places, spectra, flops):
        return call_kernel(
            lambda *refs: spectra_kernel(places, not spectra, *refs),
            "add_spectra",
            [*traces, forward],
            {},
            spectra,
            [] if spectra else [spectra_shape],
            [],
            flops,
        )

    def more_sums(name, traces, places, jobs, spectra, base):
        return call_kernel(
            lambda *refs: more_kernel(rounds, all_pairs, places, jobs, bool(base), *refs),
            name,
            [index, *traces, forward] if traces else [index],
            anywhere,
            [spectra, *base],
            [] if base else [half_shape] * outs,
            scratch,
            1,
        )

    own, *pieces = prepare(waveforms, event_mask, station_weight)
    index, order = pair_index(partners, counts, pair_list, events)
    index = index.reshape(-1)
    mirror_first, mirror_last = (to_mirror(piece) for piece in pieces)
    across = [to_across(piece) for piece in pieces]
    sibling = to_sibling(own)
    spectra, *partial = call_kernel(
        lambda *refs: first_near_kernel(blocks, rounds, all_pairs, *refs),
        "first_near",
        [index, own, sibling, forward],
        anywhere,
        [],
        [spectra_shape] + [half_shape] * (2 * outs),
        scratch,
        1,
    )
    mirror_first, *partial = lax.optimization_barrier((mirror_first, *partial))
    far_first, near_first = to_across(mirror_first), to_sibling(mirror_first)
    (other,) = add_spectra([mirror_first], [(0, 0)], [], 1)
    other, *partial = lax.optimization_barrier((other, *partial))
    _, *partial = call_kernel(
        lambda *refs: first_far_kernel(blocks, rounds, all_pairs, *refs),
        "first_far",
        [index, *across, forward],
        anywhere,
        [spectra, *partial],
        [],
        scratch,
        1,
    )
    mirror_last, other, *partial = lax.optimization_barrier((mirror_last, other, *partial))
    far_last, near_last = to_across(mirror_last), to_sibling(mirror_last)
    early, late = partial[:outs], partial[outs:]
    later = piece_spots(events // 2)[1][0]
    sent = blocks[1:] if swap else blocks
    *early_kept, early_sent = early
    *late_kept, late_sent = late

    def add_sent(name, traces, places, half, parts, spectra, value):
        return more_sums(name, traces, places, [(half, parts, sent, 0, 1)], spectra, [value])

    other, early_sent = add_sent("own_sums", [mirror_last], [(0, later)], 0, (0,), other, early_sent)
    (other,) = add_spectra([near_first], [(1, 0)], [other], 1)
    other, early_sent = add_sent("sibling_sums", [near_last], [(1, later)], 0, (1,), other, early_sent)
    if not swap:
        other, late_sent = add_sent("near_sums", [far_first], [(2, 0)], 1, (0, 1), other, late_sent)
        other, late_sent = add_sent("across_sums", [far_last], [(2, later)], 1, (2,), other, late_sent)
        other, early_sent = add_sent("across_sums", [], [], 0, (2,), other, early_sent)
        early, late = spread(early_sent), spread(late_sent)
    else:
        early_received = swap_stations(early_sent)
        other, late_sent = add_sent("near_sums", [far_first], [(2, 0)], 1, (0, 1), other, late_sent)
        other, late_sent = add_sent("across_sums", [far_last], [(2, later)], 1, (2,), other, late_sent)
        late_received = swap_stations(invert(late_sent, inverse))
        jobs = [(0, (0, 1), blocks[:1], 0, 1), (1, (0, 2), blocks[:1], 1, 2)]
        other, early_kept, late_kept = more_sums("kept_sums", [], [], jobs, other, early_kept + late_kept)

        def with_across(spectra, kept):
            jobs = [(0, (2,), blocks, 0, 2)]
            _, more_kept, more_sent = more_sums("across_sums", [], [], jobs, spectra, [])
            return kept + more_kept + swap_stations(more_sent)

        early_kept = lax.cond(order[0, rounds] > rounds // 2, with_across, lambda _, kept: kept, other, early_kept)
        early, late = (early_kept, early_received), (invert(late_kept, inverse), late_received)
    result = finish(order, *early, inverse, half_turns(rounds, 0), True, None)
    result = finish(order, *late, inverse, half_turns(rounds, 1), not swap, result)
    return result.reshape(rounds, 1, all_pairs // length, 2 * samples)


def solution(mesh):
    return jax.shard_map(
        on_device,
        mesh=mesh,
        in_specs=(
            P(("groups", "cluster"), "station", None, None),
            P(("groups", "cluster"), "station"),
            P("groups"),
            P(None, "groups"),
            P(None, ("groups", "cluster"), None, None),
            P("groups"),
        ),
        out_specs=P(None, ("groups", "cluster"), "station", None),
        check_vma=False,
    )
```

```python
import math

import jax
import jax.numpy as jnp
import ml_dtypes
import numpy as np
from jax import lax
from jax.experimental import pallas as pl
from jax.experimental.pallas import tpu as pltpu
from jax.sharding import PartitionSpec as P

epsilon = 1e-06
SUB, LANES = 8, 128
HALF = SUB // 2
TILES = 6
ENTRIES = 3
UNROLL = 4
FIRST_SHARE = 9
VMEM_BYTES = 16 * 1024 * 1024
PREPARE_VMEM_BYTES = 62 * 1024 * 1024
F32 = jnp.float32
BF16 = jnp.bfloat16


def split_table(table):
    high = table.astype(ml_dtypes.bfloat16)
    low = (table - high.astype(np.float64)).astype(ml_dtypes.bfloat16)
    return np.stack([high, low])


def forward_table(samples):
    steps = np.arange(samples)
    angles = (steps[:, None] * steps[None, :] % (2 * samples)) * (math.pi / samples)
    return split_table(np.concatenate([np.cos(angles), -np.sin(angles)], axis=1))


def inverse_table(samples):
    record = 2 * samples
    bins = np.arange(samples)
    lags = (np.arange(record) + samples) % record
    angles = (bins[:, None] * lags[None, :] % record) * (math.pi / samples)
    gain = np.where(bins == 0, 1.0, 2.0)[:, None] / record
    return split_table(np.concatenate([gain * np.cos(angles), -gain * np.sin(angles)], axis=0))


def split_dot(value, table_ref):
    rows = value.shape[0]
    high = value.astype(BF16)
    low = (value - high.astype(F32)).astype(BF16)
    both = jnp.dot(jnp.concatenate([high, low], axis=0), table_ref[0], preferred_element_type=F32)
    return both[:rows] + (both[rows:] + jnp.dot(high, table_ref[1], preferred_element_type=F32))


def piece_spots(twos):
    count = twos * FIRST_SHARE // 16
    return [(0, count), (count, twos - count)]


def prepare_kernel(waves_hbm, mask_hbm, weight_hbm, *refs):
    all_hbm, *out_hbms, waves_ref, mask_ref, weight_ref, result_ref, sems = refs
    pieces = len(out_hbms)
    twos, _, channels, stations, _ = waves_ref.shape
    spots = piece_spots(twos)
    copies = [
        pltpu.make_async_copy(weight_hbm, weight_ref, sems.at[0]),
        pltpu.make_async_copy(mask_hbm, mask_ref, sems.at[1]),
    ]
    for piece, (first, count) in enumerate(spots):
        spot = pl.ds(first, count)
        copies.append(pltpu.make_async_copy(waves_hbm.at[spot], waves_ref.at[spot], sems.at[2 + piece]))
    for copy in copies:
        copy.start()
    events = 2 * twos
    rows = 3 * SUB * twos
    row = lax.broadcasted_iota(jnp.int32, (rows, events), 0)
    group, row_here = row // (SUB * twos), row % (SUB * twos)
    event_of_row = jnp.where(group < 2, 2 * (row_here // SUB) + group, row_here // HALF)
    at_event = (event_of_row == lax.broadcasted_iota(jnp.int32, (rows, events), 1)).astype(F32)
    row = lax.broadcasted_iota(jnp.int32, (rows, stations), 0)
    at_station = row % HALF == lax.broadcasted_iota(jnp.int32, (rows, stations), 1)
    station_id = lax.broadcasted_iota(jnp.int32, (stations, events), 0)
    first_weight = lax.axis_index("station") * stations
    copies[0].wait()
    network = channels * sum(weight_ref[station] for station in range(weight_ref.shape[0]))
    weight = jnp.zeros((stations, events), F32)
    for station in range(stations):
        weight = jnp.where(station_id == station, weight_ref[first_weight + station], weight)
    copies[1].wait()
    amplitude = mask_ref[...].astype(F32) * jnp.sqrt(weight / network)
    picked = lax.dot_general(
        at_event,
        amplitude,
        (((1,), (1,)), ((), ())),
        precision=lax.Precision.HIGHEST,
        preferred_element_type=F32,
    )
    factor = jnp.sum(jnp.where(at_station, picked, 0.0), axis=1, keepdims=True).reshape(3, twos, SUB, 1)
    results = []
    for piece, (first, count) in enumerate(spots):
        copies[2 + piece].wait()
        spot = slice(first, first + count)
        for group in range(3):
            for side in range(2):
                part = waves_ref[spot, group, side] if group < 2 else waves_ref[spot, side, 2]
                result_ref[group, spot, side * HALF : (side + 1) * HALF, :] = part
            traces = result_ref[group, spot]
            energy = jnp.sum(traces * traces, axis=-1, keepdims=True)
            result_ref[group, spot] = traces * (lax.rsqrt(energy + epsilon) * factor[group, spot])
        for number, target in enumerate((out_hbms[piece], all_hbm.at[:, pl.ds(first, count)])):
            sem = sems.at[2 + pieces + 2 * piece + number]
            results.append(pltpu.make_async_copy(result_ref.at[:, pl.ds(first, count)], target, sem))
            results[-1].start()
    for copy in results:
        copy.wait()


def prepare(waveforms, event_mask, station_weight):
    events, stations, channels, samples = waveforms.shape
    waves = jnp.transpose(waveforms, (0, 2, 1, 3)).reshape(events // 2, 2, channels, stations, samples)
    hbm = pl.BlockSpec(memory_space=pltpu.HBM)
    spots = piece_spots(events // 2)
    pieces = len(spots)
    shape = (3, events // 2, SUB, samples)
    return pl.pallas_call(
        prepare_kernel,
        out_shape=[jax.ShapeDtypeStruct(shape, F32)]
        + [jax.ShapeDtypeStruct((3, count, SUB, samples), F32) for _, count in spots],
        in_specs=[hbm] * 3,
        out_specs=[hbm] * (1 + pieces),
        scratch_shapes=[
            pltpu.VMEM(waves.shape, F32),
            pltpu.VMEM((stations, events), event_mask.dtype),
            pltpu.SMEM(station_weight.shape, F32),
            pltpu.VMEM(shape, F32),
            pltpu.SemaphoreType.DMA((2 + 3 * pieces,)),
        ],
        compiler_params=pltpu.CompilerParams(vmem_limit_bytes=PREPARE_VMEM_BYTES),
        name="prepare",
    )(waves, event_mask.T, station_weight)


def index_kernel(events, partners_ref, counts_ref, pairs_ref, index_ref, order_ref):
    rounds, _, _, all_pairs = pairs_ref.shape
    here = lax.axis_index("cluster")
    sibling = jnp.where(here % 2 == 0, here + 1, here - 1)
    own_count = counts_ref[here]
    partners = [partners_ref[turn, here] for turn in range(rounds)]
    parts = [jnp.where(partner == here, 0, jnp.where(partner == sibling, 1, 2)) for partner in partners]
    across = jnp.int32(0)
    lane = lax.broadcasted_iota(jnp.int32, (1, LANES), 1)
    order = jnp.zeros((1, LANES), jnp.int32)
    for turn in range(rounds):
        part = parts[turn]
        across += (part == 2).astype(jnp.int32)
        place = jnp.int32(0)
        for other in range(rounds):
            ahead = parts[other] <= part if other < turn else parts[other] < part
            place += ahead.astype(jnp.int32)
        order = jnp.where(lane == place, turn, order)
        first, second = pairs_ref[turn, 0, 0:1], pairs_ref[turn, 0, 1:2]
        valid = (first < own_count) & (second < counts_ref[partners[turn]])
        entries = (
            TILES * jnp.where(valid, first, events),
            TILES * (second + part * (events + 2)),
            jnp.full((1, all_pairs), part, jnp.int32),
        )
        for kind, entry in enumerate(entries):
            for row in range(all_pairs // LANES):
                spot = (ENTRIES * place + kind) * (all_pairs // LANES) + row
                index_ref[pl.ds(spot, 1)] = entry[:, row * LANES : (row + 1) * LANES]
    order_ref[...] = jnp.where(lane == rounds, across, order)


def pair_index(partners, counts, pair_list, events):
    rounds, _, all_pairs, _ = pair_list.shape
    vmem = pl.BlockSpec(memory_space=pltpu.VMEM)
    smem = pl.BlockSpec(memory_space=pltpu.SMEM)
    return pl.pallas_call(
        lambda *refs: index_kernel(events, *refs),
        out_shape=[
            jax.ShapeDtypeStruct((rounds * ENTRIES * all_pairs // LANES, LANES), jnp.int32),
            jax.ShapeDtypeStruct((1, LANES), jnp.int32),
        ],
        in_specs=[smem, smem, vmem],
        out_specs=[vmem, vmem],
        compiler_params=pltpu.CompilerParams(vmem_limit_bytes=VMEM_BYTES),
        name="pair_index",
    )(partners, counts, jnp.transpose(pair_list, (0, 1, 3, 2)))


def fill_spectra(traces_ref, part, first, table_ref, spectra_ref):
    _, twos, _, samples = traces_ref.shape
    spot = pl.ds(first, twos)
    spectrum = split_dot(traces_ref[...].reshape(3 * twos * SUB, samples), table_ref)
    tiles = [
        spectrum[:, block * LANES : (block + 1) * LANES].reshape(3, twos, SUB, LANES) for block in range(4)
    ]
    low_half = lax.broadcasted_iota(jnp.int32, (twos, SUB, LANES), 1) < HALF
    for group in range(3):
        for side in range(2):
            lower, upper = tiles[2 * side][group], tiles[2 * side + 1][group]
            first = jnp.where(low_half, lower, pltpu.roll(upper, HALF, 1))
            second = jnp.where(low_half, pltpu.roll(lower, HALF, 1), upper)
            if group < 2:
                spectra_ref[part, spot, group, 3 * side] = first
                spectra_ref[part, spot, group, 3 * side + 1] = second
            else:
                spectra_ref[part, spot, 0, 3 * side + 2] = first
                spectra_ref[part, spot, 1, 3 * side + 2] = second


def clear_last(spectra_ref):
    spectra_ref[0, spectra_ref.shape[1] - 1] = jnp.zeros(spectra_ref.shape[2:], F32)


def spectra_kernel(places, first, *refs):
    trace_refs, table_ref, spectra_ref = refs[: len(places)], refs[len(places)], refs[-1]
    for (part, pair), traces_ref in zip(places, trace_refs, strict=True):
        fill_spectra(traces_ref, part, pair, table_ref, spectra_ref)
    if first:
        clear_last(spectra_ref)


def add_pairs(index_ref, all_pairs, turns, wanted, blocks, spectra_ref, base_refs, out_refs):
    slots = 2 * spectra_ref.shape[1]
    length = lax.axis_size("station")
    station_here = lax.axis_index("station")
    swap = length == 4
    block_pairs = all_pairs // length
    flat_ref = spectra_ref.reshape(spectra_ref.shape[0] * slots * TILES, SUB, LANES)
    row_id = lax.broadcasted_iota(jnp.int32, (SUB, LANES), 0)
    in_four, in_two, in_one = row_id < 4, row_id % 4 < 2, row_id % 2 < 1

    def down(value, rows):
        return pltpu.roll(value, rows % SUB, 0)

    def fold_four(sums):
        even, odd = (
            jnp.where(in_two, one + down(one, -2), other + down(other, 2)) for one, other in (sums[0::2], sums[1::2])
        )
        return jnp.where(in_one, even + down(even, -1), odd + down(odd, 1))

    def fold_eight(sums):
        one, other = fold_four(sums[:4]), fold_four(sums[4:])
        return jnp.where(in_four, one, down(other, 4)), jnp.where(in_four, down(one, 4), other)

    def one_turn(place, turn):
        for number, block in enumerate(blocks):
            if swap:
                source = station_here if block == 0 else station_here + 1 - 2 * (station_here % 2)
                which, row = number, place * block_pairs
            else:
                source = station_here // len(blocks) * len(blocks) + block
                which, row = 0, (place * len(blocks) + block) * block_pairs
            start = source * block_pairs

            def eight_pairs(group, carry):
                real, imag = [], []
                first = start + group * SUB
                for spot in range(SUB):
                    entry = ENTRIES * turn * all_pairs + spot
                    left = flat_ref[pl.ds(index_ref[entry + first], TILES)]
                    right = flat_ref[pl.ds(index_ref[entry + all_pairs + first], TILES)]
                    reals, imags = [], []
                    for tile in range(3):
                        left_real, left_imag = left[tile], left[tile + 3]
                        right_real, right_imag = right[tile], right[tile + 3]
                        reals.append(left_real * right_real + left_imag * right_imag)
                        imags.append(left_imag * right_real - left_real * right_imag)
                    real.append(reals[0] + reals[1] + reals[2])
                    imag.append(imags[0] + imags[1] + imags[2])
                rows = pl.ds(pl.multiple_of(row + group * SUB, SUB), SUB)
                for column, total in enumerate((*fold_eight(real), *fold_eight(imag))):
                    spot = pl.ds(column * LANES, LANES)
                    if base_refs is not None:
                        total += base_refs[which][rows, spot]
                    out_refs[which][rows, spot] = total
                return carry

            lax.fori_loop(0, block_pairs // SUB, eight_pairs, 0, unroll=min(UNROLL, block_pairs // SUB))

    for place, turn in enumerate(turns):
        pl.when(wanted(index_ref[(ENTRIES * turn + 2) * all_pairs]))(lambda: one_turn(place, turn))


def half_turns(rounds, half):
    return range(half * rounds // 2, (half + 1) * rounds // 2)


def index_copy(index_hbm, index_ref, sem):
    copy = pltpu.make_async_copy(index_hbm, index_ref, sem)
    copy.start()
    return copy


def first_near_kernel(blocks, rounds, all_pairs, index_hbm, own_ref, sibling_ref, table_ref, spectra_ref, *refs):
    *out_refs, index_ref, sem = refs
    copy = index_copy(index_hbm, index_ref, sem)
    fill_spectra(own_ref, 0, 0, table_ref, spectra_ref)
    fill_spectra(sibling_ref, 1, 0, table_ref, spectra_ref)
    clear_last(spectra_ref)
    copy.wait()
    for out_ref in out_refs:
        out_ref[...] = jnp.zeros(out_ref.shape, F32)
    for half in range(2):
        turns = half_turns(rounds, half)
        some = out_refs[half * len(out_refs) // 2 : (half + 1) * len(out_refs) // 2]
        add_pairs(index_ref, all_pairs, turns, lambda part: part < 2, blocks, spectra_ref, None, some)


def more_kernel(all_pairs, places, jobs, with_inverse, has_base, *refs):
    count = len(places)
    index_hbm, trace_refs, refs = refs[0], refs[1 : 1 + count], refs[1 + count :]
    if count:
        table_ref, refs = refs[0], refs[1:]
    if with_inverse:
        inverse_ref, refs = refs[0], refs[1:]
    *refs, index_ref, sem = refs
    arrays = len(refs) // 2 - 1 if has_base else len(refs) - 2
    base_refs = refs[1 : 1 + arrays] if has_base else None
    spectra_ref, *out_refs = refs[-1 - arrays :]
    copy = index_copy(index_hbm, index_ref, sem)
    for (part, pair), traces_ref in zip(places, trace_refs, strict=True):
        fill_spectra(traces_ref, part, pair, table_ref, spectra_ref)
    if not has_base:
        for out_ref in out_refs:
            out_ref[...] = jnp.zeros(out_ref.shape, F32)
    copy.wait()
    for turns, parts, blocks, first, last in jobs:

        def wanted(part, parts=parts):
            return (part >= parts[0]) & (part <= parts[-1])

        base = base_refs[first:last] if has_base else None
        add_pairs(index_ref, all_pairs, turns, wanted, blocks, spectra_ref, base, out_refs[first:last])
    if with_inverse:
        out_refs[-1][...] = split_dot(out_refs[-1][...], inverse_ref)


def call_kernel(kernel, name, operands, specs, updated, out_shapes, scratch, flops):
    vmem = pl.BlockSpec(memory_space=pltpu.VMEM)
    operands = [*operands, *updated]
    shapes = [*(jax.ShapeDtypeStruct(value.shape, value.dtype) for value in updated), *out_shapes]
    first_in = len(operands) - len(updated)
    in_specs = [vmem] * len(operands)
    out_specs = [vmem] * len(shapes)
    for place, spec in specs.items():
        in_specs[place] = spec
        if place >= first_in:
            out_specs[place - first_in] = spec
    return pl.pallas_call(
        kernel,
        out_shape=shapes,
        in_specs=in_specs,
        out_specs=out_specs,
        scratch_shapes=scratch,
        input_output_aliases={first_in + i: i for i in range(len(updated))},
        compiler_params=pltpu.CompilerParams(vmem_limit_bytes=VMEM_BYTES),
        cost_estimate=pl.CostEstimate(flops=flops, bytes_accessed=flops // 1000, transcendentals=0),
        name=name,
    )(*operands)


def finish_kernel(turns, invert, terms, order_ref, table_ref, *refs):
    term_refs, (out_hbm, result_ref, sems) = refs[:terms], refs[-3:]
    rows = result_ref.shape[0] // len(turns)
    lane = lax.broadcasted_iota(jnp.int32, (1, LANES), 1)
    order = order_ref[...].astype(F32)
    targets = [jnp.sum(jnp.where(lane == turn, order, 0.0)).astype(jnp.int32) for turn in turns]
    total = sum(ref[...] for ref in term_refs)
    result_ref[...] = split_dot(total, table_ref) if invert else total
    copies = [
        pltpu.make_async_copy(
            result_ref.at[pl.ds(number * rows, rows)],
            out_hbm.at[pl.ds(pl.multiple_of(target * rows, SUB), rows)],
            sems.at[number],
        )
        for number, target in enumerate(targets)
    ]
    for copy in copies:
        copy.start()
    for copy in copies:
        copy.wait()


def finish(order, terms, table, turns, invert, result):
    rows, lags = terms[0].shape
    vmem = pl.BlockSpec(memory_space=pltpu.VMEM)
    hbm = pl.BlockSpec(memory_space=pltpu.HBM)
    operands = [order, table, *terms] + ([] if result is None else [result])
    return pl.pallas_call(
        lambda *refs: finish_kernel(turns, invert, len(terms), *refs),
        out_shape=jax.ShapeDtypeStruct((2 * rows, lags), F32),
        in_specs=[vmem] * (2 + len(terms)) + ([] if result is None else [hbm]),
        out_specs=hbm,
        scratch_shapes=[
            pltpu.VMEM((rows, lags), F32),
            pltpu.SemaphoreType.DMA((len(turns),)),
        ],
        input_output_aliases={} if result is None else {2 + len(terms): 0},
        compiler_params=pltpu.CompilerParams(vmem_limit_bytes=VMEM_BYTES),
        cost_estimate=pl.CostEstimate(flops=1, bytes_accessed=1, transcendentals=0),
        name="finish",
    )(*operands)


def on_device(waveforms, event_mask, station_weight, partners, pair_list, counts):
    events, stations, channels, samples = waveforms.shape
    rounds, _, all_pairs, _ = pair_list.shape
    clusters = lax.axis_size("cluster")
    length = lax.axis_size("station")
    assert (stations, channels, samples) == (HALF, 3, 2 * LANES)
    assert events % 4 == 0 and rounds % 2 == 0 and clusters % 2 == 0 and length % 4 == 0
    forward = jnp.asarray(forward_table(samples))
    inverse = jnp.asarray(inverse_table(samples))

    def to_sibling(value):
        return lax.ppermute(value, "cluster", [(i, i ^ 1) for i in range(clusters)])

    def to_across(value):
        return lax.ppermute(value, "cluster", [(i, (i + 1 if i % 2 else i - 1) % clusters) for i in range(clusters)])

    def to_mirror(value):
        return lax.ppermute(value, "station", [(i, length - 1 - i) for i in range(length)])

    def swap_stations(value):
        return lax.ppermute(value, "station", [(i, i ^ 1) for i in range(length)])

    def spread(value):
        groups = np.arange(length).reshape(2, length // 2).tolist()
        value = value.reshape(rounds // 2, all_pairs // 2, 2 * samples)
        kept = lax.psum_scatter(value, "station", scatter_dimension=1, axis_index_groups=groups, tiled=True)
        return [kept.reshape(-1, 2 * samples)]

    def invert(cross, table):
        return call_kernel(invert_kernel, "invert", [cross, table], {}, [], [half_shape], [], 1)[0]

    swap = length == 4
    blocks = list(range(length // 2))
    outs = 2 if swap else 1
    half_shape = jax.ShapeDtypeStruct((rounds * all_pairs // 4 // outs, 2 * samples), F32)
    spectra_shape = jax.ShapeDtypeStruct((3, events // 2 + 1, 2, TILES, SUB, LANES), F32)
    scratch = [
        pltpu.SMEM((rounds * ENTRIES * all_pairs,), jnp.int32),
        pltpu.SemaphoreType.DMA,
    ]

    anywhere = {0: pl.BlockSpec(memory_space=pl.ANY)}

    def add_spectra(traces, places, spectra, flops):
        return call_kernel(
            lambda *refs: spectra_kernel(places, not spectra, *refs),
            "add_spectra",
            [*traces, forward],
            {},
            spectra,
            [] if spectra else [spectra_shape],
            [],
            flops,
        )

    early_turns, late_turns = half_turns(rounds, 0), half_turns(rounds, 1)

    def more_sums(name, traces, places, jobs, spectra, base, with_inverse=False):
        tables = [forward] * bool(traces) + [inverse] * with_inverse
        return call_kernel(
            lambda *refs: more_kernel(all_pairs, places, jobs, with_inverse, bool(base), *refs),
            name,
            [index, *traces, *tables],
            anywhere,
            [spectra, *base],
            [] if base else [half_shape] * outs,
            scratch,
            1,
        )

    own, *pieces = prepare(waveforms, event_mask, station_weight)
    index, order = pair_index(partners, counts, pair_list, events)
    index = index.reshape(-1)
    mirror_first, mirror_last = (to_mirror(piece) for piece in pieces)
    across = [to_across(piece) for piece in pieces]
    sibling = to_sibling(own)
    spectra, *partial = call_kernel(
        lambda *refs: first_near_kernel(blocks, rounds, all_pairs, *refs),
        "first_near",
        [index, own, sibling, forward],
        anywhere,
        [],
        [spectra_shape] + [half_shape] * (2 * outs),
        scratch,
        1,
    )
    mirror_first, *partial = lax.optimization_barrier((mirror_first, *partial))
    far_first, near_first = to_across(mirror_first), to_sibling(mirror_first)
    (other,) = add_spectra([mirror_first], [(0, 0)], [], 1)
    early, late = partial[:outs], partial[outs:]
    later = mirror_first.shape[1]
    other, spectra = lax.optimization_barrier((other, spectra))
    (spectra,) = add_spectra(across, [(2, 0), (2, later)], [spectra], 1)
    mirror_last, other, spectra = lax.optimization_barrier((mirror_last, other, spectra))
    far_last, near_last = to_across(mirror_last), to_sibling(mirror_last)
    sent = blocks[1:] if swap else blocks
    *early_kept, early_sent = early

    def add_sent(name, traces, places, turns, parts, spectra, value, **options):
        return more_sums(name, traces, places, [(turns, parts, sent, 0, 1)], spectra, [value], **options)

    traces, places = [mirror_last, near_first, near_last], [(0, later), (1, 0), (1, later)]
    other, early_sent = add_sent("near_sums", traces, places, early_turns, (0, 1), other, early_sent)
    early_sent, spectra, *late = lax.optimization_barrier((early_sent, spectra, *late))
    jobs = [(late_turns, (2,), blocks, 0, outs)]
    spectra, *late = more_sums("across_sums", [], [], jobs, spectra, late)
    *late_kept, late_sent = late
    other, late_sent = add_sent("near_sums", [far_first], [(2, 0)], late_turns, (0, 1), other, late_sent)
    traces, places = [far_last], [(2, later)]
    if swap:
        early_received = swap_stations(early_sent)
        other, late_sent = add_sent(
            "across_sums", traces, places, late_turns, (2,), other, late_sent, with_inverse=True
        )
        late_received = swap_stations(late_sent)
        jobs = [(early_turns, (0, 1), blocks[:1], 0, 1), (late_turns, (0, 1, 2), blocks[:1], 1, 2)]
        kept = early_kept + late_kept
        other, early_kept, late_kept = more_sums("kept_sums", [], [], jobs, other, kept, with_inverse=True)

        def with_across(spectra, other, kept):
            jobs = [(early_turns, (2,), blocks, 0, 2)]
            _, *more = more_sums("across_sums", [], [], jobs, spectra, [])
            _, more_kept, more_sent = more_sums("across_sums", [], [], jobs, other, more)
            return kept + more_kept + swap_stations(more_sent)

        many = order[0, rounds] > len(late_turns)
        early_kept = lax.cond(many, with_across, lambda _, __, kept: kept, spectra, other, early_kept)
        early, late = [early_kept, early_received], [late_kept, late_received]
    else:
        other, late_sent = add_sent("across_sums", traces, places, late_turns, (2,), other, late_sent)
        spectra, early_sent = add_sent("across_sums", [], [], early_turns, (2,), spectra, early_sent)
        other, early_sent = add_sent("across_sums", [], [], early_turns, (2,), other, early_sent)
        early, late = spread(early_sent), spread(late_sent)
    result = finish(order, early, inverse, early_turns, True, None)
    result = finish(order, late, inverse, late_turns, not swap, result)
    return result.reshape(rounds, 1, all_pairs // length, 2 * samples)


def solution(mesh):
    return jax.shard_map(
        on_device,
        mesh=mesh,
        in_specs=(
            P(("groups", "cluster"), "station", None, None),
            P(("groups", "cluster"), "station"),
            P("groups"),
            P(None, "groups"),
            P(None, ("groups", "cluster"), None, None),
            P("groups"),
        ),
        out_specs=P(None, ("groups", "cluster"), "station", None),
        check_vma=False,
    )
```

```python
import math

import jax
import jax.numpy as jnp
import ml_dtypes
import numpy as np
from jax import lax
from jax.experimental import pallas as pl
from jax.experimental.pallas import tpu as pltpu
from jax.sharding import PartitionSpec as P

epsilon = 1e-06
SUB, LANES = 8, 128
HALF = SUB // 2
TILES = 6
ENTRIES = 3
UNROLL = 4
FIRST_SHARE = 9
VMEM_BYTES = 16 * 1024 * 1024
PREPARE_VMEM_BYTES = 62 * 1024 * 1024
F32 = jnp.float32
BF16 = jnp.bfloat16


def split_table(table):
    high = table.astype(ml_dtypes.bfloat16)
    low = (table - high.astype(np.float64)).astype(ml_dtypes.bfloat16)
    return np.stack([high, low])


def forward_table(samples):
    steps = np.arange(samples)
    angles = (steps[:, None] * steps[None, :] % (2 * samples)) * (math.pi / samples)
    return split_table(np.concatenate([np.cos(angles), -np.sin(angles)], axis=1))


def inverse_table(samples):
    record = 2 * samples
    bins = np.arange(samples)
    lags = (np.arange(record) + samples) % record
    angles = (bins[:, None] * lags[None, :] % record) * (math.pi / samples)
    gain = np.where(bins == 0, 1.0, 2.0)[:, None] / record
    return split_table(np.concatenate([gain * np.cos(angles), -gain * np.sin(angles)], axis=0))


def split_dot(value, table_ref):
    rows = value.shape[0]
    high = value.astype(BF16)
    low = (value - high.astype(F32)).astype(BF16)
    both = jnp.dot(jnp.concatenate([high, low], axis=0), table_ref[0], preferred_element_type=F32)
    return both[:rows] + (both[rows:] + jnp.dot(high, table_ref[1], preferred_element_type=F32))


def piece_spots(twos):
    count = twos * FIRST_SHARE // 16
    return [(0, count), (count, twos - count)]


def prepare_kernel(waves_hbm, mask_hbm, weight_hbm, *refs):
    all_hbm, *out_hbms, waves_ref, mask_ref, weight_ref, result_ref, sems = refs
    pieces = len(out_hbms)
    twos, _, channels, stations, _ = waves_ref.shape
    spots = piece_spots(twos)
    copies = [
        pltpu.make_async_copy(weight_hbm, weight_ref, sems.at[0]),
        pltpu.make_async_copy(mask_hbm, mask_ref, sems.at[1]),
    ]
    for piece, (first, count) in enumerate(spots):
        spot = pl.ds(first, count)
        copies.append(pltpu.make_async_copy(waves_hbm.at[spot], waves_ref.at[spot], sems.at[2 + piece]))
    for copy in copies:
        copy.start()
    events = 2 * twos
    rows = 3 * SUB * twos
    row = lax.broadcasted_iota(jnp.int32, (rows, events), 0)
    group, row_here = row // (SUB * twos), row % (SUB * twos)
    event_of_row = jnp.where(group < 2, 2 * (row_here // SUB) + group, row_here // HALF)
    at_event = (event_of_row == lax.broadcasted_iota(jnp.int32, (rows, events), 1)).astype(F32)
    row = lax.broadcasted_iota(jnp.int32, (rows, stations), 0)
    at_station = row % HALF == lax.broadcasted_iota(jnp.int32, (rows, stations), 1)
    station_id = lax.broadcasted_iota(jnp.int32, (stations, events), 0)
    first_weight = lax.axis_index("station") * stations
    copies[0].wait()
    network = channels * sum(weight_ref[station] for station in range(weight_ref.shape[0]))
    weight = jnp.zeros((stations, events), F32)
    for station in range(stations):
        weight = jnp.where(station_id == station, weight_ref[first_weight + station], weight)
    copies[1].wait()
    amplitude = mask_ref[...].astype(F32) * jnp.sqrt(weight / network)
    picked = lax.dot_general(
        at_event,
        amplitude,
        (((1,), (1,)), ((), ())),
        precision=lax.Precision.HIGHEST,
        preferred_element_type=F32,
    )
    factor = jnp.sum(jnp.where(at_station, picked, 0.0), axis=1, keepdims=True).reshape(3, twos, SUB, 1)
    results = []
    for piece, (first, count) in enumerate(spots):
        copies[2 + piece].wait()
        spot = slice(first, first + count)
        for group in range(3):
            for side in range(2):
                part = waves_ref[spot, group, side] if group < 2 else waves_ref[spot, side, 2]
                result_ref[group, spot, side * HALF : (side + 1) * HALF, :] = part
            traces = result_ref[group, spot]
            energy = jnp.sum(traces * traces, axis=-1, keepdims=True)
            result_ref[group, spot] = traces * (lax.rsqrt(energy + epsilon) * factor[group, spot])
        for number, target in enumerate((out_hbms[piece], all_hbm.at[:, pl.ds(first, count)])):
            sem = sems.at[2 + pieces + 2 * piece + number]
            results.append(pltpu.make_async_copy(result_ref.at[:, pl.ds(first, count)], target, sem))
            results[-1].start()
    for copy in results:
        copy.wait()


def prepare(waveforms, event_mask, station_weight):
    events, stations, channels, samples = waveforms.shape
    waves = jnp.transpose(waveforms, (0, 2, 1, 3)).reshape(events // 2, 2, channels, stations, samples)
    hbm = pl.BlockSpec(memory_space=pltpu.HBM)
    spots = piece_spots(events // 2)
    pieces = len(spots)
    shape = (3, events // 2, SUB, samples)
    return pl.pallas_call(
        prepare_kernel,
        out_shape=[jax.ShapeDtypeStruct(shape, F32)]
        + [jax.ShapeDtypeStruct((3, count, SUB, samples), F32) for _, count in spots],
        in_specs=[hbm] * 3,
        out_specs=[hbm] * (1 + pieces),
        scratch_shapes=[
            pltpu.VMEM(waves.shape, F32),
            pltpu.VMEM((stations, events), event_mask.dtype),
            pltpu.SMEM(station_weight.shape, F32),
            pltpu.VMEM(shape, F32),
            pltpu.SemaphoreType.DMA((2 + 3 * pieces,)),
        ],
        compiler_params=pltpu.CompilerParams(vmem_limit_bytes=PREPARE_VMEM_BYTES),
        name="prepare",
    )(waves, event_mask.T, station_weight)


def index_kernel(events, partners_ref, counts_ref, pairs_ref, index_ref, order_ref):
    rounds, _, _, all_pairs = pairs_ref.shape
    here = lax.axis_index("cluster")
    sibling = jnp.where(here % 2 == 0, here + 1, here - 1)
    own_count = counts_ref[here]
    partners = [partners_ref[turn, here] for turn in range(rounds)]
    parts = [jnp.where(partner == here, 0, jnp.where(partner == sibling, 1, 2)) for partner in partners]
    across = jnp.int32(0)
    lane = lax.broadcasted_iota(jnp.int32, (1, LANES), 1)
    order = jnp.zeros((1, LANES), jnp.int32)
    for turn in range(rounds):
        part = parts[turn]
        across += (part == 2).astype(jnp.int32)
        place = jnp.int32(0)
        for other in range(rounds):
            ahead = parts[other] <= part if other < turn else parts[other] < part
            place += ahead.astype(jnp.int32)
        order = jnp.where(lane == place, turn, order)
        first, second = pairs_ref[turn, 0, 0:1], pairs_ref[turn, 0, 1:2]
        valid = (first < own_count) & (second < counts_ref[partners[turn]])
        entries = (
            TILES * jnp.where(valid, first, events),
            TILES * (second + part * (events + 2)),
            jnp.full((1, all_pairs), part, jnp.int32),
        )
        for kind, entry in enumerate(entries):
            for row in range(all_pairs // LANES):
                spot = (ENTRIES * place + kind) * (all_pairs // LANES) + row
                index_ref[pl.ds(spot, 1)] = entry[:, row * LANES : (row + 1) * LANES]
    order_ref[...] = jnp.where(lane == rounds, across, order)


def pair_index(partners, counts, pair_list, events):
    rounds, _, all_pairs, _ = pair_list.shape
    vmem = pl.BlockSpec(memory_space=pltpu.VMEM)
    smem = pl.BlockSpec(memory_space=pltpu.SMEM)
    return pl.pallas_call(
        lambda *refs: index_kernel(events, *refs),
        out_shape=[
            jax.ShapeDtypeStruct((rounds * ENTRIES * all_pairs // LANES, LANES), jnp.int32),
            jax.ShapeDtypeStruct((1, LANES), jnp.int32),
        ],
        in_specs=[smem, smem, vmem],
        out_specs=[vmem, vmem],
        compiler_params=pltpu.CompilerParams(vmem_limit_bytes=VMEM_BYTES),
        name="pair_index",
    )(partners, counts, jnp.transpose(pair_list, (0, 1, 3, 2)))


def fill_spectra(traces_ref, part, first, table_ref, spectra_ref):
    _, twos, _, samples = traces_ref.shape
    spot = pl.ds(first, twos)
    spectrum = split_dot(traces_ref[...].reshape(3 * twos * SUB, samples), table_ref)
    tiles = [
        spectrum[:, block * LANES : (block + 1) * LANES].reshape(3, twos, SUB, LANES) for block in range(4)
    ]
    low_half = lax.broadcasted_iota(jnp.int32, (twos, SUB, LANES), 1) < HALF
    for group in range(3):
        for side in range(2):
            lower, upper = tiles[2 * side][group], tiles[2 * side + 1][group]
            first = jnp.where(low_half, lower, pltpu.roll(upper, HALF, 1))
            second = jnp.where(low_half, pltpu.roll(lower, HALF, 1), upper)
            if group < 2:
                spectra_ref[part, spot, group, 3 * side] = first
                spectra_ref[part, spot, group, 3 * side + 1] = second
            else:
                spectra_ref[part, spot, 0, 3 * side + 2] = first
                spectra_ref[part, spot, 1, 3 * side + 2] = second


def clear_last(spectra_ref):
    spectra_ref[0, spectra_ref.shape[1] - 1] = jnp.zeros(spectra_ref.shape[2:], F32)


def spectra_kernel(places, first, *refs):
    trace_refs, table_ref, spectra_ref = refs[: len(places)], refs[len(places)], refs[-1]
    for (part, pair), traces_ref in zip(places, trace_refs, strict=True):
        fill_spectra(traces_ref, part, pair, table_ref, spectra_ref)
    if first:
        clear_last(spectra_ref)


def add_pairs(index_ref, all_pairs, turns, wanted, blocks, spectra_ref, base_refs, out_refs):
    slots = 2 * spectra_ref.shape[1]
    length = lax.axis_size("station")
    station_here = lax.axis_index("station")
    swap = length == 4
    block_pairs = all_pairs // length
    flat_ref = spectra_ref.reshape(spectra_ref.shape[0] * slots * TILES, SUB, LANES)
    row_id = lax.broadcasted_iota(jnp.int32, (SUB, LANES), 0)
    in_four, in_two, in_one = row_id < 4, row_id % 4 < 2, row_id % 2 < 1

    def down(value, rows):
        return pltpu.roll(value, rows % SUB, 0)

    def fold_four(sums):
        even, odd = (
            jnp.where(in_two, one + down(one, -2), other + down(other, 2)) for one, other in (sums[0::2], sums[1::2])
        )
        return jnp.where(in_one, even + down(even, -1), odd + down(odd, 1))

    def fold_eight(sums):
        one, other = fold_four(sums[:4]), fold_four(sums[4:])
        return jnp.where(in_four, one, down(other, 4)), jnp.where(in_four, down(one, 4), other)

    def one_turn(place, turn):
        for number, block in enumerate(blocks):
            if swap:
                source = station_here if block == 0 else station_here + 1 - 2 * (station_here % 2)
                which, row = number, place * block_pairs
            else:
                source = station_here // len(blocks) * len(blocks) + block
                which, row = 0, (place * len(blocks) + block) * block_pairs
            start = source * block_pairs

            def eight_pairs(group, carry):
                real, imag = [], []
                first = start + group * SUB
                for spot in range(SUB):
                    entry = ENTRIES * turn * all_pairs + spot
                    left = flat_ref[pl.ds(index_ref[entry + first], TILES)]
                    right = flat_ref[pl.ds(index_ref[entry + all_pairs + first], TILES)]
                    reals, imags = [], []
                    for tile in range(3):
                        left_real, left_imag = left[tile], left[tile + 3]
                        right_real, right_imag = right[tile], right[tile + 3]
                        reals.append(left_real * right_real + left_imag * right_imag)
                        imags.append(left_imag * right_real - left_real * right_imag)
                    real.append(reals[0] + reals[1] + reals[2])
                    imag.append(imags[0] + imags[1] + imags[2])
                rows = pl.ds(pl.multiple_of(row + group * SUB, SUB), SUB)
                for column, total in enumerate((*fold_eight(real), *fold_eight(imag))):
                    spot = pl.ds(column * LANES, LANES)
                    if base_refs is not None:
                        total += base_refs[which][rows, spot]
                    out_refs[which][rows, spot] = total
                return carry

            lax.fori_loop(0, block_pairs // SUB, eight_pairs, 0, unroll=min(UNROLL, block_pairs // SUB))

    for place, turn in enumerate(turns):
        pl.when(wanted(index_ref[(ENTRIES * turn + 2) * all_pairs]))(lambda: one_turn(place, turn))


def half_turns(rounds, half):
    return range(half * rounds // 2, (half + 1) * rounds // 2)


def index_copy(index_hbm, index_ref, sem):
    copy = pltpu.make_async_copy(index_hbm, index_ref, sem)
    copy.start()
    return copy


def first_near_kernel(blocks, rounds, all_pairs, index_hbm, own_ref, sibling_ref, table_ref, spectra_ref, *refs):
    *out_refs, index_ref, sem = refs
    copy = index_copy(index_hbm, index_ref, sem)
    fill_spectra(own_ref, 0, 0, table_ref, spectra_ref)
    fill_spectra(sibling_ref, 1, 0, table_ref, spectra_ref)
    clear_last(spectra_ref)
    copy.wait()
    for out_ref in out_refs:
        out_ref[...] = jnp.zeros(out_ref.shape, F32)
    for half in range(2):
        turns = half_turns(rounds, half)
        some = out_refs[half * len(out_refs) // 2 : (half + 1) * len(out_refs) // 2]
        add_pairs(index_ref, all_pairs, turns, lambda part: part < 2, blocks, spectra_ref, None, some)


def more_kernel(all_pairs, places, jobs, with_inverse, has_base, *refs):
    count = len(places)
    index_hbm, trace_refs, refs = refs[0], refs[1 : 1 + count], refs[1 + count :]
    if count:
        table_ref, refs = refs[0], refs[1:]
    if with_inverse:
        inverse_ref, refs = refs[0], refs[1:]
    *refs, index_ref, sem = refs
    arrays = len(refs) // 2 - 1 if has_base else len(refs) - 2
    base_refs = refs[1 : 1 + arrays] if has_base else None
    spectra_ref, *out_refs = refs[-1 - arrays :]
    copy = index_copy(index_hbm, index_ref, sem)
    for (part, pair), traces_ref in zip(places, trace_refs, strict=True):
        fill_spectra(traces_ref, part, pair, table_ref, spectra_ref)
    if not has_base:
        for out_ref in out_refs:
            out_ref[...] = jnp.zeros(out_ref.shape, F32)
    copy.wait()
    for turns, parts, blocks, first, last in jobs:

        def wanted(part, parts=parts):
            return (part >= parts[0]) & (part <= parts[-1])

        base = base_refs[first:last] if has_base else None
        add_pairs(index_ref, all_pairs, turns, wanted, blocks, spectra_ref, base, out_refs[first:last])
    if with_inverse:
        out_refs[-1][...] = split_dot(out_refs[-1][...], inverse_ref)


def call_kernel(kernel, name, operands, specs, updated, out_shapes, scratch, flops):
    vmem = pl.BlockSpec(memory_space=pltpu.VMEM)
    operands = [*operands, *updated]
    shapes = [*(jax.ShapeDtypeStruct(value.shape, value.dtype) for value in updated), *out_shapes]
    first_in = len(operands) - len(updated)
    in_specs = [vmem] * len(operands)
    out_specs = [vmem] * len(shapes)
    for place, spec in specs.items():
        in_specs[place] = spec
        if place >= first_in:
            out_specs[place - first_in] = spec
    return pl.pallas_call(
        kernel,
        out_shape=shapes,
        in_specs=in_specs,
        out_specs=out_specs,
        scratch_shapes=scratch,
        input_output_aliases={first_in + i: i for i in range(len(updated))},
        compiler_params=pltpu.CompilerParams(vmem_limit_bytes=VMEM_BYTES),
        cost_estimate=pl.CostEstimate(flops=flops, bytes_accessed=flops // 1000, transcendentals=0),
        name=name,
    )(*operands)


def finish_kernel(turns, invert, terms, order_ref, table_ref, *refs):
    term_refs, (out_hbm, result_ref, sems) = refs[:terms], refs[-3:]
    rows = result_ref.shape[0] // len(turns)
    lane = lax.broadcasted_iota(jnp.int32, (1, LANES), 1)
    order = order_ref[...].astype(F32)
    targets = [jnp.sum(jnp.where(lane == turn, order, 0.0)).astype(jnp.int32) for turn in turns]
    total = sum(ref[...] for ref in term_refs)
    result_ref[...] = split_dot(total, table_ref) if invert else total
    copies = [
        pltpu.make_async_copy(
            result_ref.at[pl.ds(number * rows, rows)],
            out_hbm.at[pl.ds(pl.multiple_of(target * rows, SUB), rows)],
            sems.at[number],
        )
        for number, target in enumerate(targets)
    ]
    for copy in copies:
        copy.start()
    for copy in copies:
        copy.wait()


def finish(order, terms, table, turns, invert, result):
    rows, lags = terms[0].shape
    vmem = pl.BlockSpec(memory_space=pltpu.VMEM)
    hbm = pl.BlockSpec(memory_space=pltpu.HBM)
    operands = [order, table, *terms] + ([] if result is None else [result])
    return pl.pallas_call(
        lambda *refs: finish_kernel(turns, invert, len(terms), *refs),
        out_shape=jax.ShapeDtypeStruct((2 * rows, lags), F32),
        in_specs=[vmem] * (2 + len(terms)) + ([] if result is None else [hbm]),
        out_specs=hbm,
        scratch_shapes=[
            pltpu.VMEM((rows, lags), F32),
            pltpu.SemaphoreType.DMA((len(turns),)),
        ],
        input_output_aliases={} if result is None else {2 + len(terms): 0},
        compiler_params=pltpu.CompilerParams(vmem_limit_bytes=VMEM_BYTES),
        cost_estimate=pl.CostEstimate(flops=1, bytes_accessed=1, transcendentals=0),
        name="finish",
    )(*operands)


def on_device(waveforms, event_mask, station_weight, partners, pair_list, counts):
    events, stations, channels, samples = waveforms.shape
    rounds, _, all_pairs, _ = pair_list.shape
    clusters = lax.axis_size("cluster")
    length = lax.axis_size("station")
    assert (stations, channels, samples) == (HALF, 3, 2 * LANES)
    assert events % 4 == 0 and rounds % 2 == 0 and clusters % 2 == 0 and length % 4 == 0
    forward = jnp.asarray(forward_table(samples))
    inverse = jnp.asarray(inverse_table(samples))

    def to_sibling(value):
        return lax.ppermute(value, "cluster", [(i, i ^ 1) for i in range(clusters)])

    def to_across(value):
        return lax.ppermute(value, "cluster", [(i, (i + 1 if i % 2 else i - 1) % clusters) for i in range(clusters)])

    def to_mirror(value):
        return lax.ppermute(value, "station", [(i, length - 1 - i) for i in range(length)])

    def swap_stations(value):
        return lax.ppermute(value, "station", [(i, i ^ 1) for i in range(length)])

    def spread(value):
        groups = np.arange(length).reshape(2, length // 2).tolist()
        value = value.reshape(rounds // 2, all_pairs // 2, 2 * samples)
        kept = lax.psum_scatter(value, "station", scatter_dimension=1, axis_index_groups=groups, tiled=True)
        return [kept.reshape(-1, 2 * samples)]

    def invert(cross, table):
        return call_kernel(invert_kernel, "invert", [cross, table], {}, [], [half_shape], [], 1)[0]

    swap = length == 4
    blocks = list(range(length // 2))
    outs = 2 if swap else 1
    half_shape = jax.ShapeDtypeStruct((rounds * all_pairs // 4 // outs, 2 * samples), F32)
    spectra_shape = jax.ShapeDtypeStruct((3, events // 2 + 1, 2, TILES, SUB, LANES), F32)
    scratch = [
        pltpu.SMEM((rounds * ENTRIES * all_pairs,), jnp.int32),
        pltpu.SemaphoreType.DMA,
    ]

    anywhere = {0: pl.BlockSpec(memory_space=pl.ANY)}

    def add_spectra(traces, places, spectra, flops):
        return call_kernel(
            lambda *refs: spectra_kernel(places, not spectra, *refs),
            "add_spectra",
            [*traces, forward],
            {},
            spectra,
            [] if spectra else [spectra_shape],
            [],
            flops,
        )

    early_turns, late_turns = half_turns(rounds, 0), half_turns(rounds, 1)

    def more_sums(name, traces, places, jobs, spectra, base, with_inverse=False):
        tables = [forward] * bool(traces) + [inverse] * with_inverse
        return call_kernel(
            lambda *refs: more_kernel(all_pairs, places, jobs, with_inverse, bool(base), *refs),
            name,
            [index, *traces, *tables],
            anywhere,
            [spectra, *base],
            [] if base else [half_shape] * outs,
            scratch,
            1,
        )

    own, *pieces = prepare(waveforms, event_mask, station_weight)
    index, order = pair_index(partners, counts, pair_list, events)
    index = index.reshape(-1)
    mirror_first, mirror_last = (to_mirror(piece) for piece in pieces)
    across = [to_across(piece) for piece in pieces]
    sibling = to_sibling(own)
    spectra, *partial = call_kernel(
        lambda *refs: first_near_kernel(blocks, rounds, all_pairs, *refs),
        "first_near",
        [index, own, sibling, forward],
        anywhere,
        [],
        [spectra_shape] + [half_shape] * (2 * outs),
        scratch,
        1,
    )
    mirror_first, *partial = lax.optimization_barrier((mirror_first, *partial))
    far_first, near_first = to_across(mirror_first), to_sibling(mirror_first)
    (other,) = add_spectra([mirror_first], [(0, 0)], [], 1)
    early, late = partial[:outs], partial[outs:]
    later = mirror_first.shape[1]
    other, spectra = lax.optimization_barrier((other, spectra))
    (spectra,) = add_spectra(across, [(2, 0), (2, later)], [spectra], 1)
    mirror_last, other, spectra = lax.optimization_barrier((mirror_last, other, spectra))
    far_last, near_last = to_across(mirror_last), to_sibling(mirror_last)
    sent = blocks[1:] if swap else blocks
    *early_kept, early_sent = early

    def add_sent(name, traces, places, turns, parts, spectra, value, **options):
        return more_sums(name, traces, places, [(turns, parts, sent, 0, 1)], spectra, [value], **options)

    traces, places = [mirror_last, near_first, near_last], [(0, later), (1, 0), (1, later)]
    other, early_sent = add_sent("near_sums", traces, places, early_turns, (0, 1), other, early_sent)
    early_sent, spectra, *late = lax.optimization_barrier((early_sent, spectra, *late))
    jobs = [(late_turns, (2,), blocks, 0, outs)]
    spectra, *late = more_sums("across_sums", [], [], jobs, spectra, late)
    *late_kept, late_sent = late
    other, late_sent = add_sent("near_sums", [far_first], [(2, 0)], late_turns, (0, 1), other, late_sent)
    traces, places = [far_last], [(2, later)]
    if swap:
        early_received = swap_stations(early_sent)
        other, late_sent = add_sent(
            "across_sums", traces, places, late_turns, (2,), other, late_sent, with_inverse=True
        )
        late_received = swap_stations(late_sent)
        jobs = [(early_turns, (0, 1), blocks[:1], 0, 1), (late_turns, (0, 1, 2), blocks[:1], 1, 2)]
        kept = early_kept + late_kept
        other, early_kept, late_kept = more_sums("kept_sums", [], [], jobs, other, kept, with_inverse=True)

        def with_across(count):
            def add(spectra, other, kept):
                jobs = [(early_turns, (2,), blocks, 0, 2)]
                _, *more = more_sums("across_sums", [], [], jobs, spectra, [])
                _, more_kept, more_sent = more_sums("across_sums", [], [], jobs, other, more)
                split = (len(early_turns) - count) * all_pairs // length
                received = jnp.pad(swap_stations(more_sent[split:]), ((split, 0), (0, 0)))
                return kept + more_kept + received

            return add

        short = jnp.clip(order[0, rounds] - len(late_turns), 0, len(early_turns))
        choices = [lambda _, __, kept: kept] + [with_across(count + 1) for count in range(len(early_turns))]
        early_kept = lax.switch(short, choices, spectra, other, early_kept)
        early, late = [early_kept, early_received], [late_kept, late_received]
    else:
        other, late_sent = add_sent("across_sums", traces, places, late_turns, (2,), other, late_sent)
        spectra, early_sent = add_sent("across_sums", [], [], early_turns, (2,), spectra, early_sent)
        other, early_sent = add_sent("across_sums", [], [], early_turns, (2,), other, early_sent)
        early, late = spread(early_sent), spread(late_sent)
    result = finish(order, early, inverse, early_turns, True, None)
    result = finish(order, late, inverse, late_turns, not swap, result)
    return result.reshape(rounds, 1, all_pairs // length, 2 * samples)


def solution(mesh):
    return jax.shard_map(
        on_device,
        mesh=mesh,
        in_specs=(
            P(("groups", "cluster"), "station", None, None),
            P(("groups", "cluster"), "station"),
            P("groups"),
            P(None, "groups"),
            P(None, ("groups", "cluster"), None, None),
            P("groups"),
        ),
        out_specs=P(None, ("groups", "cluster"), "station", None),
        check_vma=False,
    )
```

```python
import math

import jax
import jax.numpy as jnp
import ml_dtypes
import numpy as np
from jax import lax
from jax.experimental import pallas as pl
from jax.experimental.pallas import tpu as pltpu
from jax.sharding import PartitionSpec as P

epsilon = 1e-06
SUB, LANES = 8, 128
HALF = SUB // 2
TILES = 6
ENTRIES = 3
UNROLL = 4
FIRST_SHARE = 9
VMEM_BYTES = 16 * 1024 * 1024
PREPARE_VMEM_BYTES = 62 * 1024 * 1024
F32 = jnp.float32
BF16 = jnp.bfloat16


def split_table(table):
    high = table.astype(ml_dtypes.bfloat16)
    low = (table - high.astype(np.float64)).astype(ml_dtypes.bfloat16)
    return np.stack([high, low])


def forward_table(samples):
    steps = np.arange(samples)
    angles = (steps[:, None] * steps[None, :] % (2 * samples)) * (math.pi / samples)
    return split_table(np.concatenate([np.cos(angles), -np.sin(angles)], axis=1))


def inverse_table(samples):
    record = 2 * samples
    bins = np.arange(samples)
    lags = (np.arange(record) + samples) % record
    angles = (bins[:, None] * lags[None, :] % record) * (math.pi / samples)
    gain = np.where(bins == 0, 1.0, 2.0)[:, None] / record
    return split_table(np.concatenate([gain * np.cos(angles), -gain * np.sin(angles)], axis=0))


def split_dot(value, table_ref):
    rows = value.shape[0]
    high = value.astype(BF16)
    low = (value - high.astype(F32)).astype(BF16)
    both = jnp.dot(jnp.concatenate([high, low], axis=0), table_ref[0], preferred_element_type=F32)
    return both[:rows] + (both[rows:] + jnp.dot(high, table_ref[1], preferred_element_type=F32))


def piece_spots(twos):
    count = twos * FIRST_SHARE // 16
    return [(0, count), (count, twos - count)]


def prepare_kernel(waves_hbm, mask_hbm, weight_hbm, *refs):
    all_hbm, *out_hbms, waves_ref, mask_ref, weight_ref, result_ref, sems = refs
    pieces = len(out_hbms)
    twos, _, channels, stations, _ = waves_ref.shape
    spots = piece_spots(twos)
    copies = [
        pltpu.make_async_copy(weight_hbm, weight_ref, sems.at[0]),
        pltpu.make_async_copy(mask_hbm, mask_ref, sems.at[1]),
    ]
    for piece, (first, count) in enumerate(spots):
        spot = pl.ds(first, count)
        copies.append(pltpu.make_async_copy(waves_hbm.at[spot], waves_ref.at[spot], sems.at[2 + piece]))
    for copy in copies:
        copy.start()
    events = 2 * twos
    rows = 3 * SUB * twos
    row = lax.broadcasted_iota(jnp.int32, (rows, events), 0)
    group, row_here = row // (SUB * twos), row % (SUB * twos)
    event_of_row = jnp.where(group < 2, 2 * (row_here // SUB) + group, row_here // HALF)
    at_event = (event_of_row == lax.broadcasted_iota(jnp.int32, (rows, events), 1)).astype(F32).astype(BF16)
    row = lax.broadcasted_iota(jnp.int32, (rows, stations), 0)
    at_station = row % HALF == lax.broadcasted_iota(jnp.int32, (rows, stations), 1)
    station_id = lax.broadcasted_iota(jnp.int32, (1, stations), 1)
    first_weight = lax.axis_index("station") * stations
    copies[0].wait()
    network = channels * sum(weight_ref[station] for station in range(weight_ref.shape[0]))
    weight = jnp.zeros((1, stations), F32)
    for station in range(stations):
        weight = jnp.where(station_id == station, weight_ref[first_weight + station], weight)
    share = jnp.where(at_station, jnp.sqrt(weight / network), 0.0)
    copies[1].wait()
    picked = lax.dot_general(
        at_event,
        mask_ref[...].astype(F32).astype(BF16),
        (((1,), (1,)), ((), ())),
        preferred_element_type=F32,
    )
    factor = jnp.sum(picked * share, axis=1, keepdims=True).reshape(3, twos, SUB, 1)
    results = []
    for piece, (first, count) in enumerate(spots):
        copies[2 + piece].wait()
        spot = slice(first, first + count)
        for group in range(3):
            for side in range(2):
                part = waves_ref[spot, group, side] if group < 2 else waves_ref[spot, side, 2]
                result_ref[group, spot, side * HALF : (side + 1) * HALF, :] = part
            traces = result_ref[group, spot]
            energy = jnp.sum(traces * traces, axis=-1, keepdims=True)
            result_ref[group, spot] = traces * (lax.rsqrt(energy + epsilon) * factor[group, spot])
        for number, target in enumerate((out_hbms[piece], all_hbm.at[:, pl.ds(first, count)])):
            sem = sems.at[2 + pieces + 2 * piece + number]
            results.append(pltpu.make_async_copy(result_ref.at[:, pl.ds(first, count)], target, sem))
            results[-1].start()
    for copy in results:
        copy.wait()


def prepare(waveforms, event_mask, station_weight):
    events, stations, channels, samples = waveforms.shape
    waves = jnp.transpose(waveforms, (0, 2, 1, 3)).reshape(events // 2, 2, channels, stations, samples)
    hbm = pl.BlockSpec(memory_space=pltpu.HBM)
    spots = piece_spots(events // 2)
    pieces = len(spots)
    shape = (3, events // 2, SUB, samples)
    return pl.pallas_call(
        prepare_kernel,
        out_shape=[jax.ShapeDtypeStruct(shape, F32)]
        + [jax.ShapeDtypeStruct((3, count, SUB, samples), F32) for _, count in spots],
        in_specs=[hbm] * 3,
        out_specs=[hbm] * (1 + pieces),
        scratch_shapes=[
            pltpu.VMEM(waves.shape, F32),
            pltpu.VMEM((stations, events), event_mask.dtype),
            pltpu.SMEM(station_weight.shape, F32),
            pltpu.VMEM(shape, F32),
            pltpu.SemaphoreType.DMA((2 + 3 * pieces,)),
        ],
        compiler_params=pltpu.CompilerParams(vmem_limit_bytes=PREPARE_VMEM_BYTES),
        name="prepare",
    )(waves, event_mask.T, station_weight)


def index_kernel(events, partners_ref, counts_ref, pairs_ref, index_ref, order_ref):
    rounds, _, _, all_pairs = pairs_ref.shape
    here = lax.axis_index("cluster")
    sibling = jnp.where(here % 2 == 0, here + 1, here - 1)
    own_count = counts_ref[here]
    partners = [partners_ref[turn, here] for turn in range(rounds)]
    parts = [jnp.where(partner == here, 0, jnp.where(partner == sibling, 1, 2)) for partner in partners]
    across = jnp.int32(0)
    lane = lax.broadcasted_iota(jnp.int32, (1, LANES), 1)
    order = jnp.zeros((1, LANES), jnp.int32)
    for turn in range(rounds):
        part = parts[turn]
        across += (part == 2).astype(jnp.int32)
        place = jnp.int32(0)
        for other in range(rounds):
            ahead = parts[other] <= part if other < turn else parts[other] < part
            place += ahead.astype(jnp.int32)
        order = jnp.where(lane == place, turn, order)
        first, second = pairs_ref[turn, 0, 0:1], pairs_ref[turn, 0, 1:2]
        valid = (first < own_count) & (second < counts_ref[partners[turn]])
        entries = (
            TILES * jnp.where(valid, first, events),
            TILES * (second + part * (events + 2)),
            jnp.full((1, all_pairs), part, jnp.int32),
        )
        for kind, entry in enumerate(entries):
            for row in range(all_pairs // LANES):
                spot = (ENTRIES * place + kind) * (all_pairs // LANES) + row
                index_ref[pl.ds(spot, 1)] = entry[:, row * LANES : (row + 1) * LANES]
    order_ref[...] = jnp.where(lane == rounds, across, order)


def pair_index(partners, counts, pair_list, events):
    rounds, _, all_pairs, _ = pair_list.shape
    vmem = pl.BlockSpec(memory_space=pltpu.VMEM)
    smem = pl.BlockSpec(memory_space=pltpu.SMEM)
    return pl.pallas_call(
        lambda *refs: index_kernel(events, *refs),
        out_shape=[
            jax.ShapeDtypeStruct((rounds * ENTRIES * all_pairs // LANES, LANES), jnp.int32),
            jax.ShapeDtypeStruct((1, LANES), jnp.int32),
        ],
        in_specs=[smem, smem, vmem],
        out_specs=[vmem, vmem],
        compiler_params=pltpu.CompilerParams(vmem_limit_bytes=VMEM_BYTES),
        name="pair_index",
    )(partners, counts, jnp.transpose(pair_list, (0, 1, 3, 2)))


def fill_spectra(traces_ref, part, first, table_ref, spectra_ref):
    _, twos, _, samples = traces_ref.shape
    spot = pl.ds(first, twos)
    spectrum = split_dot(traces_ref[...].reshape(3 * twos * SUB, samples), table_ref)
    tiles = [
        spectrum[:, block * LANES : (block + 1) * LANES].reshape(3, twos, SUB, LANES) for block in range(4)
    ]
    low_half = lax.broadcasted_iota(jnp.int32, (twos, SUB, LANES), 1) < HALF
    for group in range(3):
        for side in range(2):
            lower, upper = tiles[2 * side][group], tiles[2 * side + 1][group]
            first = jnp.where(low_half, lower, pltpu.roll(upper, HALF, 1))
            second = jnp.where(low_half, pltpu.roll(lower, HALF, 1), upper)
            if group < 2:
                spectra_ref[part, spot, group, 3 * side] = first
                spectra_ref[part, spot, group, 3 * side + 1] = second
            else:
                spectra_ref[part, spot, 0, 3 * side + 2] = first
                spectra_ref[part, spot, 1, 3 * side + 2] = second


def clear_last(spectra_ref):
    spectra_ref[0, spectra_ref.shape[1] - 1] = jnp.zeros(spectra_ref.shape[2:], F32)


def spectra_kernel(places, first, *refs):
    trace_refs, table_ref, spectra_ref = refs[: len(places)], refs[len(places)], refs[-1]
    for (part, pair), traces_ref in zip(places, trace_refs, strict=True):
        fill_spectra(traces_ref, part, pair, table_ref, spectra_ref)
    if first:
        clear_last(spectra_ref)


def add_pairs(index_ref, all_pairs, turns, wanted, blocks, spectra_ref, base_refs, out_refs):
    slots = 2 * spectra_ref.shape[1]
    length = lax.axis_size("station")
    station_here = lax.axis_index("station")
    swap = length == 4
    block_pairs = all_pairs // length
    flat_ref = spectra_ref.reshape(spectra_ref.shape[0] * slots * TILES, SUB, LANES)
    row_id = lax.broadcasted_iota(jnp.int32, (SUB, LANES), 0)
    in_four, in_two, in_one = row_id < 4, row_id % 4 < 2, row_id % 2 < 1

    def down(value, rows):
        return pltpu.roll(value, rows % SUB, 0)

    def fold_four(sums):
        even, odd = (
            jnp.where(in_two, one + down(one, -2), other + down(other, 2)) for one, other in (sums[0::2], sums[1::2])
        )
        return jnp.where(in_one, even + down(even, -1), odd + down(odd, 1))

    def fold_eight(sums):
        one, other = fold_four(sums[:4]), fold_four(sums[4:])
        return jnp.where(in_four, one, down(other, 4)), jnp.where(in_four, down(one, 4), other)

    def one_turn(place, turn):
        for number, block in enumerate(blocks):
            if swap:
                source = station_here if block == 0 else station_here + 1 - 2 * (station_here % 2)
                which, row = number, place * block_pairs
            else:
                source = station_here // len(blocks) * len(blocks) + block
                which, row = 0, (place * len(blocks) + block) * block_pairs
            start = source * block_pairs

            def eight_pairs(group, carry):
                real, imag = [], []
                first = start + group * SUB
                for spot in range(SUB):
                    entry = ENTRIES * turn * all_pairs + spot
                    left = flat_ref[pl.ds(index_ref[entry + first], TILES)]
                    right = flat_ref[pl.ds(index_ref[entry + all_pairs + first], TILES)]
                    reals, imags = [], []
                    for tile in range(3):
                        left_real, left_imag = left[tile], left[tile + 3]
                        right_real, right_imag = right[tile], right[tile + 3]
                        reals.append(left_real * right_real + left_imag * right_imag)
                        imags.append(left_imag * right_real - left_real * right_imag)
                    real.append(reals[0] + reals[1] + reals[2])
                    imag.append(imags[0] + imags[1] + imags[2])
                rows = pl.ds(pl.multiple_of(row + group * SUB, SUB), SUB)
                for column, total in enumerate((*fold_eight(real), *fold_eight(imag))):
                    spot = pl.ds(column * LANES, LANES)
                    if base_refs is not None:
                        total += base_refs[which][rows, spot]
                    out_refs[which][rows, spot] = total
                return carry

            lax.fori_loop(0, block_pairs // SUB, eight_pairs, 0, unroll=min(UNROLL, block_pairs // SUB))

    for place, turn in enumerate(turns):
        pl.when(wanted(index_ref[(ENTRIES * turn + 2) * all_pairs]))(lambda: one_turn(place, turn))


def half_turns(rounds, half):
    return range(half * rounds // 2, (half + 1) * rounds // 2)


def index_copy(index_hbm, index_ref, sem):
    copy = pltpu.make_async_copy(index_hbm, index_ref, sem)
    copy.start()
    return copy


def first_near_kernel(blocks, rounds, all_pairs, index_hbm, own_ref, sibling_ref, table_ref, spectra_ref, *refs):
    *out_refs, index_ref, sem = refs
    copy = index_copy(index_hbm, index_ref, sem)
    fill_spectra(own_ref, 0, 0, table_ref, spectra_ref)
    fill_spectra(sibling_ref, 1, 0, table_ref, spectra_ref)
    clear_last(spectra_ref)
    copy.wait()
    for out_ref in out_refs:
        out_ref[...] = jnp.zeros(out_ref.shape, F32)
    for half in range(2):
        turns = half_turns(rounds, half)
        some = out_refs[half * len(out_refs) // 2 : (half + 1) * len(out_refs) // 2]
        add_pairs(index_ref, all_pairs, turns, lambda part: part < 2, blocks, spectra_ref, None, some)


def more_kernel(all_pairs, places, jobs, with_inverse, has_base, *refs):
    count = len(places)
    index_hbm, trace_refs, refs = refs[0], refs[1 : 1 + count], refs[1 + count :]
    if count:
        table_ref, refs = refs[0], refs[1:]
    if with_inverse:
        inverse_ref, refs = refs[0], refs[1:]
    *refs, index_ref, sem = refs
    arrays = len(refs) // 2 - 1 if has_base else len(refs) - 2
    base_refs = refs[1 : 1 + arrays] if has_base else None
    spectra_ref, *out_refs = refs[-1 - arrays :]
    copy = index_copy(index_hbm, index_ref, sem)
    for (part, pair), traces_ref in zip(places, trace_refs, strict=True):
        fill_spectra(traces_ref, part, pair, table_ref, spectra_ref)
    if not has_base:
        for out_ref in out_refs:
            out_ref[...] = jnp.zeros(out_ref.shape, F32)
    copy.wait()
    for turns, parts, blocks, first, last in jobs:

        def wanted(part, parts=parts):
            return (part >= parts[0]) & (part <= parts[-1])

        base = base_refs[first:last] if has_base else None
        add_pairs(index_ref, all_pairs, turns, wanted, blocks, spectra_ref, base, out_refs[first:last])
    if with_inverse:
        out_refs[-1][...] = split_dot(out_refs[-1][...], inverse_ref)


def call_kernel(kernel, name, operands, specs, updated, out_shapes, scratch, flops):
    vmem = pl.BlockSpec(memory_space=pltpu.VMEM)
    operands = [*operands, *updated]
    shapes = [*(jax.ShapeDtypeStruct(value.shape, value.dtype) for value in updated), *out_shapes]
    first_in = len(operands) - len(updated)
    in_specs = [vmem] * len(operands)
    out_specs = [vmem] * len(shapes)
    for place, spec in specs.items():
        in_specs[place] = spec
        if place >= first_in:
            out_specs[place - first_in] = spec
    return pl.pallas_call(
        kernel,
        out_shape=shapes,
        in_specs=in_specs,
        out_specs=out_specs,
        scratch_shapes=scratch,
        input_output_aliases={first_in + i: i for i in range(len(updated))},
        compiler_params=pltpu.CompilerParams(vmem_limit_bytes=VMEM_BYTES),
        cost_estimate=pl.CostEstimate(flops=flops, bytes_accessed=flops // 1000, transcendentals=0),
        name=name,
    )(*operands)


def finish_kernel(turns, invert, terms, order_ref, table_ref, *refs):
    term_refs, (out_hbm, result_ref, sems) = refs[:terms], refs[-3:]
    rows = result_ref.shape[0] // len(turns)
    lane = lax.broadcasted_iota(jnp.int32, (1, LANES), 1)
    order = order_ref[...].astype(F32)
    targets = [jnp.sum(jnp.where(lane == turn, order, 0.0)).astype(jnp.int32) for turn in turns]
    total = sum(ref[...] for ref in term_refs)
    result_ref[...] = split_dot(total, table_ref) if invert else total
    copies = [
        pltpu.make_async_copy(
            result_ref.at[pl.ds(number * rows, rows)],
            out_hbm.at[pl.ds(pl.multiple_of(target * rows, SUB), rows)],
            sems.at[number],
        )
        for number, target in enumerate(targets)
    ]
    for copy in copies:
        copy.start()
    for copy in copies:
        copy.wait()


def finish(order, terms, table, turns, invert, result):
    rows, lags = terms[0].shape
    vmem = pl.BlockSpec(memory_space=pltpu.VMEM)
    hbm = pl.BlockSpec(memory_space=pltpu.HBM)
    operands = [order, table, *terms] + ([] if result is None else [result])
    return pl.pallas_call(
        lambda *refs: finish_kernel(turns, invert, len(terms), *refs),
        out_shape=jax.ShapeDtypeStruct((2 * rows, lags), F32),
        in_specs=[vmem] * (2 + len(terms)) + ([] if result is None else [hbm]),
        out_specs=hbm,
        scratch_shapes=[
            pltpu.VMEM((rows, lags), F32),
            pltpu.SemaphoreType.DMA((len(turns),)),
        ],
        input_output_aliases={} if result is None else {2 + len(terms): 0},
        compiler_params=pltpu.CompilerParams(vmem_limit_bytes=VMEM_BYTES),
        cost_estimate=pl.CostEstimate(flops=1, bytes_accessed=1, transcendentals=0),
        name="finish",
    )(*operands)


def on_device(waveforms, event_mask, station_weight, partners, pair_list, counts):
    events, stations, channels, samples = waveforms.shape
    rounds, _, all_pairs, _ = pair_list.shape
    clusters = lax.axis_size("cluster")
    length = lax.axis_size("station")
    assert (stations, channels, samples) == (HALF, 3, 2 * LANES)
    assert events % 4 == 0 and rounds % 2 == 0 and clusters % 2 == 0 and length % 4 == 0
    forward = jnp.asarray(forward_table(samples))
    inverse = jnp.asarray(inverse_table(samples))

    def to_sibling(value):
        return lax.ppermute(value, "cluster", [(i, i ^ 1) for i in range(clusters)])

    def to_across(value):
        return lax.ppermute(value, "cluster", [(i, (i + 1 if i % 2 else i - 1) % clusters) for i in range(clusters)])

    def to_mirror(value):
        return lax.ppermute(value, "station", [(i, length - 1 - i) for i in range(length)])

    def swap_stations(value):
        return lax.ppermute(value, "station", [(i, i ^ 1) for i in range(length)])

    def spread(value):
        groups = np.arange(length).reshape(2, length // 2).tolist()
        value = value.reshape(rounds // 2, all_pairs // 2, 2 * samples)
        kept = lax.psum_scatter(value, "station", scatter_dimension=1, axis_index_groups=groups, tiled=True)
        return [kept.reshape(-1, 2 * samples)]

    def invert(cross, table):
        return call_kernel(invert_kernel, "invert", [cross, table], {}, [], [half_shape], [], 1)[0]

    swap = length == 4
    blocks = list(range(length // 2))
    outs = 2 if swap else 1
    half_shape = jax.ShapeDtypeStruct((rounds * all_pairs // 4 // outs, 2 * samples), F32)
    spectra_shape = jax.ShapeDtypeStruct((3, events // 2 + 1, 2, TILES, SUB, LANES), F32)
    scratch = [
        pltpu.SMEM((rounds * ENTRIES * all_pairs,), jnp.int32),
        pltpu.SemaphoreType.DMA,
    ]

    anywhere = {0: pl.BlockSpec(memory_space=pl.ANY)}

    def add_spectra(traces, places, spectra, flops):
        return call_kernel(
            lambda *refs: spectra_kernel(places, not spectra, *refs),
            "add_spectra",
            [*traces, forward],
            {},
            spectra,
            [] if spectra else [spectra_shape],
            [],
            flops,
        )

    early_turns, late_turns = half_turns(rounds, 0), half_turns(rounds, 1)

    def more_sums(name, traces, places, jobs, spectra, base, with_inverse=False):
        tables = [forward] * bool(traces) + [inverse] * with_inverse
        return call_kernel(
            lambda *refs: more_kernel(all_pairs, places, jobs, with_inverse, bool(base), *refs),
            name,
            [index, *traces, *tables],
            anywhere,
            [spectra, *base],
            [] if base else [half_shape] * outs,
            scratch,
            1,
        )

    own, *pieces = prepare(waveforms, event_mask, station_weight)
    index, order = pair_index(partners, counts, pair_list, events)
    index = index.reshape(-1)
    mirror_first, mirror_last = (to_mirror(piece) for piece in pieces)
    across = [to_across(piece) for piece in pieces]
    sibling = to_sibling(own)
    spectra, *partial = call_kernel(
        lambda *refs: first_near_kernel(blocks, rounds, all_pairs, *refs),
        "first_near",
        [index, own, sibling, forward],
        anywhere,
        [],
        [spectra_shape] + [half_shape] * (2 * outs),
        scratch,
        1,
    )
    mirror_first, *partial = lax.optimization_barrier((mirror_first, *partial))
    far_first, near_first = to_across(mirror_first), to_sibling(mirror_first)
    (other,) = add_spectra([mirror_first], [(0, 0)], [], 1)
    early, late = partial[:outs], partial[outs:]
    later = mirror_first.shape[1]
    other, spectra = lax.optimization_barrier((other, spectra))
    (spectra,) = add_spectra(across, [(2, 0), (2, later)], [spectra], 1)
    mirror_last, other, spectra = lax.optimization_barrier((mirror_last, other, spectra))
    far_last, near_last = to_across(mirror_last), to_sibling(mirror_last)
    sent = blocks[1:] if swap else blocks
    *early_kept, early_sent = early

    def add_sent(name, traces, places, turns, parts, spectra, value, **options):
        return more_sums(name, traces, places, [(turns, parts, sent, 0, 1)], spectra, [value], **options)

    traces, places = [mirror_last, near_first, near_last], [(0, later), (1, 0), (1, later)]
    other, early_sent = add_sent("near_sums", traces, places, early_turns, (0, 1), other, early_sent)
    early_sent, spectra, *late = lax.optimization_barrier((early_sent, spectra, *late))
    jobs = [(late_turns, (2,), blocks, 0, outs)]
    spectra, *late = more_sums("across_sums", [], [], jobs, spectra, late)
    *late_kept, late_sent = late
    other, late_sent = add_sent("near_sums", [far_first], [(2, 0)], late_turns, (0, 1), other, late_sent)
    traces, places = [far_last], [(2, later)]
    if swap:
        early_received = swap_stations(early_sent)
        other, late_sent = add_sent(
            "across_sums", traces, places, late_turns, (2,), other, late_sent, with_inverse=True
        )
        late_received = swap_stations(late_sent)
        jobs = [(early_turns, (0, 1), blocks[:1], 0, 1), (late_turns, (0, 1, 2), blocks[:1], 1, 2)]
        kept = early_kept + late_kept
        other, early_kept, late_kept = more_sums("kept_sums", [], [], jobs, other, kept, with_inverse=True)

        def with_across(count):
            def add(spectra, other, kept):
                jobs = [(early_turns, (2,), blocks, 0, 2)]
                _, *more = more_sums("across_sums", [], [], jobs, spectra, [])
                _, more_kept, more_sent = more_sums("across_sums", [], [], jobs, other, more)
                split = (len(early_turns) - count) * all_pairs // length
                received = jnp.pad(swap_stations(more_sent[split:]), ((split, 0), (0, 0)))
                return kept + more_kept + received

            return add

        short = jnp.clip(order[0, rounds] - len(late_turns), 0, len(early_turns))
        choices = [lambda _, __, kept: kept] + [with_across(count + 1) for count in range(len(early_turns))]
        early_kept = lax.switch(short, choices, spectra, other, early_kept)
        early, late = [early_kept, early_received], [late_kept, late_received]
    else:
        other, late_sent = add_sent("across_sums", traces, places, late_turns, (2,), other, late_sent)
        spectra, early_sent = add_sent("across_sums", [], [], early_turns, (2,), spectra, early_sent)
        other, early_sent = add_sent("across_sums", [], [], early_turns, (2,), other, early_sent)
        early, late = spread(early_sent), spread(late_sent)
    result = finish(order, early, inverse, early_turns, True, None)
    result = finish(order, late, inverse, late_turns, not swap, result)
    return result.reshape(rounds, 1, all_pairs // length, 2 * samples)


def solution(mesh):
    return jax.shard_map(
        on_device,
        mesh=mesh,
        in_specs=(
            P(("groups", "cluster"), "station", None, None),
            P(("groups", "cluster"), "station"),
            P("groups"),
            P(None, "groups"),
            P(None, ("groups", "cluster"), None, None),
            P("groups"),
        ),
        out_specs=P(None, ("groups", "cluster"), "station", None),
        check_vma=False,
    )
```

```python
import math

import jax
import jax.numpy as jnp
import ml_dtypes
import numpy as np
from jax import lax
from jax.experimental import pallas as pl
from jax.experimental.pallas import tpu as pltpu
from jax.sharding import PartitionSpec as P

epsilon = 1e-06
SUB, LANES = 8, 128
HALF = SUB // 2
TILES = 6
ENTRIES = 3
UNROLL = 4
FIRST_SHARE = 9
VMEM_BYTES = 16 * 1024 * 1024
PREPARE_VMEM_BYTES = 62 * 1024 * 1024
F32 = jnp.float32
BF16 = jnp.bfloat16


def split_table(table):
    high = table.astype(ml_dtypes.bfloat16)
    low = (table - high.astype(np.float64)).astype(ml_dtypes.bfloat16)
    return np.stack([high, low])


def forward_table(samples):
    steps = np.arange(samples)
    angles = (steps[:, None] * steps[None, :] % (2 * samples)) * (math.pi / samples)
    return split_table(np.concatenate([np.cos(angles), -np.sin(angles)], axis=1))


def inverse_table(samples):
    record = 2 * samples
    bins = np.arange(samples)
    lags = (np.arange(record) + samples) % record
    angles = (bins[:, None] * lags[None, :] % record) * (math.pi / samples)
    gain = np.where(bins == 0, 1.0, 2.0)[:, None] / record
    return split_table(np.concatenate([gain * np.cos(angles), -gain * np.sin(angles)], axis=0))


def split_dot(value, table_ref):
    rows = value.shape[0]
    high = value.astype(BF16)
    low = (value - high.astype(F32)).astype(BF16)
    both = jnp.dot(jnp.concatenate([high, low], axis=0), table_ref[0], preferred_element_type=F32)
    return both[:rows] + (both[rows:] + jnp.dot(high, table_ref[1], preferred_element_type=F32))


def piece_spots(twos):
    count = twos * FIRST_SHARE // 16
    return [(0, count), (count, twos - count)]


def prepare_kernel(waves_hbm, mask_hbm, weight_hbm, *refs):
    all_hbm, *out_hbms, waves_ref, mask_ref, weight_ref, result_ref, sems = refs
    pieces = len(out_hbms)
    twos, _, channels, stations, _ = waves_ref.shape
    spots = piece_spots(twos)
    copies = [
        pltpu.make_async_copy(weight_hbm, weight_ref, sems.at[0]),
        pltpu.make_async_copy(mask_hbm, mask_ref, sems.at[1]),
    ]
    for piece, (first, count) in enumerate(spots):
        spot = pl.ds(first, count)
        copies.append(pltpu.make_async_copy(waves_hbm.at[spot], waves_ref.at[spot], sems.at[2 + piece]))
    for copy in copies:
        copy.start()
    events = 2 * twos
    rows = 3 * SUB * twos
    row = lax.broadcasted_iota(jnp.int32, (rows, events), 0)
    group, row_here = row // (SUB * twos), row % (SUB * twos)
    event_of_row = jnp.where(group < 2, 2 * (row_here // SUB) + group, row_here // HALF)
    at_event = (event_of_row == lax.broadcasted_iota(jnp.int32, (rows, events), 1)).astype(F32).astype(BF16)
    row = lax.broadcasted_iota(jnp.int32, (rows, stations), 0)
    at_station = row % HALF == lax.broadcasted_iota(jnp.int32, (rows, stations), 1)
    station_id = lax.broadcasted_iota(jnp.int32, (1, stations), 1)
    first_weight = lax.axis_index("station") * stations
    copies[0].wait()
    network = channels * sum(weight_ref[station] for station in range(weight_ref.shape[0]))
    weight = jnp.zeros((1, stations), F32)
    for station in range(stations):
        weight = jnp.where(station_id == station, weight_ref[first_weight + station], weight)
    share = jnp.where(at_station, jnp.sqrt(weight / network), 0.0)
    copies[1].wait()
    picked = lax.dot_general(
        at_event,
        mask_ref[...].astype(F32).astype(BF16),
        (((1,), (1,)), ((), ())),
        preferred_element_type=F32,
    )
    factor = jnp.sum(picked * share, axis=1, keepdims=True).reshape(3, twos, SUB, 1)
    results = []
    for piece, (first, count) in enumerate(spots):
        copies[2 + piece].wait()
        spot = slice(first, first + count)
        for group in range(3):
            for side in range(2):
                part = waves_ref[spot, group, side] if group < 2 else waves_ref[spot, side, 2]
                result_ref[group, spot, side * HALF : (side + 1) * HALF, :] = part
            traces = result_ref[group, spot]
            energy = jnp.sum(traces * traces, axis=-1, keepdims=True)
            result_ref[group, spot] = traces * (lax.rsqrt(energy + epsilon) * factor[group, spot])
        for number, target in enumerate((out_hbms[piece], all_hbm.at[:, pl.ds(first, count)])):
            sem = sems.at[2 + pieces + 2 * piece + number]
            results.append(pltpu.make_async_copy(result_ref.at[:, pl.ds(first, count)], target, sem))
            results[-1].start()
    for copy in results:
        copy.wait()


def prepare(waveforms, event_mask, station_weight):
    events, stations, channels, samples = waveforms.shape
    waves = jnp.transpose(waveforms, (0, 2, 1, 3)).reshape(events // 2, 2, channels, stations, samples)
    hbm = pl.BlockSpec(memory_space=pltpu.HBM)
    spots = piece_spots(events // 2)
    pieces = len(spots)
    shape = (3, events // 2, SUB, samples)
    return pl.pallas_call(
        prepare_kernel,
        out_shape=[jax.ShapeDtypeStruct(shape, F32)]
        + [jax.ShapeDtypeStruct((3, count, SUB, samples), F32) for _, count in spots],
        in_specs=[hbm] * 3,
        out_specs=[hbm] * (1 + pieces),
        scratch_shapes=[
            pltpu.VMEM(waves.shape, F32),
            pltpu.VMEM((stations, events), event_mask.dtype),
            pltpu.SMEM(station_weight.shape, F32),
            pltpu.VMEM(shape, F32),
            pltpu.SemaphoreType.DMA((2 + 3 * pieces,)),
        ],
        compiler_params=pltpu.CompilerParams(vmem_limit_bytes=PREPARE_VMEM_BYTES),
        name="prepare",
    )(waves, event_mask.T, station_weight)


def index_kernel(events, partners_ref, counts_ref, pairs_ref, index_ref, order_ref):
    rounds, _, _, all_pairs = pairs_ref.shape
    here = lax.axis_index("cluster")
    sibling = jnp.where(here % 2 == 0, here + 1, here - 1)
    own_count = counts_ref[here]
    partners = [partners_ref[turn, here] for turn in range(rounds)]
    parts = [jnp.where(partner == here, 0, jnp.where(partner == sibling, 1, 2)) for partner in partners]
    across = jnp.int32(0)
    lane = lax.broadcasted_iota(jnp.int32, (1, LANES), 1)
    order = jnp.zeros((1, LANES), jnp.int32)
    for turn in range(rounds):
        part = parts[turn]
        across += (part == 2).astype(jnp.int32)
        place = jnp.int32(0)
        for other in range(rounds):
            ahead = parts[other] <= part if other < turn else parts[other] < part
            place += ahead.astype(jnp.int32)
        order = jnp.where(lane == place, turn, order)
        first, second = pairs_ref[turn, 0, 0:1], pairs_ref[turn, 0, 1:2]
        valid = (first < own_count) & (second < counts_ref[partners[turn]])
        entries = (
            TILES * jnp.where(valid, first, events),
            TILES * (second + part * (events + 2)),
            jnp.full((1, all_pairs), part, jnp.int32),
        )
        for kind, entry in enumerate(entries):
            for row in range(all_pairs // LANES):
                spot = (ENTRIES * place + kind) * (all_pairs // LANES) + row
                index_ref[pl.ds(spot, 1)] = entry[:, row * LANES : (row + 1) * LANES]
    order_ref[...] = jnp.where(lane == rounds, across, order)


def pair_index(partners, counts, pair_list, events):
    rounds, _, all_pairs, _ = pair_list.shape
    vmem = pl.BlockSpec(memory_space=pltpu.VMEM)
    smem = pl.BlockSpec(memory_space=pltpu.SMEM)
    return pl.pallas_call(
        lambda *refs: index_kernel(events, *refs),
        out_shape=[
            jax.ShapeDtypeStruct((rounds * ENTRIES * all_pairs // LANES, LANES), jnp.int32),
            jax.ShapeDtypeStruct((1, LANES), jnp.int32),
        ],
        in_specs=[smem, smem, vmem],
        out_specs=[vmem, vmem],
        compiler_params=pltpu.CompilerParams(vmem_limit_bytes=VMEM_BYTES),
        name="pair_index",
    )(partners, counts, jnp.transpose(pair_list, (0, 1, 3, 2)))


def fill_spectra(traces_ref, part, first, table_ref, spectra_ref):
    _, twos, _, samples = traces_ref.shape
    spot = pl.ds(first, twos)
    spectrum = split_dot(traces_ref[...].reshape(3 * twos * SUB, samples), table_ref)
    tiles = [
        spectrum[:, block * LANES : (block + 1) * LANES].reshape(3, twos, SUB, LANES) for block in range(4)
    ]
    low_half = lax.broadcasted_iota(jnp.int32, (twos, SUB, LANES), 1) < HALF
    for group in range(3):
        for side in range(2):
            lower, upper = tiles[2 * side][group], tiles[2 * side + 1][group]
            first = jnp.where(low_half, lower, pltpu.roll(upper, HALF, 1))
            second = jnp.where(low_half, pltpu.roll(lower, HALF, 1), upper)
            if group < 2:
                spectra_ref[part, spot, group, 3 * side] = first
                spectra_ref[part, spot, group, 3 * side + 1] = second
            else:
                spectra_ref[part, spot, 0, 3 * side + 2] = first
                spectra_ref[part, spot, 1, 3 * side + 2] = second


def clear_last(spectra_ref):
    spectra_ref[0, spectra_ref.shape[1] - 1] = jnp.zeros(spectra_ref.shape[2:], F32)


def spectra_kernel(places, first, *refs):
    trace_refs, table_ref, spectra_ref = refs[: len(places)], refs[len(places)], refs[-1]
    for (part, pair), traces_ref in zip(places, trace_refs, strict=True):
        fill_spectra(traces_ref, part, pair, table_ref, spectra_ref)
    if first:
        clear_last(spectra_ref)


def add_pairs(index_ref, all_pairs, turns, wanted, blocks, spectra_ref, base_refs, out_refs):
    slots = 2 * spectra_ref.shape[1]
    length = lax.axis_size("station")
    station_here = lax.axis_index("station")
    swap = length == 4
    block_pairs = all_pairs // length
    flat_ref = spectra_ref.reshape(spectra_ref.shape[0] * slots * TILES, SUB, LANES)
    row_id = lax.broadcasted_iota(jnp.int32, (SUB, LANES), 0)
    in_four, in_two, in_one = row_id < 4, row_id % 4 < 2, row_id % 2 < 1

    def down(value, rows):
        return pltpu.roll(value, rows % SUB, 0)

    def fold_four(sums):
        even, odd = (
            jnp.where(in_two, one + down(one, -2), other + down(other, 2)) for one, other in (sums[0::2], sums[1::2])
        )
        return jnp.where(in_one, even + down(even, -1), odd + down(odd, 1))

    def fold_eight(sums):
        one, other = fold_four(sums[:4]), fold_four(sums[4:])
        return jnp.where(in_four, one, down(other, 4)), jnp.where(in_four, down(one, 4), other)

    def one_turn(place, turn):
        for number, block in enumerate(blocks):
            if swap:
                source = station_here if block == 0 else station_here + 1 - 2 * (station_here % 2)
                which, row = number, place * block_pairs
            else:
                source = station_here // len(blocks) * len(blocks) + block
                which, row = 0, (place * len(blocks) + block) * block_pairs
            start = source * block_pairs

            def eight_pairs(group, carry):
                real, imag = [], []
                first = start + group * SUB
                for spot in range(SUB):
                    entry = ENTRIES * turn * all_pairs + spot
                    left = flat_ref[pl.ds(index_ref[entry + first], TILES)]
                    right = flat_ref[pl.ds(index_ref[entry + all_pairs + first], TILES)]
                    reals, imags = [], []
                    for tile in range(3):
                        left_real, left_imag = left[tile], left[tile + 3]
                        right_real, right_imag = right[tile], right[tile + 3]
                        reals.append(left_real * right_real + left_imag * right_imag)
                        imags.append(left_imag * right_real - left_real * right_imag)
                    real.append(reals[0] + reals[1] + reals[2])
                    imag.append(imags[0] + imags[1] + imags[2])
                rows = pl.ds(pl.multiple_of(row + group * SUB, SUB), SUB)
                for column, total in enumerate((*fold_eight(real), *fold_eight(imag))):
                    spot = pl.ds(column * LANES, LANES)
                    if base_refs is not None:
                        total += base_refs[which][rows, spot]
                    out_refs[which][rows, spot] = total
                return carry

            lax.fori_loop(0, block_pairs // SUB, eight_pairs, 0, unroll=min(UNROLL, block_pairs // SUB))

    for place, turn in enumerate(turns):
        pl.when(wanted(index_ref[(ENTRIES * turn + 2) * all_pairs]))(lambda: one_turn(place, turn))


def half_turns(rounds, half):
    return range(half * rounds // 2, (half + 1) * rounds // 2)


def index_copy(index_hbm, index_ref, sem):
    copy = pltpu.make_async_copy(index_hbm, index_ref, sem)
    copy.start()
    return copy


def first_near_kernel(blocks, rounds, all_pairs, index_hbm, own_ref, sibling_ref, table_ref, spectra_ref, *refs):
    *out_refs, index_ref, sem = refs
    copy = index_copy(index_hbm, index_ref, sem)
    fill_spectra(own_ref, 0, 0, table_ref, spectra_ref)
    fill_spectra(sibling_ref, 1, 0, table_ref, spectra_ref)
    clear_last(spectra_ref)
    copy.wait()
    for out_ref in out_refs:
        out_ref[...] = jnp.zeros(out_ref.shape, F32)
    for half in range(2):
        turns = half_turns(rounds, half)
        some = out_refs[half * len(out_refs) // 2 : (half + 1) * len(out_refs) // 2]
        add_pairs(index_ref, all_pairs, turns, lambda part: part < 2, blocks, spectra_ref, None, some)


def more_kernel(all_pairs, places, jobs, with_inverse, has_base, *refs):
    count = len(places)
    index_hbm, trace_refs, refs = refs[0], refs[1 : 1 + count], refs[1 + count :]
    if count:
        table_ref, refs = refs[0], refs[1:]
    if with_inverse:
        inverse_ref, refs = refs[0], refs[1:]
    *refs, index_ref, sem = refs
    arrays = len(refs) // 2 - 1 if has_base else len(refs) - 2
    base_refs = refs[1 : 1 + arrays] if has_base else None
    spectra_ref, *out_refs = refs[-1 - arrays :]
    copy = index_copy(index_hbm, index_ref, sem)
    for (part, pair, *_), traces_ref in zip(places, trace_refs, strict=True):
        if part != 1:
            fill_spectra(traces_ref, part, pair, table_ref, spectra_ref)
    if not has_base:
        for out_ref in out_refs:
            out_ref[...] = jnp.zeros(out_ref.shape, F32)
    copy.wait()
    for (part, pair, *turn), traces_ref in zip(places, trace_refs, strict=True):
        if part == 1:
            mixed = index_ref[(ENTRIES * turn[0] + 2) * all_pairs] > 0
            fill = lambda ref=traces_ref, pair=pair: fill_spectra(ref, 1, pair, table_ref, spectra_ref)
            pl.when(mixed if turn[1] else jnp.logical_not(mixed))(fill)
    for turns, parts, blocks, first, last in jobs:

        def wanted(part, parts=parts):
            return (part >= parts[0]) & (part <= parts[-1])

        base = base_refs[first:last] if has_base else None
        add_pairs(index_ref, all_pairs, turns, wanted, blocks, spectra_ref, base, out_refs[first:last])
    if with_inverse:
        out_refs[-1][...] = split_dot(out_refs[-1][...], inverse_ref)


def call_kernel(kernel, name, operands, specs, updated, out_shapes, scratch, flops):
    vmem = pl.BlockSpec(memory_space=pltpu.VMEM)
    operands = [*operands, *updated]
    shapes = [*(jax.ShapeDtypeStruct(value.shape, value.dtype) for value in updated), *out_shapes]
    first_in = len(operands) - len(updated)
    in_specs = [vmem] * len(operands)
    out_specs = [vmem] * len(shapes)
    for place, spec in specs.items():
        in_specs[place] = spec
        if place >= first_in:
            out_specs[place - first_in] = spec
    return pl.pallas_call(
        kernel,
        out_shape=shapes,
        in_specs=in_specs,
        out_specs=out_specs,
        scratch_shapes=scratch,
        input_output_aliases={first_in + i: i for i in range(len(updated))},
        compiler_params=pltpu.CompilerParams(vmem_limit_bytes=VMEM_BYTES),
        cost_estimate=pl.CostEstimate(flops=flops, bytes_accessed=flops // 1000, transcendentals=0),
        name=name,
    )(*operands)


def finish_kernel(turns, invert, terms, order_ref, table_ref, *refs):
    term_refs, (out_hbm, result_ref, sems) = refs[:terms], refs[-3:]
    rows = result_ref.shape[0] // len(turns)
    lane = lax.broadcasted_iota(jnp.int32, (1, LANES), 1)
    order = order_ref[...].astype(F32)
    targets = [jnp.sum(jnp.where(lane == turn, order, 0.0)).astype(jnp.int32) for turn in turns]
    total = sum(ref[...] for ref in term_refs)
    result_ref[...] = split_dot(total, table_ref) if invert else total
    copies = [
        pltpu.make_async_copy(
            result_ref.at[pl.ds(number * rows, rows)],
            out_hbm.at[pl.ds(pl.multiple_of(target * rows, SUB), rows)],
            sems.at[number],
        )
        for number, target in enumerate(targets)
    ]
    for copy in copies:
        copy.start()
    for copy in copies:
        copy.wait()


def finish(order, terms, table, turns, invert, result):
    rows, lags = terms[0].shape
    vmem = pl.BlockSpec(memory_space=pltpu.VMEM)
    hbm = pl.BlockSpec(memory_space=pltpu.HBM)
    operands = [order, table, *terms] + ([] if result is None else [result])
    return pl.pallas_call(
        lambda *refs: finish_kernel(turns, invert, len(terms), *refs),
        out_shape=jax.ShapeDtypeStruct((2 * rows, lags), F32),
        in_specs=[vmem] * (2 + len(terms)) + ([] if result is None else [hbm]),
        out_specs=hbm,
        scratch_shapes=[
            pltpu.VMEM((rows, lags), F32),
            pltpu.SemaphoreType.DMA((len(turns),)),
        ],
        input_output_aliases={} if result is None else {2 + len(terms): 0},
        compiler_params=pltpu.CompilerParams(vmem_limit_bytes=VMEM_BYTES),
        cost_estimate=pl.CostEstimate(flops=1, bytes_accessed=1, transcendentals=0),
        name="finish",
    )(*operands)


def on_device(waveforms, event_mask, station_weight, partners, pair_list, counts):
    events, stations, channels, samples = waveforms.shape
    rounds, _, all_pairs, _ = pair_list.shape
    clusters = lax.axis_size("cluster")
    length = lax.axis_size("station")
    assert (stations, channels, samples) == (HALF, 3, 2 * LANES)
    assert events % 4 == 0 and rounds % 2 == 0 and clusters % 2 == 0 and length % 4 == 0
    forward = jnp.asarray(forward_table(samples))
    inverse = jnp.asarray(inverse_table(samples))

    def to_sibling(value):
        return lax.ppermute(value, "cluster", [(i, i ^ 1) for i in range(clusters)])

    def to_across(value):
        return lax.ppermute(value, "cluster", [(i, (i + 1 if i % 2 else i - 1) % clusters) for i in range(clusters)])

    def to_mirror(value):
        return lax.ppermute(value, "station", [(i, length - 1 - i) for i in range(length)])

    def swap_stations(value):
        return lax.ppermute(value, "station", [(i, i ^ 1) for i in range(length)])

    def spread(value):
        groups = np.arange(length).reshape(2, length // 2).tolist()
        value = value.reshape(rounds // 2, all_pairs // 2, 2 * samples)
        kept = lax.psum_scatter(value, "station", scatter_dimension=1, axis_index_groups=groups, tiled=True)
        return [kept.reshape(-1, 2 * samples)]

    def invert(cross, table):
        return call_kernel(invert_kernel, "invert", [cross, table], {}, [], [half_shape], [], 1)[0]

    swap = length == 4
    blocks = list(range(length // 2))
    outs = 2 if swap else 1
    half_shape = jax.ShapeDtypeStruct((rounds * all_pairs // 4 // outs, 2 * samples), F32)
    spectra_shape = jax.ShapeDtypeStruct((3, events // 2 + 1, 2, TILES, SUB, LANES), F32)
    scratch = [
        pltpu.SMEM((rounds * ENTRIES * all_pairs,), jnp.int32),
        pltpu.SemaphoreType.DMA,
    ]

    anywhere = {0: pl.BlockSpec(memory_space=pl.ANY)}

    def add_spectra(traces, places, spectra, flops):
        return call_kernel(
            lambda *refs: spectra_kernel(places, not spectra, *refs),
            "add_spectra",
            [*traces, forward],
            {},
            spectra,
            [] if spectra else [spectra_shape],
            [],
            flops,
        )

    early_turns, late_turns = half_turns(rounds, 0), half_turns(rounds, 1)

    def more_sums(name, traces, places, jobs, spectra, base, with_inverse=False):
        tables = [forward] * bool(traces) + [inverse] * with_inverse
        return call_kernel(
            lambda *refs: more_kernel(all_pairs, places, jobs, with_inverse, bool(base), *refs),
            name,
            [index, *traces, *tables],
            anywhere,
            [spectra, *base],
            [] if base else [half_shape] * outs,
            scratch,
            1,
        )

    own, *pieces = prepare(waveforms, event_mask, station_weight)
    index, order = pair_index(partners, counts, pair_list, events)
    index = index.reshape(-1)
    mirror_first, mirror_last = (to_mirror(piece) for piece in pieces)
    across = [to_across(piece) for piece in pieces]
    sibling = to_sibling(own)
    spectra, *partial = call_kernel(
        lambda *refs: first_near_kernel(blocks, rounds, all_pairs, *refs),
        "first_near",
        [index, own, sibling, forward],
        anywhere,
        [],
        [spectra_shape] + [half_shape] * (2 * outs),
        scratch,
        1,
    )
    mirror_first, *partial = lax.optimization_barrier((mirror_first, *partial))
    far_first, near_first = to_across(mirror_first), to_sibling(mirror_first)
    (other,) = add_spectra([mirror_first], [(0, 0)], [], 1)
    early, late = partial[:outs], partial[outs:]
    later = mirror_first.shape[1]
    other, spectra = lax.optimization_barrier((other, spectra))
    (spectra,) = add_spectra(across, [(2, 0), (2, later)], [spectra], 1)
    mirror_last, other, spectra = lax.optimization_barrier((mirror_last, other, spectra))
    far_last, near_last = to_across(mirror_last), to_sibling(mirror_last)
    sent = blocks[1:] if swap else blocks
    *early_kept, early_sent = early

    def add_sent(name, traces, places, turns, parts, spectra, value, **options):
        return more_sums(name, traces, places, [(turns, parts, sent, 0, 1)], spectra, [value], **options)

    last = early_turns[-1]
    traces = [mirror_last, near_first, near_last]
    places = [(0, later), (1, 0, last, True), (1, later, last, True)]
    other, early_sent = add_sent("near_sums", traces, places, early_turns, (0, 1), other, early_sent)
    early_sent, spectra, *late = lax.optimization_barrier((early_sent, spectra, *late))
    jobs = [(late_turns, (2,), blocks, 0, outs)]
    spectra, *late = more_sums("across_sums", [], [], jobs, spectra, late)
    *late_kept, late_sent = late
    traces = [far_first, near_first, near_last]
    places = [(2, 0), (1, 0, last, False), (1, later, last, False)]
    other, late_sent = add_sent("near_sums", traces, places, late_turns, (0, 1), other, late_sent)
    traces, places = [far_last], [(2, later)]
    if swap:
        early_received = swap_stations(early_sent)
        other, late_sent = add_sent(
            "across_sums", traces, places, late_turns, (2,), other, late_sent, with_inverse=True
        )
        late_received = swap_stations(late_sent)
        jobs = [(early_turns, (0, 1), blocks[:1], 0, 1), (late_turns, (0, 1, 2), blocks[:1], 1, 2)]
        kept = early_kept + late_kept
        other, early_kept, late_kept = more_sums("kept_sums", [], [], jobs, other, kept, with_inverse=True)

        def with_across(count):
            def add(spectra, other, kept):
                jobs = [(early_turns, (2,), blocks, 0, 2)]
                _, *more = more_sums("across_sums", [], [], jobs, spectra, [])
                _, more_kept, more_sent = more_sums("across_sums", [], [], jobs, other, more)
                split = (len(early_turns) - count) * all_pairs // length
                received = jnp.pad(swap_stations(more_sent[split:]), ((split, 0), (0, 0)))
                return kept + more_kept + received

            return add

        short = jnp.clip(order[0, rounds] - len(late_turns), 0, len(early_turns))
        choices = [lambda _, __, kept: kept] + [with_across(count + 1) for count in range(len(early_turns))]
        early_kept = lax.switch(short, choices, spectra, other, early_kept)
        early, late = [early_kept, early_received], [late_kept, late_received]
    else:
        other, late_sent = add_sent("across_sums", traces, places, late_turns, (2,), other, late_sent)
        spectra, early_sent = add_sent("across_sums", [], [], early_turns, (2,), spectra, early_sent)
        other, early_sent = add_sent("across_sums", [], [], early_turns, (2,), other, early_sent)
        early, late = spread(early_sent), spread(late_sent)
    result = finish(order, early, inverse, early_turns, True, None)
    result = finish(order, late, inverse, late_turns, not swap, result)
    return result.reshape(rounds, 1, all_pairs // length, 2 * samples)


def solution(mesh):
    return jax.shard_map(
        on_device,
        mesh=mesh,
        in_specs=(
            P(("groups", "cluster"), "station", None, None),
            P(("groups", "cluster"), "station"),
            P("groups"),
            P(None, "groups"),
            P(None, ("groups", "cluster"), None, None),
            P("groups"),
        ),
        out_specs=P(None, ("groups", "cluster"), "station", None),
        check_vma=False,
    )
```
